256 devices in a mesh: tile: 64 (over y, x_hi, z), vert: 4 (over x_lo, core).
Axes of the slice: x: 4 (x_hi: 2, x_lo: 2; x = x_hi * 2 + x_lo), y: 4, z: 8, core: 2. Of those that a mesh axis runs over, the one named last changes fastest.
Arguments:
- phase_init: float32 [7, 256, 16, 512], P(None, 'tile', None, 'vert'), may hold values from 0 to 0.25
- flow_init: float32 [19, 256, 16, 512], P(None, 'tile', None, 'vert'), may hold values from 0 to 0.2
- solid_mask: int32 [256, 16, 512], P('tile', None, 'vert'), may hold values from 0 to 1, as said below
- sensor_cells: int32 [3, 32768], replicated, may hold values from 0 to 510, as said below
- sensor_weights: float32 [32768], replicated, may hold values from 0.5 to 2
Outputs:
- grad_phase: float32 [7, 256, 16, 512], P(None, 'tile', None, 'vert')
- grad_flow: float32 [19, 256, 16, 512], P(None, 'tile', None, 'vert')
The draws below stay inside these ranges and needn't reach their ends.
Inputs may be any that keep to these rules, and one draw needn't show every extreme that they name: `solid_mask`: 1 marks a solid cell, 0 a fluid one; every cell whose first index is 0 or 255, or whose third index is 0 or 511, is solid. `sensor_cells`: rows 0, 1, 2 hold a probe's cell indices along the first, second and third dimensions; each probe's cell is fluid; several probes may share a cell.
All inputs are finite; a program needn't handle non-finite values.
Results may differ from the reference program's by a relative error of at most 0.0003.
Values sent between devices are 32-bit elements; how exact they have to be, the bound alone decides.
No kernel may reach another device: no remote copies, remote signals or barrier semaphores. Data moves between devices by JAX's collectives and lax.ppermute only.
A program may use at most 64 MiB of HBM per device.

```python
import math
import jax
import jax.numpy as jnp
import numpy as np
from jax import lax

CX = 4
LAYERS = 16
CZ = 128
NX = 256
NZ = 512
SENSORS = 32768
N_TILE = 64


def draw_solid_mask(key, part):
    key = jax.random.fold_in(key, 11)
    across = jnp.arange(NX)[:, None, None]
    height = jnp.arange(NZ)[None, None, :]
    outer_walls = (across == 0) | (across == NX - 1) | (height == 0) | (height == NZ - 1)
    inside = (across >= 3) & (across <= NX - 4)
    plates = inside & (height % CZ == CZ // 2) & (height > 0) & (height < NZ - 1)
    stiffeners = inside & (height % CZ == CZ // 2 + 1) & (height < NZ - 1) & (jax.random.randint(key, (NX, LAYERS, NZ), 0, 4) == 0)
    return (outer_walls | plates | stiffeners).astype(jnp.int32)


def draw_sensor_cells(key, part):
    key = jax.random.fold_in(key, 23)
    subkeys = jax.random.split(key, 4)
    across = jax.random.randint(subkeys[0], (SENSORS,), 3, NX - 3)
    layer_index = jax.random.randint(subkeys[1], (SENSORS,), 0, LAYERS)
    deck_level = jax.random.randint(subkeys[2], (SENSORS,), 0, NZ // CZ - 1)
    offset_up = jax.random.randint(subkeys[3], (SENSORS,), 2, CZ)
    height = deck_level * CZ + CZ // 2 + offset_up
    tiles = NX // CX
    probe_index = jnp.arange(SENSORS)
    forced = (probe_index >= 1) & (probe_index <= tiles * (NZ // CZ - 1))
    shifted = jnp.maximum(probe_index - 1, 0)
    across = jnp.where(forced, shifted % tiles * CX + CX // 2, across)
    height = jnp.where(forced, (shifted // tiles + 1) * CZ, height)
    across = across.at[0].set(NX - 4)
    layer_index = layer_index.at[0].set(0)
    height = height.at[0].set(NZ - 2)
    return jnp.stack([across, layer_index, height]).astype(jnp.int32)


def block_levels(key, dims, shards, low, largest):
    def one(axis_at, shards_of):
        steps = jax.random.uniform(jax.random.fold_in(jax.random.fold_in(key, 6), axis_at), (shards_of,), jnp.float32, low / len(shards), largest / len(shards))
        return jnp.repeat(jnp.exp(steps), dims[axis_at] // shards_of).reshape((-1,) + (1,) * (len(dims) - axis_at - 1))

    loudness = one(*shards[0])
    for cut in shards[1:]:
        loudness = loudness * one(*cut)
    return loudness


def setup_inputs(seed: int = 0) -> dict:
    splits = jax.random.split(jax.random.key(seed), 6)
    phase_init = jnp.clip(0.25 * jax.random.uniform(splits[0], (7, NX, LAYERS, NZ), jnp.float32) ** block_levels(splits[0], (7, NX, LAYERS, NZ), ((1, 64), (3, 4)), -0.2, 0.2), 0.0, 0.25)
    flow_init = jnp.clip(0.2 * jax.random.uniform(splits[1], (19, NX, LAYERS, NZ), jnp.float32) ** block_levels(splits[1], (19, NX, LAYERS, NZ), ((1, 64), (3, 4)), -0.2, 0.2), 0.0, 0.2)
    solid_mask = draw_solid_mask(jax.random.fold_in(splits[5], 71), 0)
    sensor_cells = draw_sensor_cells(jax.random.fold_in(splits[5], 71), 0)
    sensor_weights = jnp.clip(jnp.exp(jax.random.uniform(splits[4], (SENSORS,), jnp.float32, math.log(0.5), math.log(2.0))), 0.5, 2.0)
    return dict(phase_init=phase_init, flow_init=flow_init, solid_mask=solid_mask, sensor_cells=sensor_cells, sensor_weights=sensor_weights)


flow_dirs = np.array([[0, 0, 0], [1, 0, 0], [-1, 0, 0], [0, 1, 0], [0, -1, 0], [0, 0, 1], [0, 0, -1], [1, 1, 0], [-1, -1, 0], [1, -1, 0], [-1, 1, 0], [1, 0, 1], [-1, 0, -1], [1, 0, -1], [-1, 0, 1], [0, 1, 1], [0, -1, -1], [0, 1, -1], [0, -1, 1]])
flow_weights = np.array([1.0 / 3.0] + [1.0 / 18.0] * 6 + [1.0 / 36.0] * 12)
flow_back = np.array([0, 2, 1, 4, 3, 6, 5, 8, 7, 10, 9, 12, 11, 14, 13, 16, 15, 18, 17])
phase_weights = np.array([0.25] + [0.125] * 6)
all_dirs = np.concatenate([flow_dirs[:7], flow_dirs])
rho_air = 0.05
tau_air = 0.6
tau_water = 0.9
tau_phase = 0.8
beta_bulk = 0.3
kappa_grad = 0.6
sharpen = 0.075
gravity = 0.02
shaking = 0.01
soft_floor = 0.01

def spread_table(matrix, vectors):
    return jnp.tensordot(matrix, vectors, axes=1, precision=lax.Precision.HIGHEST)

def neighbours(padded):
    centre = padded[1:-1, :, 1:-1]
    ahead_x = padded[2:, :, 1:-1]
    behind_x = padded[:-2, :, 1:-1]
    ahead_y = jnp.roll(centre, -1, axis=1)
    behind_y = jnp.roll(centre, 1, axis=1)
    ahead_z = padded[1:-1, :, 2:]
    behind_z = padded[1:-1, :, :-2]
    gradient = jnp.stack([0.5 * (ahead_x - behind_x), 0.5 * (ahead_y - behind_y), 0.5 * (ahead_z - behind_z)])
    laplace = ahead_x + behind_x + ahead_y + behind_y + ahead_z + behind_z - 6.0 * centre
    return (gradient, laplace)

def collide(phase_dist, flow_dist, gradient, laplace, solid_cells):
    velocity_table = jnp.asarray(flow_dirs, jnp.float32)
    weight_table = jnp.asarray(flow_weights, jnp.float32)[:, None, None, None]
    phase_weight = jnp.asarray(phase_weights, jnp.float32)[:, None, None, None]
    phase_sum = lax.optimization_barrier(jnp.sum(phase_dist, axis=0))
    clipped = jnp.clip(phase_sum, 0.0, 1.0)
    density = rho_air + (1.0 - rho_air) * clipped
    relax_time = tau_air + (tau_water - tau_air) * clipped
    potential = 4.0 * beta_bulk * phase_sum * (phase_sum - 1.0) * (phase_sum - 0.5) - kappa_grad * laplace
    pressure = lax.optimization_barrier(jnp.sum(flow_dist, axis=0))
    momentum = spread_table(velocity_table.T, flow_dist)
    body_force = jnp.stack([-shaking * density, jnp.zeros_like(density), -gravity * (density - rho_air)])
    force = potential * gradient + body_force
    velocity = momentum + force / (2.0 * density)
    speed_sq = lax.optimization_barrier(jnp.sum(velocity * velocity, axis=0))
    projected = spread_table(velocity_table, velocity)
    flow_equil = weight_table * (pressure + 3.0 * projected + 4.5 * projected * projected - 1.5 * speed_sq)
    force_along = spread_table(velocity_table, force)
    work_rate = lax.optimization_barrier(jnp.sum(velocity * force, axis=0))
    source = weight_table * (1.0 - 0.5 / relax_time) * (3.0 * (force_along - work_rate) + 9.0 * projected * force_along) / density
    flow_post = flow_dist - (flow_dist - flow_equil) / relax_time + source
    flow_post = solid_cells * flow_dist[flow_back] + (1.0 - solid_cells) * flow_post
    grad_length = jnp.sqrt(lax.optimization_barrier(jnp.sum(gradient * gradient, axis=0)) + soft_floor)
    carried = phase_sum * velocity + sharpen * phase_sum * (1.0 - phase_sum) * gradient / grad_length
    phase_along = spread_table(velocity_table[:7], carried)
    phase_equil = phase_weight * (phase_sum + 4.0 * phase_along)
    phase_post = phase_dist - (phase_dist - phase_equil) / tau_phase
    phase_post = solid_cells * phase_dist[flow_back[:7]] + (1.0 - solid_cells) * phase_post
    return (phase_post, flow_post)

def advect(padded, velocity_set, rim_width, grow_by, direction):
    count_x = padded.shape[1] - 2 * (rim_width - grow_by)
    count_z = padded.shape[3] - 2 * (rim_width - grow_by)
    shifted_list = []
    for slot_index in range(velocity_set.shape[0]):
        step_x = int(velocity_set[slot_index][0])
        step_y = int(velocity_set[slot_index][1])
        step_z = int(velocity_set[slot_index][2])
        start_x = rim_width - grow_by - direction * step_x
        start_z = rim_width - grow_by - direction * step_z
        window_cut = padded[slot_index, start_x:start_x + count_x, :, start_z:start_z + count_z]
        shifted_list.append(jnp.roll(window_cut, direction * step_y, axis=1))
    return jnp.stack(shifted_list)

def pad_cells(field, leading):
    return jnp.pad(field, ((0, 0),) * leading + ((1, 1), (0, 0), (1, 1)))

def to_blocks(array):
    leading = array.shape[:-3]
    shaped = array.reshape(leading + (N_TILE, CX, LAYERS, NZ))
    return jnp.moveaxis(shaped, len(leading), 0)

def from_blocks(array):
    moved_back = jnp.moveaxis(array, 0, -4)
    return moved_back.reshape(moved_back.shape[:-4] + (NX, LAYERS, NZ))

def reference(phase_init, flow_init, solid_mask, sensor_cells, sensor_weights):
    solid_cells = solid_mask.astype(jnp.float32)
    solid_blocks = to_blocks(solid_cells)

    def stencil_of(phase_sum):
        return neighbours(pad_cells(phase_sum, 0))

    def stream_of(post_all):
        return advect(pad_cells(post_all, 1), all_dirs, 1, 0, 1)

    def forward_block(pieces):
        phase_dist, flow_dist, gradient, laplace, solid_part = pieces
        return jnp.concatenate(collide(phase_dist, flow_dist, gradient, laplace, solid_part))

    def backward_block(pieces):
        phase_dist, flow_dist, gradient, laplace, solid_part, adjoint = pieces

        def local_part(phase_part, flow_part, grad_part, laplace_part):
            return jnp.concatenate(collide(phase_part, flow_part, grad_part, laplace_part, solid_part))
        _, pullback = jax.vjp(local_part, phase_dist, flow_dist, gradient, laplace)
        return pullback(adjoint)

    def retreat(adjoint, phase_dist, flow_dist, gradient, laplace):
        _, stream_back = jax.vjp(stream_of, jnp.zeros((26, NX, LAYERS, NZ), jnp.float32))
        adj_post = stream_back(adjoint)[0]
        blocks = lax.map(backward_block, (to_blocks(phase_dist), to_blocks(flow_dist), to_blocks(gradient), to_blocks(laplace), solid_blocks, to_blocks(adj_post)))
        d_phase = from_blocks(blocks[0])
        d_flow = from_blocks(blocks[1])
        d_gradient = from_blocks(blocks[2])
        d_laplace = from_blocks(blocks[3])
        _, stencil_back = jax.vjp(stencil_of, jnp.zeros((NX, LAYERS, NZ), jnp.float32))
        d_sum = stencil_back((d_gradient, d_laplace))[0]
        return jnp.concatenate([d_phase + d_sum[None], d_flow])
    gradient0, laplace0 = stencil_of(lax.optimization_barrier(jnp.sum(phase_init, axis=0)))
    post_blocks = lax.map(forward_block, (to_blocks(phase_init), to_blocks(flow_init), to_blocks(gradient0), to_blocks(laplace0), solid_blocks))
    state_mid = stream_of(from_blocks(post_blocks))
    phase_mid = state_mid[:7]
    flow_mid = state_mid[7:]
    gradient1, laplace1 = stencil_of(lax.optimization_barrier(jnp.sum(phase_mid, axis=0)))
    seed_field = jnp.zeros((NX, LAYERS, NZ), jnp.float32).at[sensor_cells[0], sensor_cells[1], sensor_cells[2]].add(sensor_weights)
    adjoint_late = jnp.concatenate([jnp.zeros((7, NX, LAYERS, NZ), jnp.float32), jnp.broadcast_to(seed_field, (19, NX, LAYERS, NZ))])
    adjoint_mid = retreat(adjoint_late, phase_mid, flow_mid, gradient1, laplace1)
    result = retreat(adjoint_mid, phase_init, flow_init, gradient0, laplace0)
    return (result[:7], result[7:])
```

```python
import functools

import jax
import jax.numpy as jnp
import numpy as np
from jax import lax
from jax.experimental import pallas as pl
from jax.experimental.pallas import tpu as pltpu
from jax.sharding import PartitionSpec as P

DIRS = [
    (0, 0, 0), (1, 0, 0), (-1, 0, 0), (0, 1, 0), (0, -1, 0), (0, 0, 1), (0, 0, -1),
    (1, 1, 0), (-1, -1, 0), (1, -1, 0), (-1, 1, 0), (1, 0, 1), (-1, 0, -1), (1, 0, -1),
    (-1, 0, 1), (0, 1, 1), (0, -1, -1), (0, 1, -1), (0, -1, 1),
]
BACK = [0, 2, 1, 4, 3, 6, 5, 8, 7, 10, 9, 12, 11, 14, 13, 16, 15, 18, 17]
W = [1.0 / 3.0] + [1.0 / 18.0] * 6 + [1.0 / 36.0] * 12
W0, W1, W2 = 1.0 / 3.0, 1.0 / 18.0, 1.0 / 36.0
PAIRS = [(q, q + 1) for q in range(1, 19, 2)]
TO_RIGHT = [q for q in range(19) if DIRS[q][0] == 1]
TO_LEFT = [q for q in range(19) if DIRS[q][0] == -1]
RIM = 8
SHARP = 0.075
FLUID = 26
F32 = jnp.float32
VMEM_LIMIT = 40 * 2**20


def lanes():
    return lax.broadcasted_iota(jnp.int32, (16, 128), 1)


def roll(x, shift, axis):
    shift = shift % x.shape[axis]
    return x if shift == 0 else pltpu.roll(x, shift, axis)


def load_pair(ref, *at):
    *head, row = at
    return (ref[(*head, 2 * row)], ref[(*head, 2 * row + 1)])


def store_pair(ref, pair, *at):
    *head, row = at
    ref[(*head, 2 * row)] = pair[0]
    ref[(*head, 2 * row + 1)] = pair[1]


def both(fn, *pairs):
    return tuple(fn(*each) for each in zip(*pairs))


def moved(pair, step_y, step_z):
    if step_y:
        pair = both(lambda t: roll(t, -step_y, 0), pair)
    if step_z:
        a = roll(pair[0], -step_z, 1)
        b = roll(pair[1], -step_z, 1)
        edge = lanes() == (127 if step_z > 0 else 0)
        pair = (jnp.where(edge, b, a), jnp.where(edge, a, b))
    return pair


def pack(msg_ref, fields):
    lane = lanes()
    count = len(fields)
    for base in range(0, count, 8):
        acc = jnp.zeros((16, 128), F32)
        for slot, (main, rim) in enumerate(fields[base : base + 8]):
            msg_ref[base + slot] = main
            acc = jnp.where(lane // 16 == slot, roll(rim, 8 + 16 * slot, 1), acc)
        msg_ref[count + base // 8] = acc


def unpack(msg_ref, count, k):
    return (msg_ref[k], roll(msg_ref[count + k // 8], -(8 + 16 * (k % 8)), 1))


def total(values):
    out = values[0]
    for value in values[1:]:
        out = out + value
    return out


def along(step, vec):
    out = None
    for c, v in zip(step, vec):
        if c == 0:
            continue
        if out is None:
            out = v if c > 0 else -v
        else:
            out = out + v if c > 0 else out - v
    return out


def momentum_of(pops, axis):
    plus = [pops[q] for q in range(19) if DIRS[q][axis] == 1]
    minus = [pops[q] for q in range(19) if DIRS[q][axis] == -1]
    return total([a - b for a, b in zip(plus, minus)])


def state_of(phi, mom, grad, lap):
    clipped = jnp.clip(phi, 0.0, 1.0)
    rho = 0.05 + 0.95 * clipped
    omega = 1.0 / (0.6 + 0.3 * clipped)
    inv_rho = 1.0 / rho
    potential = 1.2 * phi * (phi - 1.0) * (phi - 0.5) - 0.6 * lap
    force = (
        potential * grad[0] - 0.01 * rho,
        potential * grad[1],
        potential * grad[2] - 0.02 * (rho - 0.05),
    )
    half = 0.5 * inv_rho
    vel = tuple(m + f * half for m, f in zip(mom, force))
    kappa = (1.0 - 0.5 * omega) * inv_rho
    return dict(
        phi=phi, grad=grad, omega=omega, inv_rho=inv_rho, potential=potential, force=force,
        half=half, vel=vel, kappa=kappa,
    )


def dot(a, b):
    return a[0] * b[0] + a[1] * b[1] + a[2] * b[2]


def sharpening(s):
    inv_len = lax.rsqrt(dot(s["grad"], s["grad"]) + 0.01)
    return SHARP * s["phi"] * (1.0 - s["phi"]) * inv_len, inv_len


def carried_of(s, axis):
    sharp, _ = sharpening(s)
    return s["phi"] * s["vel"][axis] + sharp * s["grad"][axis]


def post_flow(pops, fluid, pressure, s, wanted):
    vel, force, omega, kappa = s["vel"], s["force"], s["omega"], s["kappa"]
    base = omega * (pressure - 1.5 * dot(vel, vel)) - 3.0 * kappa * dot(vel, force)
    odd_vec = tuple(3.0 * (omega * v + kappa * f) for v, f in zip(vel, force))
    even_vec = tuple(4.5 * omega * v + 9.0 * kappa * f for v, f in zip(vel, force))
    keep = 1.0 - omega
    out = {}
    if 0 in wanted:
        out[0] = jnp.where(fluid, keep * pops[0] + W0 * base, pops[0])
    for q, r in PAIRS:
        if q not in wanted and r not in wanted:
            continue
        step = DIRS[q]
        even = base + along(step, vel) * along(step, even_vec)
        odd = along(step, odd_vec)
        if q in wanted:
            out[q] = jnp.where(fluid, keep * pops[q] + W[q] * (even + odd), pops[r])
        if r in wanted:
            out[r] = jnp.where(fluid, keep * pops[r] + W[q] * (even - odd), pops[q])
    return out


def post_phase(pops, fluid, s, wanted):
    sharp, _ = sharpening(s)
    carried = tuple(s["phi"] * v + sharp * g for v, g in zip(s["vel"], s["grad"]))
    out = {}
    for q in wanted:
        if q == 0:
            out[q] = jnp.where(fluid, 0.3125 * s["phi"] - 0.25 * pops[0], pops[0])
        else:
            equil = 0.15625 * s["phi"] + 0.625 * along(DIRS[q], carried)
            out[q] = jnp.where(fluid, equil - 0.25 * pops[q], pops[BACK[q]])
    return out


def moments_of(adj):
    zero = None
    m0, m1 = [], [[], [], []]
    m2 = {}
    if 0 in adj:
        m0.append(W0 * adj[0])
    groups = {W1: [], W2: []}
    for q in range(1, 19):
        if q not in adj:
            continue
        a = adj[q]
        w = W[q]
        groups[w].append(a)
    for w, items in groups.items():
        if items:
            m0.append(w * total(items))

    def weighted(terms):
        parts = []
        for w in (W1, W2):
            mine = [(sign, a) for ww, sign, a in terms if ww == w]
            if not mine:
                continue
            acc = None
            for sign, a in mine:
                if acc is None:
                    acc = a if sign > 0 else -a
                else:
                    acc = acc + a if sign > 0 else acc - a
            parts.append(w * acc)
        return total(parts) if parts else None

    for i in range(3):
        m1[i] = weighted([(W[q], DIRS[q][i], adj[q]) for q in range(1, 19) if q in adj and DIRS[q][i]])
    for i in range(3):
        for j in range(i, 3):
            m2[(i, j)] = weighted(
                [
                    (W[q], DIRS[q][i] * DIRS[q][j], adj[q])
                    for q in range(1, 19)
                    if q in adj and DIRS[q][i] and DIRS[q][j]
                ]
            )
            m2[(j, i)] = m2[(i, j)]
    return total(m0), m1, m2


def apply_m2(m2, vec):
    out = []
    for i in range(3):
        terms = [m2[(i, j)] * vec[j] for j in range(3) if m2[(i, j)] is not None]
        out.append(total(terms))
    return out


def pull_stencil(s, m0, m1, m2, n1):
    vel, force = s["vel"], s["force"]
    omega, kappa, half = s["omega"], s["kappa"], s["half"]
    m2v = apply_m2(m2, vel)
    m2f = apply_m2(m2, force)
    m0_3 = 3.0 * m0
    lean = []
    for i in range(3):
        term = 9.0 * m2v[i] - m0_3 * vel[i]
        lean.append(term if m1[i] is None else term + 3.0 * m1[i])
    push = [9.0 * m2f[i] - m0_3 * force[i] for i in range(3)]
    d_vel = [omega * a + kappa * b for a, b in zip(lean, push)]
    if n1 is not None:
        five_phi = 5.0 * s["phi"]
        d_vel = [d + five_phi * n for d, n in zip(d_vel, n1)]
    d_force = [kappa * a + half * d for a, d in zip(lean, d_vel)]
    d_potential = dot(d_force, s["grad"])
    d_grad = [s["potential"] * x for x in d_force]
    if n1 is not None:
        sharp, inv_len = sharpening(s)
        tilt = dot(s["grad"], n1) * inv_len * inv_len
        sharp5 = 5.0 * sharp
        d_grad = [d + sharp5 * (n - g * tilt) for d, n, g in zip(d_grad, n1, s["grad"])]
    d_lap = -0.6 * d_potential
    return d_grad, d_lap, d_potential, d_force, d_vel, m2v, m2f


def pull_all(s, pressure, adj, kept, m0, m1, m2, n0, n1):
    d_grad, d_lap, d_potential, d_force, d_vel, m2v, m2f = pull_stencil(s, m0, m1, m2, n1)
    phi, vel, force = s["phi"], s["vel"], s["force"]
    omega, kappa, inv_rho, half = s["omega"], s["kappa"], s["inv_rho"], s["half"]
    relaxed = m0 * (pressure - 1.5 * dot(vel, vel)) + 3.0 * dot(m1, vel) + 4.5 * dot(m2v, vel)
    forced = 3.0 * dot(m1, force) - 3.0 * m0 * dot(vel, force) + 9.0 * dot(m2v, force)
    d_omega = relaxed - kept - 0.5 * inv_rho * forced
    d_rho = (
        -kappa * inv_rho * forced
        - 0.01 * d_force[0]
        - 0.02 * d_force[2]
        - dot(d_vel, force) * half * inv_rho
    )
    d_clip = 0.95 * d_rho - 0.3 * omega * omega * d_omega
    inside = jnp.where((phi > 0.0) & (phi < 1.0), 1.0, jnp.where((phi == 0.0) | (phi == 1.0), 0.5, 0.0))
    d_phi = d_potential * (1.2 * (3.0 * phi * (phi - 1.0) + 0.5)) + d_clip * inside
    if n1 is not None:
        _, inv_len = sharpening(s)
        d_phi = d_phi + 1.25 * n0 + 5.0 * (
            dot(n1, vel) + SHARP * (1.0 - 2.0 * phi) * inv_len * dot(n1, s["grad"])
        )
    d_pressure = omega * m0
    keep = 1.0 - omega
    d_flow = {0: keep * adj[0] + d_pressure}
    for q, r in PAIRS:
        lift = along(DIRS[q], d_vel)
        d_flow[q] = keep * adj[q] + (d_pressure + lift)
        d_flow[r] = keep * adj[r] + (d_pressure - lift)
    return d_flow, d_phi, d_grad, d_lap


def gradients(behind, centre, ahead):
    ahead_y, behind_y = moved(centre, 1, 0), moved(centre, -1, 0)
    ahead_z, behind_z = moved(centre, 0, 1), moved(centre, 0, -1)
    diff = lambda a, b: 0.5 * (a - b)
    lap = both(
        lambda a, b, c, d, e, f, m: a + b + c + d + e + f - 6.0 * m,
        ahead, behind, ahead_y, behind_y, ahead_z, behind_z, centre,
    )
    return both(diff, ahead, behind), both(diff, ahead_y, behind_y), both(diff, ahead_z, behind_z), lap


def behind_part(d_grad, d_lap):
    return 0.5 * d_grad + d_lap


def ahead_part(d_grad, d_lap):
    return d_lap - 0.5 * d_grad


def rim_kernel(g_ref, f_ref, solid_ref, up_ref, down_ref):
    lane = lanes()

    def row(x, carry):
        for tile in range(2):
            up = jnp.zeros((16, 128), F32)
            down = jnp.zeros((16, 128), F32)
            for slot in range(16):
                k = 16 * tile + slot
                if k > FLUID:
                    continue
                if k < 7:
                    cells = g_ref[k, x]
                elif k < 26:
                    cells = f_ref[k - 7, x]
                else:
                    cells = 1.0 - solid_ref[x].astype(F32)
                mine = lane // RIM == slot
                up = jnp.where(mine, roll(cells, 8 * slot + 8, 1), up)
                down = jnp.where(mine, roll(cells, 8 * slot, 1), down)
            up_ref[tile, x] = up
            down_ref[tile, x] = down
        return carry

    lax.fori_loop(0, 4, row, 0)


def ring_kernel(g_ref, f_ref, solid_ref, below_ref, above_ref, s_ref, right_ref, left_ref, phase_ref):
    lane = lanes()

    def row(x, carry):
        sums = [None, None]
        for k in range(27):
            if k < 7:
                cells = g_ref[k, x]
            elif k < 26:
                cells = f_ref[k - 7, x]
            else:
                cells = 1.0 - solid_ref[x].astype(F32)
            slot = k % 16
            above = roll(above_ref[k // 16, x], -8 * slot, 1)
            below = roll(below_ref[k // 16, x], 120 - 8 * slot, 1)
            rim = jnp.where(lane < 64, above, below)
            s_ref[k, 2 * x] = cells
            s_ref[k, 2 * x + 1] = rim
            if k < 7:
                sums = [a if b is None else a + b for a, b in zip((cells, rim), sums)]
        phase_ref[2 * x] = sums[0]
        phase_ref[2 * x + 1] = sums[1]
        return carry

    lax.fori_loop(0, 4, row, 0)

    for msg_ref, edge, inner, crossing in ((right_ref, 3, 2, TO_RIGHT), (left_ref, 0, 1, TO_LEFT)):
        pops = [load_pair(s_ref, 7 + q, edge) for q in range(19)]
        fluid = load_pair(s_ref, FLUID, edge)
        fields = [
            both(lambda a, b, f: jnp.where(f > 0.5, a, b), pops[q], pops[BACK[q]], fluid) for q in crossing
        ]
        fields += [load_pair(s_ref, q, edge) for q in range(7)]
        fields.append(both(lambda *p: total(p), *pops))
        for axis in range(3):
            fields.append(both(lambda *p: momentum_of(p, axis), *pops))
        fields.append(fluid)
        grads = gradients(*(load_pair(phase_ref, inner + d) for d in (-1, 0, 1)))
        phi = load_pair(phase_ref, inner)
        inner_pops = [load_pair(s_ref, 7 + q, inner) for q in range(19)]
        out = 1 if edge == 3 else 2
        crossing_phase = []
        for t in range(2):
            mom = [momentum_of([p[t] for p in inner_pops], 0)] + [jnp.zeros((16, 128), F32)] * 2
            s = state_of(phi[t], mom, tuple(g[t] for g in grads[:3]), grads[3][t])
            equil = 0.15625 * phi[t] + (0.625 if out == 1 else -0.625) * carried_of(s, 0)
            crossing_phase.append(
                jnp.where(
                    s_ref[FLUID, 2 * inner + t] > 0.5,
                    equil - 0.25 * s_ref[out, 2 * inner + t],
                    s_ref[BACK[out], 2 * inner + t],
                )
            )
        fields.append(tuple(crossing_phase))
        fields.append(phi)
        pack(msg_ref, fields)


PROBE_CHUNK = 2048


def probe_kernel(corner_ref, cells_ref, weights_ref, out_ref, acc_ref):
    first_x = corner_ref[0]
    first_z = corner_ref[1]
    acc_ref[...] = jnp.zeros_like(acc_ref)
    across = lax.broadcasted_iota(jnp.int32, (96, PROBE_CHUNK), 0)
    height = lax.broadcasted_iota(jnp.int32, (144, PROBE_CHUNK), 0)

    def chunk(i, carry):
        at = pl.ds(pl.multiple_of(i * PROBE_CHUNK, PROBE_CHUNK), PROBE_CHUNK)
        x = cells_ref[0:1, at] - (first_x - 1)
        y = cells_ref[1:2, at]
        z = cells_ref[2:3, at] - first_z
        code_xy = jnp.where((x >= 0) & (x < 6), x * 16 + y, -1)
        code_z = jnp.where((z >= -RIM) & (z < 128 + RIM), jnp.where(z >= 0, z, z + 144), -1)
        weight = weights_ref[0:1, at]
        high = weight.astype(jnp.bfloat16).astype(F32)
        low = weight - high
        hit = across == code_xy
        lhs = jnp.concatenate([jnp.where(hit, high, 0.0), jnp.where(hit, low, 0.0)], axis=0).astype(jnp.bfloat16)
        rhs = jnp.where(height == code_z, 1.0, 0.0).astype(jnp.bfloat16)
        acc_ref[...] += lax.dot_general(lhs, rhs, (((1,), (1,)), ((), ())), preferred_element_type=F32)
        return carry

    lax.fori_loop(0, cells_ref.shape[1] // PROBE_CHUNK, chunk, 0)
    lane = lanes()
    for x in range(6):
        rows = pl.ds(16 * x, 16)
        lows = pl.ds(96 + 16 * x, 16)
        out_ref[2 * x] = acc_ref[rows, 0:128] + acc_ref[lows, 0:128]
        rim = acc_ref[rows, 128:144] + acc_ref[lows, 128:144]
        rim = jnp.concatenate([rim, jnp.zeros((16, 112), F32)], axis=1)
        out_ref[2 * x + 1] = jnp.where(lane < RIM, rim, jnp.where(lane >= 120, roll(rim, 112, 1), 0.0))


N_FIRST = 19
N_SECOND = 8


def chunks(rows_from, rows_to, body):
    def step(i, carry):
        for h in range(2):
            body(i, slice(8 * h, 8 * h + 8))
        return carry

    lax.fori_loop(2 * rows_from, 2 * rows_to, step, 0)


def middle_kernel(
    s_ref, from_left_ref, from_right_ref, seed_ref,
    prim_ref, adj_ref, gamma_ref, edges_ref, to_right_ref, to_left_ref,
    phase_ref, post_ref, phase_mid_ref, grad_mid_ref, seeds_ref, back_ref, dphi_ref,
):
    sides = ((from_left_ref, 0, -2), (from_right_ref, 5, 5))
    for row in range(4):
        total_pair = both(lambda *p: total(p), *[load_pair(s_ref, q, row) for q in range(7)])
        store_pair(phase_ref, total_pair, row + 2)
    for msg_ref, at, _ in sides:
        got = [unpack(msg_ref, N_FIRST, k) for k in range(N_FIRST)]
        store_pair(phase_ref, both(lambda *p: total(p), *got[5:12]), at + 1)
        store_pair(phase_ref, got[18], 0 if at == 0 else 7)
        for i in range(4):
            store_pair(prim_ref, got[12 + i], 5 + i, at)
        store_pair(prim_ref, got[16], 9, at)
        crossing = TO_RIGHT if at == 0 else TO_LEFT
        for q, pair in zip(crossing, got[:5]):
            store_pair(post_ref, pair, 7 + q, at)
        for q in range(7):
            store_pair(post_ref, got[5 + q], q, at)
    for row in range(6):
        grads = gradients(*(load_pair(phase_ref, row + d) for d in (0, 1, 2)))
        store_pair(prim_ref, load_pair(phase_ref, row + 1), 0, row)
        for i in range(4):
            store_pair(prim_ref, grads[i], 1 + i, row)

    def prim_at(i, h):
        vals = [prim_ref[k, i, h, :] for k in range(10)]
        s = state_of(vals[0], vals[6:9], tuple(vals[1:4]), vals[4])
        return s, vals[5], vals[9] > 0.5

    def forward(i, h):
        g = [s_ref[q, i, h, :] for q in range(7)]
        f = [s_ref[7 + q, i, h, :] for q in range(19)]
        pressure = total(f)
        at = i + 2
        prim_ref[5, at, h, :] = pressure
        for axis in range(3):
            prim_ref[6 + axis, at, h, :] = momentum_of(f, axis)
        prim_ref[9, at, h, :] = s_ref[FLUID, i, h, :]
        s, pressure, fluid = prim_at(at, h)
        for q, v in post_flow(f, fluid, pressure, s, range(19)).items():
            post_ref[7 + q, at, h, :] = v
        for q, v in post_phase(g, fluid, s, range(7)).items():
            post_ref[q, at, h, :] = v

    chunks(0, 4, forward)

    for at, crossing, out in ((0, TO_RIGHT, 1), (5, TO_LEFT, 2)):

        def edge(i, h, crossing=crossing, out=out):
            s, pressure, fluid = prim_at(i, h)
            f = {q: post_ref[7 + q, i, h, :] for q in crossing}
            pops = {}
            for q in crossing:
                pops[q] = f[q]
                pops[BACK[q]] = f[q]
            for q, v in post_flow(pops, fluid, pressure, s, crossing).items():
                post_ref[7 + q, i, h, :] = v
            g = [post_ref[q, i, h, :] for q in range(7)]
            for q, v in post_phase(g, fluid, s, [0, 3, 4, 5, 6, out]).items():
                post_ref[q, i, h, :] = v

        chunks(at, at + 1, edge)

    for q in range(19):
        _, cy, cz = DIRS[q]
        if cy == 0 and cz == 0:
            continue
        rows = range(0, 6)
        for row in rows:
            here = row - 1 + DIRS[q][0]
            if 0 <= here < 4:
                store_pair(post_ref, moved(load_pair(post_ref, 7 + q, row), -cy, -cz), 7 + q, row)
    for row in range(6):
        parts = [load_pair(post_ref, 0, row)]
        for q in range(3, 7):
            parts.append(moved(load_pair(post_ref, q, row), -DIRS[q][1], -DIRS[q][2]))
        if row == 0:
            parts.append(unpack(from_left_ref, N_FIRST, 17))
        else:
            parts.append(load_pair(post_ref, 1, row - 1))
        if row == 5:
            parts.append(unpack(from_right_ref, N_FIRST, 17))
        else:
            parts.append(load_pair(post_ref, 2, row + 1))
        store_pair(phase_mid_ref, both(lambda *p: total(p), *parts), row)
    for row in range(4):
        grads = gradients(*(load_pair(phase_mid_ref, row + d) for d in (0, 1, 2)))
        for i in range(4):
            store_pair(grad_mid_ref, grads[i], i, row)
    shifts = sorted({(c[1], c[2]) for c in DIRS})
    for n, (cy, cz) in enumerate(shifts):
        for row in range(6):
            store_pair(seeds_ref, moved(load_pair(seed_ref, row), cy, cz), n, row)

    def backward(i, h):
        f = [post_ref[7 + q, i + 2 - 2 * DIRS[q][0], h, :] for q in range(19)]
        adj = [seeds_ref[shifts.index(DIRS[q][1:]), i + 2 + 2 * DIRS[q][0], h, :] for q in range(19)]
        fluid = s_ref[FLUID, i, h, :] > 0.5
        phi = phase_mid_ref[i + 2, h, :]
        pressure = total(f)
        mom = [momentum_of(f, axis) for axis in range(3)]
        s = state_of(phi, mom, tuple(grad_mid_ref[k, i, h, :] for k in range(3)), grad_mid_ref[3, i, h, :])
        kept = total([a * b for a, b in zip(adj, f)])
        m0, m1, m2 = moments_of(dict(enumerate(adj)))
        d_flow, d_phi, d_grad, d_lap = pull_all(s, pressure, adj, kept, m0, m1, m2, None, None)
        for q in range(19):
            adj_ref[q, i, h, :] = jnp.where(fluid, d_flow[q], adj[BACK[q]])
        dphi_ref[i, h, :] = jnp.where(fluid, d_phi, 0.0)
        for k in range(3):
            back_ref[k, i, h, :] = jnp.where(fluid, d_grad[k], 0.0)
        back_ref[3, i, h, :] = jnp.where(fluid, d_lap, 0.0)

    chunks(0, 4, backward)

    for q in range(19):
        _, cy, cz = DIRS[q]
        if cy or cz:
            for row in range(4):
                store_pair(adj_ref, moved(load_pair(adj_ref, q, row), cy, cz), q, row)

    for row in range(4):
        store_pair(gamma_ref, stencil_back(back_ref, dphi_ref, row), row)
    edge_parts = []
    for row, part in ((0, ahead_part), (3, behind_part)):
        pair = both(part, load_pair(back_ref, 0, row), load_pair(back_ref, 3, row))
        store_pair(edges_ref, pair, 0 if row == 0 else 1)
        edge_parts.append(pair)

    for msg_ref, row, out_dirs, part, sign, edge_pair in (
        (to_right_ref, 3, TO_RIGHT, behind_part, -1.0, edge_parts[1]),
        (to_left_ref, 0, TO_LEFT, ahead_part, 1.0, edge_parts[0]),
    ):
        gamma = load_pair(gamma_ref, row)
        next_gamma = load_pair(gamma_ref, row - 1 if row == 3 else row + 1)
        n1 = turn_gamma(both(lambda a: sign * a, next_gamma), gamma)
        partial = []
        for t in range(2):
            vals = [prim_ref[k, 2 * (row + 1) + t] for k in range(10)]
            s = state_of(vals[0], vals[6:9], tuple(vals[1:4]), vals[4])
            adj = {
                q: adj_ref[q, 2 * (row + DIRS[q][0]) + t] for q in range(19) if q not in out_dirs
            }
            m0, m1, m2 = moments_of(adj)
            d_grad, d_lap = pull_stencil(s, m0, m1, m2, [n[t] for n in n1])[:2]
            partial.append(jnp.where(vals[9] > 0.5, part(d_grad[0], d_lap), 0.0))
        back_dirs = TO_LEFT if row == 3 else TO_RIGHT
        fields = [load_pair(adj_ref, q, row) for q in back_dirs]
        fields += [gamma, edge_pair, tuple(partial)]
        pack(msg_ref, fields)


def turn_gamma(along_x, centre):
    diff = lambda a, b: 0.125 * (a - b)
    return (
        both(lambda a: 0.125 * a, along_x),
        both(diff, moved(centre, 1, 0), moved(centre, -1, 0)),
        both(diff, moved(centre, 0, 1), moved(centre, 0, -1)),
    )


def stencil_back(back_ref, start_ref, row, first=None, last=None):
    gy, gz, lap = (load_pair(back_ref, k, row) for k in (1, 2, 3))
    fold = lambda s, l, gyb, gya, lyb, lya, gzb, gza, lzb, lza: (
        s - 6.0 * l + 0.5 * (gyb - gya) + lyb + lya + 0.5 * (gzb - gza) + lzb + lza
    )
    out = both(
        fold, load_pair(start_ref, row), lap,
        moved(gy, -1, 0), moved(gy, 1, 0), moved(lap, -1, 0), moved(lap, 1, 0),
        moved(gz, 0, -1), moved(gz, 0, 1), moved(lap, 0, -1), moved(lap, 0, 1),
    )
    add = lambda a, b: a + b
    if row > 0:
        out = both(add, out, both(behind_part, load_pair(back_ref, 0, row - 1), load_pair(back_ref, 3, row - 1)))
    elif first is not None:
        out = both(add, out, first)
    if row < 3:
        out = both(add, out, both(ahead_part, load_pair(back_ref, 0, row + 1), load_pair(back_ref, 3, row + 1)))
    elif last is not None:
        out = both(add, out, last)
    return out


def last_kernel(
    s_ref, prim_ref, adj_ref, gamma_ref, edges_ref, from_left_ref, from_right_ref,
    out_g_ref, out_f_ref,
    adj_wide_ref, gamma_wide_ref, turn_ref, turned_ref, back_ref, dphi_ref,
):
    add = lambda a, b: a + b
    got_left = [unpack(from_left_ref, N_SECOND, k) for k in range(N_SECOND)]
    got_right = [unpack(from_right_ref, N_SECOND, k) for k in range(N_SECOND)]
    own_first = load_pair(edges_ref, 0)
    own_last = load_pair(edges_ref, 1)
    for row in range(1, 3):
        store_pair(gamma_wide_ref, load_pair(gamma_ref, row), row + 1)
    store_pair(gamma_wide_ref, both(add, load_pair(gamma_ref, 0), got_left[6]), 1)
    store_pair(gamma_wide_ref, both(add, load_pair(gamma_ref, 3), got_right[6]), 4)
    store_pair(gamma_wide_ref, both(add, got_left[5], own_first), 0)
    store_pair(gamma_wide_ref, both(add, got_right[5], own_last), 5)
    for q, pair in zip(TO_LEFT, got_left[:5]):
        store_pair(adj_wide_ref, pair, q, 0)
    for q, pair in zip(TO_RIGHT, got_right[:5]):
        store_pair(adj_wide_ref, pair, q, 1)
    for row in range(4):
        centre = load_pair(gamma_wide_ref, row + 1)
        for n, (cy, cz) in enumerate(((1, 0), (-1, 0), (0, 1), (0, -1))):
            store_pair(turned_ref, moved(centre, cy, cz), n, row)

    edge_parts = []
    for got, prim_row, row, own, out_dirs, part, sign in (
        (got_left, 0, 0, own_first, TO_RIGHT, behind_part, 1.0),
        (got_right, 5, 3, own_last, TO_LEFT, ahead_part, -1.0),
    ):
        gamma = load_pair(gamma_wide_ref, row + 1)
        n1 = turn_gamma(both(lambda a: sign * a, gamma), own)
        pair = []
        for t in range(2):
            vals = [prim_ref[k, 2 * prim_row + t] for k in range(10)]
            s = state_of(vals[0], vals[6:9], tuple(vals[1:4]), vals[4])
            adj = {q: adj_ref[q, 2 * row + t] for q in out_dirs}
            m0, m1, m2 = moments_of(adj)
            d_grad, d_lap = pull_stencil(s, m0, m1, m2, [n[t] for n in n1])[:2]
            pair.append(got[7][t] + jnp.where(vals[9] > 0.5, part(d_grad[0], d_lap), 0.0))
        edge_parts.append(tuple(pair))

    def gathered(row, t, h):
        adj = []
        for q in range(19):
            at = row + DIRS[q][0]
            if at < 0:
                adj.append(adj_wide_ref[q, t, h, :])
            elif at > 3:
                adj.append(adj_wide_ref[q, 2 + t, h, :])
            else:
                adj.append(adj_ref[q, 2 * at + t, h, :])
        i = 2 * row + t
        phase_adj = [
            gamma_wide_ref[i + 2, h, :],
            gamma_wide_ref[i + 4, h, :],
            gamma_wide_ref[i, h, :],
        ] + [turned_ref[n, i, h, :] for n in range(4)]
        vals = [prim_ref[k, i + 2, h, :] for k in range(10)]
        s = state_of(vals[0], vals[6:9], tuple(vals[1:4]), vals[4])
        n1 = [0.125 * (phase_adj[a] - phase_adj[a + 1]) for a in (1, 3, 5)]
        return adj, phase_adj, s, vals[5], vals[9] > 0.5, n1

    for row in range(4):
        for h in (slice(0, 8), slice(8, 16)):
            adj, phase_adj, s, pressure, fluid, n1 = gathered(row, 0, h)
            kept = total([a * s_ref[7 + q, 2 * row, h, :] for q, a in enumerate(adj)])
            n0 = 0.25 * phase_adj[0] + 0.125 * total(phase_adj[1:])
            m0, m1, m2 = moments_of(dict(enumerate(adj)))
            d_flow, d_phi, d_grad, d_lap = pull_all(s, pressure, adj, kept, m0, m1, m2, n0, n1)
            for q in range(19):
                out_f_ref[q, row, h, :] = jnp.where(fluid, d_flow[q], adj[BACK[q]])
            dphi_ref[2 * row, h, :] = jnp.where(fluid, d_phi, 0.0)
            for k in range(3):
                back_ref[k, 2 * row, h, :] = jnp.where(fluid, d_grad[k], 0.0)
            back_ref[3, 2 * row, h, :] = jnp.where(fluid, d_lap, 0.0)

            adj, phase_adj, s, pressure, fluid, n1 = gathered(row, 1, h)
            m0, m1, m2 = moments_of(dict(enumerate(adj)))
            d_grad, d_lap = pull_stencil(s, m0, m1, m2, n1)[:2]
            for k in range(3):
                back_ref[k, 2 * row + 1, h, :] = jnp.where(fluid, d_grad[k], 0.0)
            back_ref[3, 2 * row + 1, h, :] = jnp.where(fluid, d_lap, 0.0)
            dphi_ref[2 * row + 1, h, :] = jnp.zeros((8, 128), F32)

    for row in range(4):
        base = stencil_back(back_ref, dphi_ref, row, edge_parts[0], edge_parts[1])[0]
        fluid = prim_ref[9, 2 * row + 2] > 0.5
        d_phi = dphi_ref[2 * row]
        rest = base - d_phi
        i = 2 * row
        phase_adj = [gamma_wide_ref[i + 2], gamma_wide_ref[i + 4], gamma_wide_ref[i]]
        phase_adj += [turned_ref[n, i] for n in range(4)]
        for q in range(7):
            out_g_ref[q, row] = jnp.where(fluid, base - 0.25 * phase_adj[q], rest + phase_adj[BACK[q]])


def call(kernel, outs, scratch=(), flops=0, n_smem=0, n_in=0, name=None):
    vmem = pl.BlockSpec(memory_space=pltpu.VMEM)
    smem = pl.BlockSpec(memory_space=pltpu.SMEM)
    return pl.pallas_call(
        kernel,
        out_shape=[jax.ShapeDtypeStruct(shape, F32) for shape in outs],
        in_specs=[smem] * n_smem + [vmem] * n_in,
        out_specs=[vmem] * len(outs),
        scratch_shapes=[pltpu.VMEM(shape, F32) for shape in scratch],
        compiler_params=pltpu.CompilerParams(vmem_limit_bytes=VMEM_LIMIT),
        cost_estimate=pl.CostEstimate(flops=flops, bytes_accessed=flops // 8, transcendentals=0),
        name=name,
    )


def to_ahead(x, axis):
    count = lax.axis_size(axis)
    return lax.ppermute(x, axis, [(i, i + 1) for i in range(count - 1)])


def to_behind(x, axis):
    count = lax.axis_size(axis)
    return lax.ppermute(x, axis, [(i + 1, i) for i in range(count - 1)])


def shards(phase_init, flow_init, solid_mask, sensor_cells, sensor_weights):
    size_x, layers, size_z = solid_mask.shape
    corner = jnp.stack([lax.axis_index("tile") * size_x, lax.axis_index("vert") * size_z]).astype(jnp.int32)
    tile = (16, 128)
    up, down = call(rim_kernel, [(2, 4) + tile] * 2, n_in=3, flops=10**6, name="rim")(
        phase_init, flow_init, solid_mask
    )
    below = to_ahead(up, "vert")
    above = to_behind(down, "vert")
    state, right, left = call(
        ring_kernel, [(27, 8) + tile, (22,) + tile, (22,) + tile], scratch=[(8,) + tile], n_in=5, flops=10**7,
        name="ring",
    )(phase_init, flow_init, solid_mask, below, above)
    from_left = to_ahead(right, "tile")
    from_right = to_behind(left, "tile")
    (seed,) = call(probe_kernel, [(12,) + tile], scratch=[(192, 144)], n_smem=1, n_in=2, flops=2 * 10**9, name="probes")(
        corner, sensor_cells, sensor_weights.reshape(1, -1)
    )
    prim, adj, gamma, edges, right2, left2 = call(
        middle_kernel,
        [(10, 12) + tile, (19, 8) + tile, (8,) + tile, (4,) + tile, (9,) + tile, (9,) + tile],
        scratch=[
            (16,) + tile, (26, 12) + tile, (12,) + tile, (4, 8) + tile, (9, 12) + tile, (4, 8) + tile, (8,) + tile,
        ],
        n_in=4, flops=10**8, name="middle",
    )(state, from_left, from_right, seed)
    from_left2 = to_ahead(right2, "tile")
    from_right2 = to_behind(left2, "tile")
    out_g, out_f = call(
        last_kernel,
        [(7, 4) + tile, (19, 4) + tile],
        scratch=[(19, 4) + tile, (12,) + tile, (1, 8) + tile, (4, 8) + tile, (4, 8) + tile, (8,) + tile],
        n_in=7, flops=10**8, name="last",
    )(state, prim, adj, gamma, edges, from_left2, from_right2)
    return out_g, out_f


def solution(mesh):
    return jax.shard_map(
        shards,
        mesh=mesh,
        in_specs=(
            P(None, "tile", None, "vert"),
            P(None, "tile", None, "vert"),
            P("tile", None, "vert"),
            P(),
            P(),
        ),
        out_specs=(P(None, "tile", None, "vert"), P(None, "tile", None, "vert")),
        check_vma=False,
    )
```

```python
import functools

import jax
import jax.numpy as jnp
import numpy as np
from jax import lax
from jax.experimental import pallas as pl
from jax.experimental.pallas import tpu as pltpu
from jax.sharding import PartitionSpec as P

DIRS = [
    (0, 0, 0), (1, 0, 0), (-1, 0, 0), (0, 1, 0), (0, -1, 0), (0, 0, 1), (0, 0, -1),
    (1, 1, 0), (-1, -1, 0), (1, -1, 0), (-1, 1, 0), (1, 0, 1), (-1, 0, -1), (1, 0, -1),
    (-1, 0, 1), (0, 1, 1), (0, -1, -1), (0, 1, -1), (0, -1, 1),
]
BACK = [0, 2, 1, 4, 3, 6, 5, 8, 7, 10, 9, 12, 11, 14, 13, 16, 15, 18, 17]
W = [1.0 / 3.0] + [1.0 / 18.0] * 6 + [1.0 / 36.0] * 12
W0, W1, W2 = 1.0 / 3.0, 1.0 / 18.0, 1.0 / 36.0
PAIRS = [(q, q + 1) for q in range(1, 19, 2)]
TO_RIGHT = [q for q in range(19) if DIRS[q][0] == 1]
TO_LEFT = [q for q in range(19) if DIRS[q][0] == -1]
RIM = 8
SHARP = 0.075
FLUID = 26
F32 = jnp.float32
VMEM_LIMIT = 40 * 2**20


def lanes():
    return lax.broadcasted_iota(jnp.int32, (16, 128), 1)


def roll(x, shift, axis):
    shift = shift % x.shape[axis]
    return x if shift == 0 else pltpu.roll(x, shift, axis)


def load_pair(ref, *at):
    *head, row = at
    return (ref[(*head, 2 * row)], ref[(*head, 2 * row + 1)])


def store_pair(ref, pair, *at):
    *head, row = at
    ref[(*head, 2 * row)] = pair[0]
    ref[(*head, 2 * row + 1)] = pair[1]


def both(fn, *pairs):
    return tuple(fn(*each) for each in zip(*pairs))


def moved(pair, step_y, step_z):
    if step_y:
        pair = both(lambda t: roll(t, -step_y, 0), pair)
    if step_z:
        a = roll(pair[0], -step_z, 1)
        b = roll(pair[1], -step_z, 1)
        edge = lanes() == (127 if step_z > 0 else 0)
        pair = (jnp.where(edge, b, a), jnp.where(edge, a, b))
    return pair


def is_odd(axis):
    return jnp.full((16, 128), lax.rem(lax.axis_index(axis), 2), jnp.int32) == 1


def rim_slots(count, wide):
    slots, at = [], 0
    for k in range(count):
        width = 8 if k in wide else 4
        if at % 128 + 2 * width > 128:
            at += 128 - at % 128
        slots.append((at // 128, at % 128, width))
        at += 2 * width
    return slots


def message_tiles(count, wide=()):
    return count + rim_slots(count, wide)[-1][0] + 1


def packed(fields, wide):
    lane = lanes()
    out = [main for main, _ in fields]
    slots = rim_slots(len(fields), wide)
    for tile in range(slots[-1][0] + 1):
        acc = jnp.zeros((16, 128), F32)
        for (at, first, width), (_, rim) in zip(slots, fields):
            if at == tile:
                mine = (lane >= first) & (lane < first + 2 * width)
                acc = jnp.where(mine, roll(rim, first + width, 1), acc)
        out.append(acc)
    return out


def pack(odd_ref, even_ref, right, left, wide=()):
    odd = is_odd("tile")
    for n, (r, l) in enumerate(zip(packed(right, wide), packed(left, wide))):
        odd_ref[n] = jnp.where(odd, r, l)
        even_ref[n] = jnp.where(odd, l, r)


def received(odd_ref, even_ref, count, wide=()):
    odd = is_odd("tile")
    slots = rim_slots(count, wide)
    tiles = message_tiles(count, wide)
    got_odd = [odd_ref[n] for n in range(tiles)]
    got_even = [even_ref[n] for n in range(tiles)]
    sides = []
    for one, two in ((got_even, got_odd), (got_odd, got_even)):
        msg = [jnp.where(odd, a, b) for a, b in zip(one, two)]
        sides.append(
            [(msg[k], roll(msg[count + at], -(first + width), 1)) for k, (at, first, width) in enumerate(slots)]
        )
    return sides


def total(values):
    out = values[0]
    for value in values[1:]:
        out = out + value
    return out


def along(step, vec):
    out = None
    for c, v in zip(step, vec):
        if c == 0:
            continue
        if out is None:
            out = v if c > 0 else -v
        else:
            out = out + v if c > 0 else out - v
    return out


def momentum_of(pops, axis):
    plus = [pops[q] for q in range(19) if DIRS[q][axis] == 1]
    minus = [pops[q] for q in range(19) if DIRS[q][axis] == -1]
    return total([a - b for a, b in zip(plus, minus)])


def state_of(phi, mom, grad, lap):
    clipped = jnp.clip(phi, 0.0, 1.0)
    rho = 0.05 + 0.95 * clipped
    omega = 1.0 / (0.6 + 0.3 * clipped)
    inv_rho = 1.0 / rho
    potential = 1.2 * phi * (phi - 1.0) * (phi - 0.5) - 0.6 * lap
    force = (
        potential * grad[0] - 0.01 * rho,
        potential * grad[1],
        potential * grad[2] - 0.02 * (rho - 0.05),
    )
    half = 0.5 * inv_rho
    vel = tuple(m + f * half for m, f in zip(mom, force))
    kappa = (1.0 - 0.5 * omega) * inv_rho
    return dict(
        phi=phi, grad=grad, omega=omega, inv_rho=inv_rho, potential=potential, force=force,
        half=half, vel=vel, kappa=kappa,
    )


def dot(a, b):
    return a[0] * b[0] + a[1] * b[1] + a[2] * b[2]


def sharpening(s):
    inv_len = lax.rsqrt(dot(s["grad"], s["grad"]) + 0.01)
    return SHARP * s["phi"] * (1.0 - s["phi"]) * inv_len, inv_len


def carried_of(s, axis):
    sharp, _ = sharpening(s)
    return s["phi"] * s["vel"][axis] + sharp * s["grad"][axis]


def post_flow(pops, fluid, pressure, s, wanted):
    vel, force, omega, kappa = s["vel"], s["force"], s["omega"], s["kappa"]
    base = omega * (pressure - 1.5 * dot(vel, vel)) - 3.0 * kappa * dot(vel, force)
    odd_vec = tuple(3.0 * (omega * v + kappa * f) for v, f in zip(vel, force))
    even_vec = tuple(4.5 * omega * v + 9.0 * kappa * f for v, f in zip(vel, force))
    keep = 1.0 - omega
    out = {}
    if 0 in wanted:
        out[0] = jnp.where(fluid, keep * pops[0] + W0 * base, pops[0])
    for q, r in PAIRS:
        if q not in wanted and r not in wanted:
            continue
        step = DIRS[q]
        even = base + along(step, vel) * along(step, even_vec)
        odd = along(step, odd_vec)
        if q in wanted:
            out[q] = jnp.where(fluid, keep * pops[q] + W[q] * (even + odd), pops[r])
        if r in wanted:
            out[r] = jnp.where(fluid, keep * pops[r] + W[q] * (even - odd), pops[q])
    return out


def post_phase(pops, fluid, s, wanted):
    sharp, _ = sharpening(s)
    carried = tuple(s["phi"] * v + sharp * g for v, g in zip(s["vel"], s["grad"]))
    out = {}
    for q in wanted:
        if q == 0:
            out[q] = jnp.where(fluid, 0.3125 * s["phi"] - 0.25 * pops[0], pops[0])
        else:
            equil = 0.15625 * s["phi"] + 0.625 * along(DIRS[q], carried)
            out[q] = jnp.where(fluid, equil - 0.25 * pops[q], pops[BACK[q]])
    return out


def moments_of(adj):
    zero = None
    m0, m1 = [], [[], [], []]
    m2 = {}
    if 0 in adj:
        m0.append(W0 * adj[0])
    groups = {W1: [], W2: []}
    for q in range(1, 19):
        if q not in adj:
            continue
        a = adj[q]
        w = W[q]
        groups[w].append(a)
    for w, items in groups.items():
        if items:
            m0.append(w * total(items))

    def weighted(terms):
        parts = []
        for w in (W1, W2):
            mine = [(sign, a) for ww, sign, a in terms if ww == w]
            if not mine:
                continue
            acc = None
            for sign, a in mine:
                if acc is None:
                    acc = a if sign > 0 else -a
                else:
                    acc = acc + a if sign > 0 else acc - a
            parts.append(w * acc)
        return total(parts) if parts else None

    for i in range(3):
        m1[i] = weighted([(W[q], DIRS[q][i], adj[q]) for q in range(1, 19) if q in adj and DIRS[q][i]])
    for i in range(3):
        for j in range(i, 3):
            m2[(i, j)] = weighted(
                [
                    (W[q], DIRS[q][i] * DIRS[q][j], adj[q])
                    for q in range(1, 19)
                    if q in adj and DIRS[q][i] and DIRS[q][j]
                ]
            )
            m2[(j, i)] = m2[(i, j)]
    return total(m0), m1, m2


def apply_m2(m2, vec):
    out = []
    for i in range(3):
        terms = [m2[(i, j)] * vec[j] for j in range(3) if m2[(i, j)] is not None]
        out.append(total(terms))
    return out


def pull_stencil(s, m0, m1, m2, n1):
    vel, force = s["vel"], s["force"]
    omega, kappa, half = s["omega"], s["kappa"], s["half"]
    m2v = apply_m2(m2, vel)
    m2f = apply_m2(m2, force)
    m0_3 = 3.0 * m0
    lean = []
    for i in range(3):
        term = 9.0 * m2v[i] - m0_3 * vel[i]
        lean.append(term if m1[i] is None else term + 3.0 * m1[i])
    push = [9.0 * m2f[i] - m0_3 * force[i] for i in range(3)]
    d_vel = [omega * a + kappa * b for a, b in zip(lean, push)]
    if n1 is not None:
        five_phi = 5.0 * s["phi"]
        d_vel = [d + five_phi * n for d, n in zip(d_vel, n1)]
    d_force = [kappa * a + half * d for a, d in zip(lean, d_vel)]
    d_potential = dot(d_force, s["grad"])
    d_grad = [s["potential"] * x for x in d_force]
    if n1 is not None:
        sharp, inv_len = sharpening(s)
        tilt = dot(s["grad"], n1) * inv_len * inv_len
        sharp5 = 5.0 * sharp
        d_grad = [d + sharp5 * (n - g * tilt) for d, n, g in zip(d_grad, n1, s["grad"])]
    d_lap = -0.6 * d_potential
    return d_grad, d_lap, d_potential, d_force, d_vel, m2v, m2f


def inside_clip(phi):
    return jnp.where((phi > 0.0) & (phi < 1.0), 1.0, jnp.where((phi == 0.0) | (phi == 1.0), 0.5, 0.0))


def pull_all(s, pressure, adj, kept, m0, m1, m2, n0, n1):
    d_grad, d_lap, d_potential, d_force, d_vel, m2v, m2f = pull_stencil(s, m0, m1, m2, n1)
    phi, vel, force = s["phi"], s["vel"], s["force"]
    omega, kappa, inv_rho, half = s["omega"], s["kappa"], s["inv_rho"], s["half"]
    relaxed = m0 * (pressure - 1.5 * dot(vel, vel)) + 3.0 * dot(m1, vel) + 4.5 * dot(m2v, vel)
    forced = 3.0 * dot(m1, force) - 3.0 * m0 * dot(vel, force) + 9.0 * dot(m2v, force)
    d_omega = relaxed - kept - 0.5 * inv_rho * forced
    d_rho = (
        -kappa * inv_rho * forced
        - 0.01 * d_force[0]
        - 0.02 * d_force[2]
        - dot(d_vel, force) * half * inv_rho
    )
    d_clip = 0.95 * d_rho - 0.3 * omega * omega * d_omega
    d_phi = d_potential * (1.2 * (3.0 * phi * (phi - 1.0) + 0.5)) + d_clip * inside_clip(phi)
    if n1 is not None:
        _, inv_len = sharpening(s)
        d_phi = d_phi + 1.25 * n0 + 5.0 * (
            dot(n1, vel) + SHARP * (1.0 - 2.0 * phi) * inv_len * dot(n1, s["grad"])
        )
    d_pressure = omega * m0
    keep = 1.0 - omega
    kept_part = lambda q, rest: keep * adj[q] + rest if q in adj else rest
    d_flow = {0: kept_part(0, d_pressure)}
    for q, r in PAIRS:
        lift = along(DIRS[q], d_vel)
        d_flow[q] = kept_part(q, d_pressure + lift)
        d_flow[r] = kept_part(r, d_pressure - lift)
    return d_flow, d_phi, d_grad, d_lap


def pull_along_x(s, n0, n):
    phi, grad = s["phi"], s["grad"]
    sharp, inv_len = sharpening(s)
    d_vel = 5.0 * phi * n
    d_force = s["half"] * d_vel
    d_potential = d_force * grad[0]
    sharp5 = 5.0 * sharp
    tilt = sharp5 * (grad[0] * n * inv_len * inv_len)
    d_grad = [s["potential"] * d_force + sharp5 * n - grad[0] * tilt, -grad[1] * tilt, -grad[2] * tilt]
    d_rho = -0.01 * d_force - d_force * s["force"][0] * s["inv_rho"]
    d_phi = (
        d_potential * (1.2 * (3.0 * phi * (phi - 1.0) + 0.5))
        + 0.95 * d_rho * inside_clip(phi)
        + 1.25 * n0
        + 5.0 * n * (s["vel"][0] + SHARP * (1.0 - 2.0 * phi) * inv_len * grad[0])
    )
    return d_vel, d_phi, d_grad, -0.6 * d_potential


def gradients(behind, centre, ahead):
    ahead_y, behind_y = moved(centre, 1, 0), moved(centre, -1, 0)
    ahead_z, behind_z = moved(centre, 0, 1), moved(centre, 0, -1)
    diff = lambda a, b: 0.5 * (a - b)
    lap = both(
        lambda a, b, c, d, e, f, m: a + b + c + d + e + f - 6.0 * m,
        ahead, behind, ahead_y, behind_y, ahead_z, behind_z, centre,
    )
    return both(diff, ahead, behind), both(diff, ahead_y, behind_y), both(diff, ahead_z, behind_z), lap


def behind_part(d_grad, d_lap):
    return 0.5 * d_grad + d_lap


def ahead_part(d_grad, d_lap):
    return d_lap - 0.5 * d_grad


def rim_kernel(
    g_ref, f_ref, solid_ref, cells_ref, weights_ref,
    main_ref, probes_ref, probe_weights_ref, odd_ref, even_ref, mask_ref, sems,
):
    copies = [pltpu.make_async_copy(solid_ref, mask_ref, sems.at[0])]
    copies.append(pltpu.make_async_copy(g_ref, main_ref.at[pl.ds(0, 7)], sems.at[1]))
    for n, (first, count) in enumerate(((0, 5), (5, 5), (10, 5), (15, 4))):
        copies.append(
            pltpu.make_async_copy(
                f_ref.at[pl.ds(first, count)], main_ref.at[pl.ds(7 + first, count)], sems.at[2 + n]
            )
        )
    later = [pltpu.make_async_copy(weights_ref, probe_weights_ref, sems.at[6])]
    for i in range(3):
        later.append(pltpu.make_async_copy(cells_ref.at[:, i, :], probes_ref.at[i], sems.at[7 + i]))
    for copy in copies + later:
        copy.start()
    for copy in copies:
        copy.wait()
    lane = lanes()
    odd = is_odd("vert")

    def row(x, carry):
        main_ref[FLUID, x] = 1.0 - mask_ref[x].astype(F32)
        for tile in range(2):
            up = jnp.zeros((16, 128), F32)
            down = jnp.zeros((16, 128), F32)
            for slot in range(16):
                k = 16 * tile + slot
                if k > FLUID:
                    continue
                cells = main_ref[k, x]
                turned = roll(cells, 8 * slot + 8, 1)
                up = jnp.where(lane // RIM == slot, turned, up)
                down = jnp.where(lane // RIM == (slot + 1) % 16, turned, down)
            odd_ref[tile, x] = jnp.where(odd, up, down)
            even_ref[tile, x] = jnp.where(odd, down, up)
        return carry

    lax.fori_loop(0, 4, row, 0)
    for copy in later:
        copy.wait()


def ring_kernel(seeds_ref, main_ref, odd_in_ref, even_in_ref, rim_ref, phase_ref, odd_ref, even_ref):
    del seeds_ref
    lane = lanes()
    odd = is_odd("vert")

    def row(x, carry):
        above = [jnp.where(odd, odd_in_ref[t, x], even_in_ref[t, x]) for t in range(2)]
        below = [jnp.where(odd, even_in_ref[t, x], odd_in_ref[t, x]) for t in range(2)]
        even_group = lane // RIM % 2 == 0
        mixed = [
            (jnp.where(even_group, b, a), jnp.where(even_group, a, b)) for a, b in zip(above, below)
        ]
        sums = [None, None]
        for k in range(27):
            cells = main_ref[k, x]
            slot = k % 16
            rim = roll(mixed[k // 16][slot % 2], 120 - 8 * slot, 1)
            rim_ref[k, x] = rim
            if k < 7:
                sums = [a if b is None else a + b for a, b in zip((cells, rim), sums)]
        phase_ref[2 * x] = sums[0]
        phase_ref[2 * x + 1] = sums[1]
        return carry

    lax.fori_loop(0, 4, row, 0)

    def cells_of(k, row):
        return (main_ref[k, row], rim_ref[k, row])

    messages = []
    for edge, inner, crossing, out in ((3, 2, TO_RIGHT, 1), (0, 1, TO_LEFT, 2)):
        pops = [cells_of(7 + q, edge) for q in range(19)]
        g = [cells_of(q, edge) for q in range(7)]
        fluid = both(lambda a: a > 0.5, cells_of(FLUID, edge))
        phi = load_pair(phase_ref, edge)
        pressure = both(lambda *p: total(p), *pops)
        omega = both(lambda p: 1.0 / (0.6 + 0.3 * jnp.clip(p, 0.0, 1.0)), phi)
        fields = [
            both(
                lambda a, b, f, o, p: jnp.where(f, (1.0 - o) * a + W[q] * (o * p), b),
                pops[q], pops[BACK[q]], fluid, omega, pressure,
            )
            for q in crossing
        ]
        turn = lambda a, b, f: jnp.where(f, -0.25 * a, b)
        fields.append(both(turn, g[out], g[BACK[out]], fluid))
        parts = [both(turn, g[0], g[0], fluid)]
        for q in range(3, 7):
            parts.append(moved(both(turn, g[q], g[BACK[q]], fluid), -DIRS[q][1], -DIRS[q][2]))
        grads = gradients(*(load_pair(phase_ref, inner + d) for d in (-1, 0, 1)))
        inner_phi = load_pair(phase_ref, inner)
        inner_pops = [cells_of(7 + q, inner) for q in range(19)]
        crossing_phase = []
        for t in range(2):
            mom = [momentum_of([p[t] for p in inner_pops], 0)] + [jnp.zeros((16, 128), F32)] * 2
            s = state_of(inner_phi[t], mom, tuple(gr[t] for gr in grads[:3]), grads[3][t])
            equil = 0.15625 * inner_phi[t] + (0.625 if out == 1 else -0.625) * carried_of(s, 0)
            crossing_phase.append(
                jnp.where(
                    cells_of(FLUID, inner)[t] > 0.5,
                    equil - 0.25 * cells_of(out, inner)[t],
                    cells_of(BACK[out], inner)[t],
                )
            )
        parts.append(tuple(crossing_phase))
        fields.append(both(lambda *p: total(p), *parts))
        fields.append(phi)
        for axis in range(3):
            fields.append(both(lambda *p: momentum_of(p, axis), *pops))
        fields.append(cells_of(FLUID, edge))
        fields.append(inner_phi)
        messages.append(fields)
    pack(odd_ref, even_ref, *messages, wide=WIDE_FIRST)


SHIFTS = sorted({c[1:] for c in DIRS})
BF16 = jnp.bfloat16


def probe_kernel(probes_ref, weights_ref, out_ref, acc_ref, code_ref):
    first_x = lax.axis_index("tile") * 4
    first_z = lax.axis_index("vert") * 128
    acc_ref[...] = jnp.zeros_like(acc_ref)
    count = jnp.zeros((8, 128), jnp.int32)
    groups = probes_ref.shape[1] // 8
    for i in range(groups):
        at = slice(8 * i, 8 * i + 8)
        x = probes_ref[0, at, :] - (first_x - 1)
        y = probes_ref[1, at, :]
        z = probes_ref[2, at, :] - first_z
        here = (x >= 0) & (x < 6) & (z >= -RIM) & (z < 128 + RIM)
        ring = jnp.where(z >= 0, z, z + 144)
        code_ref[at, :] = jnp.where(here, (x * 16 + y) * 256 + ring, -1)
        count = count + here.astype(jnp.int32)
    passes = jnp.max(count)
    across = lax.broadcasted_iota(jnp.int32, (96, 128), 0).astype(F32).astype(BF16)
    height = lax.broadcasted_iota(jnp.int32, (144, 128), 0).astype(F32).astype(BF16)
    zero = jnp.zeros((), BF16)
    one = jnp.ones((), BF16)

    def one_pass(i, carry):
        code = jnp.full((8, 128), -1, jnp.int32)
        weight = jnp.zeros((8, 128), F32)
        for i in range(groups):
            at = slice(8 * i, 8 * i + 8)
            here = code_ref[at, :]
            take = (here >= 0) & (code < 0)
            code = jnp.where(take, here, code)
            weight = jnp.where(take, weights_ref[at, :], weight)
            code_ref[at, :] = jnp.where(take, -1, here)
        code_xy = (code >> 8).astype(F32)
        code_z = (code & 255).astype(F32)
        high = weight.astype(BF16).astype(F32)
        low = weight - high
        lhs, rhs = [], []
        for n in range(8):
            line = lambda v: v[n : n + 1, :].astype(BF16)
            hit = across == line(code_xy)
            lhs.append(
                jnp.concatenate([jnp.where(hit, line(high), zero), jnp.where(hit, line(low), zero)], axis=0)
            )
            rhs.append(jnp.where(height == line(code_z), one, zero))
        acc_ref[...] += lax.dot_general(
            jnp.concatenate(lhs, axis=1), jnp.concatenate(rhs, axis=1), (((1,), (1,)), ((), ())),
            preferred_element_type=F32,
        )
        return carry

    lax.fori_loop(0, passes, one_pass, 0)
    lane = lanes()
    for x in range(6):
        rows = pl.ds(16 * x, 16)
        lows = pl.ds(96 + 16 * x, 16)
        main = acc_ref[rows, 0:128] + acc_ref[lows, 0:128]
        rim = acc_ref[rows, 128:144] + acc_ref[lows, 128:144]
        rim = jnp.concatenate([rim, jnp.zeros((16, 112), F32)], axis=1)
        rim = jnp.where(lane < RIM, rim, jnp.where(lane >= 120, roll(rim, 112, 1), 0.0))
        for n, (cy, cz) in enumerate(SHIFTS):
            store_pair(out_ref, moved((main, rim), cy, cz), n, x)


N_FIRST = 13
WIDE_FIRST = (7,)
N_SECOND = 8
HALVES = (slice(0, 8), slice(8, 16))
M2_KEYS = ((0, 0), (0, 1), (0, 2), (1, 1), (1, 2), (2, 2))


def spot(refs, row):
    if row in (1, 2):
        return refs[0], row - 1
    return refs[1], {-1: 0, 0: 1, 3: 2, 4: 3}[row]


def prim_at(prims, row, t, h):
    ref, at = spot(prims, row)
    vals = [ref[k, 2 * at + t, h, :] for k in range(10)]
    return state_of(vals[0], vals[6:9], tuple(vals[1:4]), vals[4]), vals[5], vals[9] > 0.5


def put_gradients(prims, phase_pairs, row):
    ref, at = spot(prims, row)
    grads = gradients(*phase_pairs)
    store_pair(ref, phase_pairs[1], 0, at)
    for i in range(4):
        store_pair(ref, grads[i], 1 + i, at)


def forward(cells_ref, prims, posts, row, t):
    prim_ref, at = spot(prims, row)
    post_ref, _ = spot(posts, row)
    i = 2 * at + t
    for h in HALVES:
        g = [cells_ref[q, row, h, :] for q in range(7)]
        f = [cells_ref[7 + q, row, h, :] for q in range(19)]
        prim_ref[5, i, h, :] = total(f)
        for axis in range(3):
            prim_ref[6 + axis, i, h, :] = momentum_of(f, axis)
        prim_ref[9, i, h, :] = cells_ref[FLUID, row, h, :]
        s, pressure, fluid = prim_at(prims, row, t, h)
        for q, v in post_flow(f, fluid, pressure, s, range(19)).items():
            post_ref[7 + q, i, h, :] = v
        for q, v in post_phase(g, fluid, s, range(7)).items():
            post_ref[q, i, h, :] = v


def stream(posts, row):
    ref, at = spot(posts, row)
    for q in range(19):
        _, cy, cz = DIRS[q]
        if (cy or cz) and 0 <= row + DIRS[q][0] < 4:
            store_pair(ref, moved(load_pair(ref, 7 + q, at), -cy, -cz), 7 + q, at)


def inner_kernel(main_ref, rim_ref, phase_ref, seeds_ref, prim_ref, post_ref, moments_ref):
    prims, posts = (prim_ref, None), (post_ref, None)
    for row in (1, 2):
        put_gradients(prims, [load_pair(phase_ref, row + d) for d in (-1, 0, 1)], row)
        for t, cells_ref in enumerate((main_ref, rim_ref)):
            forward(cells_ref, prims, posts, row, t)
        stream(posts, row)

    def moments(i, carry):
        for h in HALVES:
            adj = {q: seeds_ref[SHIFTS.index(DIRS[q][1:]), i + 2 + 2 * DIRS[q][0], h, :] for q in range(19)}
            m0, m1, m2 = moments_of(adj)
            for k, v in enumerate([m0] + m1 + [m2[key] for key in M2_KEYS]):
                moments_ref[k, i, h, :] = v
        return carry

    lax.fori_loop(0, 8, moments, 0)


def middle_kernel(
    main_ref, rim_ref, phase_ref, odd_in_ref, even_in_ref, seeds_ref, moments_ref, prim_in_ref, post_in_ref,
    prim_ref, adj_ref, gamma_ref, edges_ref, odd_ref, even_ref,
    post_ref, phase_mid_ref, grad_mid_ref, back_ref, dphi_ref,
):
    prims, posts = (prim_in_ref, prim_ref), (post_in_ref, post_ref)
    from_left, from_right = received(odd_in_ref, even_in_ref, N_FIRST, WIDE_FIRST)
    sides = ((from_left, -1, TO_RIGHT, 1), (from_right, 4, TO_LEFT, 2))
    for got, row, crossing, out in sides:
        _, at = spot(prims, row)
        for i in range(3):
            store_pair(prim_ref, got[8 + i], 6 + i, at)
        store_pair(prim_ref, got[11], 9, at)
        for q, pair in zip(crossing, got[:5]):
            store_pair(post_ref, pair, 7 + q, at)
        store_pair(post_ref, got[5], out, at)
    phases = [from_left[12], from_left[7]] + [load_pair(phase_ref, r) for r in range(4)]
    phases += [from_right[7], from_right[12]]
    for row in (-1, 0, 3, 4):
        put_gradients(prims, phases[row + 1 : row + 4], row)
    for row in (0, 3):
        for t, cells_ref in enumerate((main_ref, rim_ref)):
            forward(cells_ref, prims, posts, row, t)
        stream(posts, row)

    mid_parts = {}
    for got, row, crossing, out in sides:
        _, at = spot(posts, row)
        spread = [[], [], []]
        for t in range(2):
            i = 2 * at + t
            halves = [[], [], []]
            for h in HALVES:
                vals = [prim_ref[k, i, h, :] for k in range(10) if k != 5]
                s = state_of(vals[0], vals[5:8], tuple(vals[1:4]), vals[4])
                fluid = vals[8] > 0.5
                vel, force, omega, kappa = s["vel"], s["force"], s["omega"], s["kappa"]
                base = -1.5 * omega * dot(vel, vel) - 3.0 * kappa * dot(vel, force)
                odd_vec = tuple(3.0 * (omega * v + kappa * f) for v, f in zip(vel, force))
                even_vec = tuple(4.5 * omega * v + 9.0 * kappa * f for v, f in zip(vel, force))
                for q in crossing:
                    step = DIRS[q]
                    gain = base + along(step, vel) * along(step, even_vec) + along(step, odd_vec)
                    kept = post_ref[7 + q, i, h, :]
                    post_ref[7 + q, i, h, :] = jnp.where(fluid, kept + W[q] * gain, kept)
                sharp, _ = sharpening(s)
                carried = tuple(s["phi"] * v + sharp * gr for v, gr in zip(vel, s["grad"]))
                kept = post_ref[out, i, h, :]
                gain = 0.15625 * s["phi"] + 0.625 * along(DIRS[out], carried)
                post_ref[out, i, h, :] = jnp.where(fluid, kept + gain, kept)
                halves[0].append(jnp.where(fluid, s["phi"], 0.0))
                halves[1].append(jnp.where(fluid, carried[1], 0.0))
                halves[2].append(jnp.where(fluid, carried[2], 0.0))
            for n in range(3):
                spread[n].append(jnp.concatenate(halves[n], axis=0))
        stream(posts, row)
        phi, cy, cz = (tuple(x) for x in spread)
        gain_y = lambda sign: both(lambda p, c: 0.15625 * p + sign * 0.625 * c, phi, cy)
        gain_z = lambda sign: both(lambda p, c: 0.15625 * p + sign * 0.625 * c, phi, cz)
        mid_parts[row] = [
            got[6], both(lambda p: 0.3125 * p, phi),
            moved(gain_y(1.0), -1, 0), moved(gain_y(-1.0), 1, 0),
            moved(gain_z(1.0), 0, -1), moved(gain_z(-1.0), 0, 1),
        ]
    def post_pair(q, row):
        ref, at = spot(posts, row)
        return load_pair(ref, q, at)

    for row in range(-1, 5):
        parts = mid_parts.get(row)
        if parts is None:
            parts = [post_pair(0, row)]
            for q in range(3, 7):
                parts.append(moved(post_pair(q, row), -DIRS[q][1], -DIRS[q][2]))
        if row > -1:
            parts.append(post_pair(1, row - 1))
        if row < 4:
            parts.append(post_pair(2, row + 1))
        store_pair(phase_mid_ref, both(lambda *p: total(p), *parts), row + 1)
    for row in range(4):
        grads = gradients(*(load_pair(phase_mid_ref, row + d) for d in (0, 1, 2)))
        for i in range(4):
            store_pair(grad_mid_ref, grads[i], i, row)
    def backward(row, t, h):
        i = 2 * row + t
        f = []
        for q in range(19):
            ref, at = spot(posts, row - DIRS[q][0])
            f.append(ref[7 + q, 2 * at + t, h, :])
        adj = {q: seeds_ref[SHIFTS.index(DIRS[q][1:]), i + 2 + 2 * DIRS[q][0], h, :] for q in range(19)}
        ref, at = spot(prims, row)
        fluid = ref[9, 2 * at + t, h, :] > 0.5
        phi = phase_mid_ref[i + 2, h, :]
        mom = [momentum_of(f, axis) for axis in range(3)]
        s = state_of(phi, mom, tuple(grad_mid_ref[k, i, h, :] for k in range(3)), grad_mid_ref[3, i, h, :])
        kept = total([adj[q] * f[q] for q in range(19)])
        m = [moments_ref[k, i, h, :] for k in range(10)]
        m2 = {}
        for key, value in zip(M2_KEYS, m[4:]):
            m2[key] = m2[key[::-1]] = value
        d_flow, d_phi, d_grad, d_lap = pull_all(s, total(f), adj, kept, m[0], m[1:4], m2, None, None)
        for q in range(19):
            adj_ref[q, i, h, :] = jnp.where(fluid, d_flow[q], adj[BACK[q]])
        dphi_ref[i, h, :] = jnp.where(fluid, d_phi, 0.0)
        for k in range(3):
            back_ref[k, i, h, :] = jnp.where(fluid, d_grad[k], 0.0)
        back_ref[3, i, h, :] = jnp.where(fluid, d_lap, 0.0)

    for row in range(4):
        for t in range(2):
            for h in HALVES:
                backward(row, t, h)

    for q in range(19):
        _, cy, cz = DIRS[q]
        if cy or cz:
            for row in range(4):
                store_pair(adj_ref, moved(load_pair(adj_ref, q, row), cy, cz), q, row)

    for row in range(4):
        store_pair(gamma_ref, stencil_back(back_ref, dphi_ref, row), row)
    edge_parts = []
    for row, part in ((0, ahead_part), (3, behind_part)):
        pair = both(part, load_pair(back_ref, 0, row), load_pair(back_ref, 3, row))
        store_pair(edges_ref, pair, 0 if row == 0 else 1)
        edge_parts.append(pair)

    messages = []
    for row, out_dirs, part, sign, edge_pair in (
        (3, TO_RIGHT, behind_part, -1.0, edge_parts[1]),
        (0, TO_LEFT, ahead_part, 1.0, edge_parts[0]),
    ):
        gamma = load_pair(gamma_ref, row)
        next_gamma = load_pair(gamma_ref, row - 1 if row == 3 else row + 1)
        n1 = turn_gamma(both(lambda a: sign * a, next_gamma), gamma)
        partial = []
        for t in range(2):
            s, _, fluid = prim_at(prims, row, t, slice(None))
            adj = {
                q: adj_ref[q, 2 * (row + DIRS[q][0]) + t] for q in range(19) if q not in out_dirs
            }
            m0, m1, m2 = moments_of(adj)
            d_grad, d_lap = pull_stencil(s, m0, m1, m2, [n[t] for n in n1])[:2]
            partial.append(jnp.where(fluid, part(d_grad[0], d_lap), 0.0))
        back_dirs = TO_LEFT if row == 3 else TO_RIGHT
        fields = [load_pair(adj_ref, q, row) for q in back_dirs]
        fields += [gamma, edge_pair, tuple(partial)]
        messages.append(fields)
    pack(odd_ref, even_ref, *messages)


def turn_gamma(along_x, centre):
    diff = lambda a, b: 0.125 * (a - b)
    return (
        both(lambda a: 0.125 * a, along_x),
        both(diff, moved(centre, 1, 0), moved(centre, -1, 0)),
        both(diff, moved(centre, 0, 1), moved(centre, 0, -1)),
    )


def stencil_back(back_ref, start_ref, row, first=None, last=None):
    gy, gz, lap = (load_pair(back_ref, k, row) for k in (1, 2, 3))
    fold = lambda l, gyb, gya, lyb, lya, gzb, gza, lzb, lza: (
        0.5 * (gyb - gya) + lyb + lya + 0.5 * (gzb - gza) + lzb + lza - 6.0 * l
    )
    out = both(
        fold, lap,
        moved(gy, -1, 0), moved(gy, 1, 0), moved(lap, -1, 0), moved(lap, 1, 0),
        moved(gz, 0, -1), moved(gz, 0, 1), moved(lap, 0, -1), moved(lap, 0, 1),
    )
    add = lambda a, b: a + b
    if start_ref is not None:
        out = both(add, out, load_pair(start_ref, row))
    if row > 0:
        out = both(add, out, both(behind_part, load_pair(back_ref, 0, row - 1), load_pair(back_ref, 3, row - 1)))
    elif first is not None:
        out = both(add, out, first)
    if row < 3:
        out = both(add, out, both(ahead_part, load_pair(back_ref, 0, row + 1), load_pair(back_ref, 3, row + 1)))
    elif last is not None:
        out = both(add, out, last)
    return out


def ahead_kernel(
    main_ref, prim_in_ref, prim_out_ref, adj_ref, gamma_ref,
    flow_ref, back_ref, dphi_ref,
    turned_ref,
):
    prims = (prim_in_ref, prim_out_ref)
    for row in (1, 2):
        centre = load_pair(gamma_ref, row)
        for n, (cy, cz) in enumerate(((1, 0), (-1, 0), (0, 1), (0, -1))):
            store_pair(turned_ref, moved(centre, cy, cz), n, row - 1)
    for row in range(4):
        for t in range(2):
            for h in HALVES:
                i = 2 * row + t
                s, pressure, fluid = prim_at(prims, row, t, h)
                adj = {
                    q: adj_ref[q, i + 2 * DIRS[q][0], h, :] for q in range(19) if 0 <= row + DIRS[q][0] < 4
                }
                m0, m1, m2 = moments_of(adj)
                n0 = n1 = None
                if row in (1, 2):
                    g = [gamma_ref[i + 2, h, :], gamma_ref[i - 2, h, :]]
                    g += [turned_ref[n, i - 2, h, :] for n in range(4)]
                    n1 = [0.125 * (g[a] - g[a + 1]) for a in (0, 2, 4)]
                if t == 1:
                    d_grad, d_lap = pull_stencil(s, m0, m1, m2, n1)[:2]
                else:
                    if row in (1, 2):
                        n0 = 0.25 * gamma_ref[i, h, :] + 0.125 * total(g)
                    kept = total([a * main_ref[7 + q, row, h, :] for q, a in adj.items()])
                    d_flow, d_phi, d_grad, d_lap = pull_all(s, pressure, adj, kept, m0, m1, m2, n0, n1)
                    for q in range(19):
                        flow_ref[q, row, h, :] = jnp.where(fluid, d_flow[q], adj.get(BACK[q], 0.0))
                    dphi_ref[row, h, :] = jnp.where(fluid, d_phi, 0.0)
                for k in range(3):
                    back_ref[k, i, h, :] = jnp.where(fluid, d_grad[k], 0.0)
                back_ref[3, i, h, :] = jnp.where(fluid, d_lap, 0.0)


def last_kernel(
    main_ref, prim_in_ref, prim_out_ref, adj_ref, gamma_ref, edges_ref, flow_ref, back_in_ref, dphi_in_ref,
    odd_in_ref, even_in_ref,
    out_g_ref, out_f_ref,
    gamma_wide_ref, turned_ref, back_ref, dphi_ref, g_ref, f_ref, sems,
):
    add = lambda a, b: a + b
    prims = (prim_in_ref, prim_out_ref)
    copies = []

    def send(src, dst):
        copies.append(pltpu.make_async_copy(src, dst, sems.at[len(copies)]))
        copies[-1].start()

    got_left, got_right = received(odd_in_ref, even_in_ref, N_SECOND)
    own_first = load_pair(edges_ref, 0)
    own_last = load_pair(edges_ref, 1)

    for row, more, sign in ((1, got_left[6], -0.125), (2, got_right[6], 0.125)):
        for t in range(2):
            for n, h in enumerate(HALVES):
                i = 2 * row + t
                s, _, fluid = prim_at(prims, row, t, h)
                delta = more[t][8 * n : 8 * n + 8]
                d_vel, d_phi, d_grad, d_lap = pull_along_x(s, 0.125 * delta, sign * delta)
                if t == 0:
                    lift = jnp.where(fluid, d_vel, 0.0)
                    for q in range(19):
                        base = flow_ref[q, row, h, :]
                        f_ref[q, row, h, :] = base + DIRS[q][0] * lift if DIRS[q][0] else base
                    dphi_ref[row, h, :] = dphi_in_ref[row, h, :] + jnp.where(fluid, d_phi, 0.0)
                for k in range(3):
                    back_ref[k, i, h, :] = back_in_ref[k, i, h, :] + jnp.where(fluid, d_grad[k], 0.0)
                back_ref[3, i, h, :] = back_in_ref[3, i, h, :] + jnp.where(fluid, d_lap, 0.0)
    send(f_ref.at[:, pl.ds(1, 2)], out_f_ref.at[:, pl.ds(1, 2)])

    for row in (1, 2):
        store_pair(gamma_wide_ref, load_pair(gamma_ref, row), row + 1)
    store_pair(gamma_wide_ref, both(add, load_pair(gamma_ref, 0), got_left[6]), 1)
    store_pair(gamma_wide_ref, both(add, load_pair(gamma_ref, 3), got_right[6]), 4)
    store_pair(gamma_wide_ref, both(add, got_left[5], own_first), 0)
    store_pair(gamma_wide_ref, both(add, got_right[5], own_last), 5)
    for row in range(4):
        centre = load_pair(gamma_wide_ref, row + 1)
        for n, (cy, cz) in enumerate(((1, 0), (-1, 0), (0, 1), (0, -1))):
            store_pair(turned_ref, moved(centre, cy, cz), n, row)

    def phase_adjoints(i, h):
        at = [gamma_wide_ref[i + 2, h, :], gamma_wide_ref[i + 4, h, :], gamma_wide_ref[i, h, :]]
        return at + [turned_ref[n, i, h, :] for n in range(4)]

    for row, got, dirs in ((0, got_left, TO_LEFT), (3, got_right, TO_RIGHT)):
        for t in range(2):
            for n, h in enumerate(HALVES):
                i = 2 * row + t
                s, pressure, fluid = prim_at(prims, row, t, h)
                adj = {q: pair[t][8 * n : 8 * n + 8] for q, pair in zip(dirs, got[:5])}
                g = phase_adjoints(i, h)
                n1 = [0.125 * (g[a] - g[a + 1]) for a in (1, 3, 5)]
                m0, m1, m2 = moments_of(adj)
                if t == 1:
                    d_grad, d_lap = pull_stencil(s, m0, m1, m2, n1)[:2]
                else:
                    n0 = 0.25 * g[0] + 0.125 * total(g[1:])
                    kept = total([a * main_ref[7 + q, row, h, :] for q, a in adj.items()])
                    d_flow, d_phi, d_grad, d_lap = pull_all(s, pressure, adj, kept, m0, m1, m2, n0, n1)
                    for q in range(19):
                        more = jnp.where(fluid, d_flow[q], adj.get(BACK[q], 0.0))
                        f_ref[q, row, h, :] = flow_ref[q, row, h, :] + more
                    dphi_ref[row, h, :] = dphi_in_ref[row, h, :] + jnp.where(fluid, d_phi, 0.0)
                for k in range(3):
                    back_ref[k, i, h, :] = back_in_ref[k, i, h, :] + jnp.where(fluid, d_grad[k], 0.0)
                back_ref[3, i, h, :] = back_in_ref[3, i, h, :] + jnp.where(fluid, d_lap, 0.0)
        send(f_ref.at[:, pl.ds(row, 1)], out_f_ref.at[:, pl.ds(row, 1)])

    edge_parts = []
    for got, prim_row, row, own, out_dirs, part, sign in (
        (got_left, -1, 0, own_first, TO_RIGHT, behind_part, 1.0),
        (got_right, 4, 3, own_last, TO_LEFT, ahead_part, -1.0),
    ):
        gamma = load_pair(gamma_wide_ref, row + 1)
        n1 = turn_gamma(both(lambda a: sign * a, gamma), own)
        pair = []
        for t in range(2):
            s, _, fluid = prim_at(prims, prim_row, t, slice(None))
            adj = {q: adj_ref[q, 2 * row + t] for q in out_dirs}
            m0, m1, m2 = moments_of(adj)
            d_grad, d_lap = pull_stencil(s, m0, m1, m2, [n[t] for n in n1])[:2]
            pair.append(got[7][t] + jnp.where(fluid, part(d_grad[0], d_lap), 0.0))
        edge_parts.append(tuple(pair))

    for row in range(4):
        rest = stencil_back(back_ref, None, row, edge_parts[0], edge_parts[1])[0]
        ref, at = spot(prims, row)
        fluid = ref[9, 2 * at] > 0.5
        base = rest + dphi_ref[row]
        phase_adj = phase_adjoints(2 * row, slice(None))
        for q in range(7):
            g_ref[q, row] = jnp.where(fluid, base - 0.25 * phase_adj[q], rest + phase_adj[BACK[q]])
    send(g_ref, out_g_ref)
    for copy in copies:
        copy.wait()


def call(kernel, outs, n_in, scratch=(), flops=0, name=None, any_in=0, any_out=False):
    vmem = pl.BlockSpec(memory_space=pltpu.VMEM)
    return pl.pallas_call(
        kernel,
        out_shape=[jax.ShapeDtypeStruct(x, F32) if isinstance(x, tuple) else x for x in outs],
        in_specs=[pl.BlockSpec(memory_space=pl.ANY)] * any_in + [vmem] * (n_in - any_in),
        out_specs=[pl.BlockSpec(memory_space=pl.ANY) if any_out else vmem] * len(outs),
        scratch_shapes=[pltpu.VMEM(x, F32) if isinstance(x, tuple) else x for x in scratch],
        compiler_params=pltpu.CompilerParams(vmem_limit_bytes=VMEM_LIMIT),
        cost_estimate=pl.CostEstimate(flops=flops, bytes_accessed=flops // 8, transcendentals=0),
        name=name,
    )


def swap(x, axis, first):
    pairs = []
    for i in range(first, lax.axis_size(axis) - 1, 2):
        pairs += [(i, i + 1), (i + 1, i)]
    return lax.ppermute(x, axis, pairs)


def shards(phase_init, flow_init, solid_mask, sensor_cells, sensor_weights):
    tile = (16, 128)
    cells = sensor_cells.reshape(3, -1, 128).transpose(1, 0, 2)
    weights = sensor_weights.reshape(-1, 128)
    main, probes, weights, odd, even = call(
        rim_kernel,
        [(27, 4) + tile, jax.ShapeDtypeStruct((3,) + weights.shape, jnp.int32), weights.shape] + [(2, 4) + tile] * 2,
        5, any_in=5, flops=10**6, name="rim",
        scratch=[pltpu.VMEM((4,) + tile, jnp.int32), pltpu.SemaphoreType.DMA((10,))],
    )(*(pltpu.with_memory_space_constraint(x, pltpu.HBM) for x in (phase_init, flow_init, solid_mask, cells, weights)))
    odd, even = swap(odd, "vert", 1), swap(even, "vert", 0)
    (seeds,) = call(probe_kernel, [(9, 12) + tile], 2, scratch=[(192, 144), pltpu.VMEM(weights.shape, jnp.int32)], flops=2 * 10**9, name="probes")(
        probes, weights
    )
    first = message_tiles(N_FIRST, WIDE_FIRST)
    rim, phase, odd, even = call(
        ring_kernel, [(27, 4) + tile, (8,) + tile] + [(first,) + tile] * 2, 4, any_in=1, flops=10**7, name="ring"
    )(seeds, main, odd, even)
    odd, even = swap(odd, "tile", 1), swap(even, "tile", 0)
    prim_in, post_in, moments = call(
        inner_kernel, [(10, 4) + tile, (26, 4) + tile, (10, 8) + tile], 4, flops=2 * 10**8, name="inner"
    )(main, rim, phase, seeds)
    second = message_tiles(N_SECOND)
    prim_out, adj, gamma, edges, odd, even = call(
        middle_kernel,
        [(10, 8) + tile, (19, 8) + tile, (8,) + tile, (4,) + tile] + [(second,) + tile] * 2,
        9,
        scratch=[(26, 8) + tile, (12,) + tile, (4, 8) + tile, (4, 8) + tile, (8,) + tile],
        flops=10**8, name="middle",
    )(main, rim, phase, odd, even, seeds, moments, prim_in, post_in)
    odd, even = swap(odd, "tile", 1), swap(even, "tile", 0)
    flow, back, dphi = call(
        ahead_kernel, [(19, 4) + tile, (4, 8) + tile, (4,) + tile], 5, scratch=[(4, 4) + tile], flops=2 * 10**8,
        name="ahead",
    )(main, prim_in, prim_out, adj, gamma)
    return tuple(
        call(
            last_kernel,
            [(7, 4) + tile, (19, 4) + tile],
            11,
            scratch=[
                (12,) + tile, (4, 8) + tile, (4, 8) + tile, (4,) + tile, (7, 4) + tile, (19, 4) + tile,
                pltpu.SemaphoreType.DMA((4,)),
            ],
            flops=10**8, name="last", any_out=True,
        )(main, prim_in, prim_out, adj, gamma, edges, flow, back, dphi, odd, even)
    )


def solution(mesh):
    return jax.shard_map(
        shards,
        mesh=mesh,
        in_specs=(
            P(None, "tile", None, "vert"),
            P(None, "tile", None, "vert"),
            P("tile", None, "vert"),
            P(),
            P(),
        ),
        out_specs=(P(None, "tile", None, "vert"), P(None, "tile", None, "vert")),
        check_vma=False,
    )
```

```python
import functools

import jax
import jax.numpy as jnp
import numpy as np
from jax import lax
from jax.experimental import pallas as pl
from jax.experimental.pallas import tpu as pltpu
from jax.sharding import PartitionSpec as P

DIRS = [
    (0, 0, 0), (1, 0, 0), (-1, 0, 0), (0, 1, 0), (0, -1, 0), (0, 0, 1), (0, 0, -1),
    (1, 1, 0), (-1, -1, 0), (1, -1, 0), (-1, 1, 0), (1, 0, 1), (-1, 0, -1), (1, 0, -1),
    (-1, 0, 1), (0, 1, 1), (0, -1, -1), (0, 1, -1), (0, -1, 1),
]
BACK = [0, 2, 1, 4, 3, 6, 5, 8, 7, 10, 9, 12, 11, 14, 13, 16, 15, 18, 17]
W = [1.0 / 3.0] + [1.0 / 18.0] * 6 + [1.0 / 36.0] * 12
W0, W1, W2 = 1.0 / 3.0, 1.0 / 18.0, 1.0 / 36.0
PAIRS = [(q, q + 1) for q in range(1, 19, 2)]
TO_RIGHT = [q for q in range(19) if DIRS[q][0] == 1]
TO_LEFT = [q for q in range(19) if DIRS[q][0] == -1]
RIM = 8
SHARP = 0.075
FLUID = 26
F32 = jnp.float32
VMEM_LIMIT = 40 * 2**20


def lanes():
    return lax.broadcasted_iota(jnp.int32, (16, 128), 1)


def roll(x, shift, axis):
    shift = shift % x.shape[axis]
    return x if shift == 0 else pltpu.roll(x, shift, axis)


def load_pair(ref, *at):
    *head, row = at
    return (ref[(*head, 2 * row)], ref[(*head, 2 * row + 1)])


def store_pair(ref, pair, *at):
    *head, row = at
    ref[(*head, 2 * row)] = pair[0]
    ref[(*head, 2 * row + 1)] = pair[1]


def both(fn, *pairs):
    return tuple(fn(*each) for each in zip(*pairs))


def moved(pair, step_y, step_z):
    if step_y:
        pair = both(lambda t: roll(t, -step_y, 0), pair)
    if step_z:
        a = roll(pair[0], -step_z, 1)
        b = roll(pair[1], -step_z, 1)
        edge = lanes() == (127 if step_z > 0 else 0)
        pair = (jnp.where(edge, b, a), jnp.where(edge, a, b))
    return pair


def is_odd(axis):
    return jnp.full((16, 128), lax.rem(lax.axis_index(axis), 2), jnp.int32) == 1


def rim_slots(count, wide):
    slots, at = [], 0
    for k in range(count):
        width = 8 if k in wide else 4
        if at % 128 + 2 * width > 128:
            at += 128 - at % 128
        slots.append((at // 128, at % 128, width))
        at += 2 * width
    return slots


def message_tiles(count, wide=()):
    return count + rim_slots(count, wide)[-1][0] + 1


def packed(fields, wide):
    lane = lanes()
    out = [main for main, _ in fields]
    slots = rim_slots(len(fields), wide)
    for tile in range(slots[-1][0] + 1):
        acc = jnp.zeros((16, 128), F32)
        for (at, first, width), (_, rim) in zip(slots, fields):
            if at == tile:
                mine = (lane >= first) & (lane < first + 2 * width)
                acc = jnp.where(mine, roll(rim, first + width, 1), acc)
        out.append(acc)
    return out


def pack(odd_ref, even_ref, right, left, wide=()):
    odd = is_odd("tile")
    for n, (r, l) in enumerate(zip(packed(right, wide), packed(left, wide))):
        odd_ref[n] = jnp.where(odd, r, l)
        even_ref[n] = jnp.where(odd, l, r)


def received(odd_ref, even_ref, count, wide=()):
    odd = is_odd("tile")
    slots = rim_slots(count, wide)
    tiles = message_tiles(count, wide)
    at = lax.axis_index("tile")
    last = lax.axis_size("tile") - 1
    parity = lax.rem(at, 2)
    ends = jnp.full((16, 128), jnp.where((at == 0) | (at == last), 1, 0), jnp.int32) == 1
    got_odd = [jnp.where(ends, 0.0, odd_ref[parity, n]) for n in range(tiles)]
    got_even = [even_ref[1 - parity, n] for n in range(tiles)]
    sides = []
    for one, two in ((got_even, got_odd), (got_odd, got_even)):
        msg = [jnp.where(odd, a, b) for a, b in zip(one, two)]
        sides.append(
            [(msg[k], roll(msg[count + at], -(first + width), 1)) for k, (at, first, width) in enumerate(slots)]
        )
    return sides


def total(values):
    out = values[0]
    for value in values[1:]:
        out = out + value
    return out


def along(step, vec):
    out = None
    for c, v in zip(step, vec):
        if c == 0:
            continue
        if out is None:
            out = v if c > 0 else -v
        else:
            out = out + v if c > 0 else out - v
    return out


def momentum_of(pops, axis):
    plus = [pops[q] for q in range(19) if DIRS[q][axis] == 1]
    minus = [pops[q] for q in range(19) if DIRS[q][axis] == -1]
    return total([a - b for a, b in zip(plus, minus)])


def state_of(phi, mom, grad, lap):
    clipped = jnp.clip(phi, 0.0, 1.0)
    rho = 0.05 + 0.95 * clipped
    omega = 1.0 / (0.6 + 0.3 * clipped)
    inv_rho = 1.0 / rho
    potential = 1.2 * phi * (phi - 1.0) * (phi - 0.5) - 0.6 * lap
    force = (
        potential * grad[0] - 0.01 * rho,
        potential * grad[1],
        potential * grad[2] - 0.02 * (rho - 0.05),
    )
    half = 0.5 * inv_rho
    vel = tuple(m + f * half for m, f in zip(mom, force))
    kappa = (1.0 - 0.5 * omega) * inv_rho
    return dict(
        phi=phi, grad=grad, omega=omega, inv_rho=inv_rho, potential=potential, force=force,
        half=half, vel=vel, kappa=kappa,
    )


def dot(a, b):
    return a[0] * b[0] + a[1] * b[1] + a[2] * b[2]


def sharpening(s):
    inv_len = lax.rsqrt(dot(s["grad"], s["grad"]) + 0.01)
    return SHARP * s["phi"] * (1.0 - s["phi"]) * inv_len, inv_len


def carried_of(s, axis):
    sharp, _ = sharpening(s)
    return s["phi"] * s["vel"][axis] + sharp * s["grad"][axis]


def post_flow(pops, fluid, pressure, s, wanted):
    vel, force, omega, kappa = s["vel"], s["force"], s["omega"], s["kappa"]
    base = omega * (pressure - 1.5 * dot(vel, vel)) - 3.0 * kappa * dot(vel, force)
    odd_vec = tuple(3.0 * (omega * v + kappa * f) for v, f in zip(vel, force))
    even_vec = tuple(4.5 * omega * v + 9.0 * kappa * f for v, f in zip(vel, force))
    keep = 1.0 - omega
    out = {}
    if 0 in wanted:
        out[0] = jnp.where(fluid, keep * pops[0] + W0 * base, pops[0])
    for q, r in PAIRS:
        if q not in wanted and r not in wanted:
            continue
        step = DIRS[q]
        even = base + along(step, vel) * along(step, even_vec)
        odd = along(step, odd_vec)
        if q in wanted:
            out[q] = jnp.where(fluid, keep * pops[q] + W[q] * (even + odd), pops[r])
        if r in wanted:
            out[r] = jnp.where(fluid, keep * pops[r] + W[q] * (even - odd), pops[q])
    return out


def post_phase(pops, fluid, s, wanted):
    sharp, _ = sharpening(s)
    carried = tuple(s["phi"] * v + sharp * g for v, g in zip(s["vel"], s["grad"]))
    out = {}
    for q in wanted:
        if q == 0:
            out[q] = jnp.where(fluid, 0.3125 * s["phi"] - 0.25 * pops[0], pops[0])
        else:
            equil = 0.15625 * s["phi"] + 0.625 * along(DIRS[q], carried)
            out[q] = jnp.where(fluid, equil - 0.25 * pops[q], pops[BACK[q]])
    return out


def moments_of(adj):
    zero = None
    m0, m1 = [], [[], [], []]
    m2 = {}
    if 0 in adj:
        m0.append(W0 * adj[0])
    groups = {W1: [], W2: []}
    for q in range(1, 19):
        if q not in adj:
            continue
        a = adj[q]
        w = W[q]
        groups[w].append(a)
    for w, items in groups.items():
        if items:
            m0.append(w * total(items))

    def weighted(terms):
        parts = []
        for w in (W1, W2):
            mine = [(sign, a) for ww, sign, a in terms if ww == w]
            if not mine:
                continue
            acc = None
            for sign, a in mine:
                if acc is None:
                    acc = a if sign > 0 else -a
                else:
                    acc = acc + a if sign > 0 else acc - a
            parts.append(w * acc)
        return total(parts) if parts else None

    for i in range(3):
        m1[i] = weighted([(W[q], DIRS[q][i], adj[q]) for q in range(1, 19) if q in adj and DIRS[q][i]])
    for i in range(3):
        for j in range(i, 3):
            m2[(i, j)] = weighted(
                [
                    (W[q], DIRS[q][i] * DIRS[q][j], adj[q])
                    for q in range(1, 19)
                    if q in adj and DIRS[q][i] and DIRS[q][j]
                ]
            )
            m2[(j, i)] = m2[(i, j)]
    return total(m0), m1, m2


def apply_m2(m2, vec):
    out = []
    for i in range(3):
        terms = [m2[(i, j)] * vec[j] for j in range(3) if m2[(i, j)] is not None]
        out.append(total(terms))
    return out


def pull_stencil(s, m0, m1, m2, n1):
    vel, force = s["vel"], s["force"]
    omega, kappa, half = s["omega"], s["kappa"], s["half"]
    m2v = apply_m2(m2, vel)
    m2f = apply_m2(m2, force)
    m0_3 = 3.0 * m0
    lean = []
    for i in range(3):
        term = 9.0 * m2v[i] - m0_3 * vel[i]
        lean.append(term if m1[i] is None else term + 3.0 * m1[i])
    push = [9.0 * m2f[i] - m0_3 * force[i] for i in range(3)]
    d_vel = [omega * a + kappa * b for a, b in zip(lean, push)]
    if n1 is not None:
        five_phi = 5.0 * s["phi"]
        d_vel = [d + five_phi * n for d, n in zip(d_vel, n1)]
    d_force = [kappa * a + half * d for a, d in zip(lean, d_vel)]
    d_potential = dot(d_force, s["grad"])
    d_grad = [s["potential"] * x for x in d_force]
    if n1 is not None:
        sharp, inv_len = sharpening(s)
        tilt = dot(s["grad"], n1) * inv_len * inv_len
        sharp5 = 5.0 * sharp
        d_grad = [d + sharp5 * (n - g * tilt) for d, n, g in zip(d_grad, n1, s["grad"])]
    d_lap = -0.6 * d_potential
    return d_grad, d_lap, d_potential, d_force, d_vel, m2v, m2f


def inside_clip(phi):
    return jnp.where((phi > 0.0) & (phi < 1.0), 1.0, jnp.where((phi == 0.0) | (phi == 1.0), 0.5, 0.0))


def pull_all(s, pressure, adj, kept, m0, m1, m2, n0, n1):
    d_grad, d_lap, d_potential, d_force, d_vel, m2v, m2f = pull_stencil(s, m0, m1, m2, n1)
    phi, vel, force = s["phi"], s["vel"], s["force"]
    omega, kappa, inv_rho, half = s["omega"], s["kappa"], s["inv_rho"], s["half"]
    relaxed = m0 * (pressure - 1.5 * dot(vel, vel)) + 3.0 * dot(m1, vel) + 4.5 * dot(m2v, vel)
    forced = 3.0 * dot(m1, force) - 3.0 * m0 * dot(vel, force) + 9.0 * dot(m2v, force)
    d_omega = relaxed - kept - 0.5 * inv_rho * forced
    d_rho = (
        -kappa * inv_rho * forced
        - 0.01 * d_force[0]
        - 0.02 * d_force[2]
        - dot(d_vel, force) * half * inv_rho
    )
    d_clip = 0.95 * d_rho - 0.3 * omega * omega * d_omega
    d_phi = d_potential * (1.2 * (3.0 * phi * (phi - 1.0) + 0.5)) + d_clip * inside_clip(phi)
    if n1 is not None:
        _, inv_len = sharpening(s)
        d_phi = d_phi + 1.25 * n0 + 5.0 * (
            dot(n1, vel) + SHARP * (1.0 - 2.0 * phi) * inv_len * dot(n1, s["grad"])
        )
    d_pressure = omega * m0
    keep = 1.0 - omega
    kept_part = lambda q, rest: keep * adj[q] + rest if q in adj else rest
    d_flow = {0: kept_part(0, d_pressure)}
    for q, r in PAIRS:
        lift = along(DIRS[q], d_vel)
        d_flow[q] = kept_part(q, d_pressure + lift)
        d_flow[r] = kept_part(r, d_pressure - lift)
    return d_flow, d_phi, d_grad, d_lap


def pull_along_x(s, n0, n):
    phi, grad = s["phi"], s["grad"]
    sharp, inv_len = sharpening(s)
    d_vel = 5.0 * phi * n
    d_force = s["half"] * d_vel
    d_potential = d_force * grad[0]
    sharp5 = 5.0 * sharp
    tilt = sharp5 * (grad[0] * n * inv_len * inv_len)
    d_grad = [s["potential"] * d_force + sharp5 * n - grad[0] * tilt, -grad[1] * tilt, -grad[2] * tilt]
    d_rho = -0.01 * d_force - d_force * s["force"][0] * s["inv_rho"]
    d_phi = (
        d_potential * (1.2 * (3.0 * phi * (phi - 1.0) + 0.5))
        + 0.95 * d_rho * inside_clip(phi)
        + 1.25 * n0
        + 5.0 * n * (s["vel"][0] + SHARP * (1.0 - 2.0 * phi) * inv_len * grad[0])
    )
    return d_vel, d_phi, d_grad, -0.6 * d_potential


def gradients(behind, centre, ahead):
    ahead_y, behind_y = moved(centre, 1, 0), moved(centre, -1, 0)
    ahead_z, behind_z = moved(centre, 0, 1), moved(centre, 0, -1)
    diff = lambda a, b: 0.5 * (a - b)
    lap = both(
        lambda a, b, c, d, e, f, m: a + b + c + d + e + f - 6.0 * m,
        ahead, behind, ahead_y, behind_y, ahead_z, behind_z, centre,
    )
    return both(diff, ahead, behind), both(diff, ahead_y, behind_y), both(diff, ahead_z, behind_z), lap


def behind_part(d_grad, d_lap):
    return 0.5 * d_grad + d_lap


def ahead_part(d_grad, d_lap):
    return d_lap - 0.5 * d_grad


def rim_kernel(
    g_ref, f_ref, solid_ref, cells_ref, weights_ref,
    main_ref, probes_ref, probe_weights_ref, odd_ref, even_ref, mask_ref, sems,
):
    copies = [pltpu.make_async_copy(solid_ref, mask_ref, sems.at[0])]
    copies.append(pltpu.make_async_copy(g_ref, main_ref.at[pl.ds(0, 7)], sems.at[1]))
    for n, (first, count) in enumerate(((0, 5), (5, 5), (10, 5), (15, 4))):
        copies.append(
            pltpu.make_async_copy(
                f_ref.at[pl.ds(first, count)], main_ref.at[pl.ds(7 + first, count)], sems.at[2 + n]
            )
        )
    later = [pltpu.make_async_copy(weights_ref, probe_weights_ref, sems.at[6])]
    for i in range(3):
        later.append(pltpu.make_async_copy(cells_ref.at[:, i, :], probes_ref.at[i], sems.at[7 + i]))
    for copy in copies + later:
        copy.start()
    for copy in copies:
        copy.wait()
    lane = lanes()
    odd = is_odd("vert")

    def row(x, carry):
        main_ref[FLUID, x] = 1.0 - mask_ref[x].astype(F32)
        for tile in range(2):
            up = jnp.zeros((16, 128), F32)
            down = jnp.zeros((16, 128), F32)
            for slot in range(16):
                k = 16 * tile + slot
                if k > FLUID:
                    continue
                cells = main_ref[k, x]
                turned = roll(cells, 8 * slot + 8, 1)
                up = jnp.where(lane // RIM == slot, turned, up)
                down = jnp.where(lane // RIM == (slot + 1) % 16, turned, down)
            odd_ref[tile, x] = jnp.where(odd, up, down)
            even_ref[tile, x] = jnp.where(odd, down, up)
        return carry

    lax.fori_loop(0, 4, row, 0)
    for copy in later:
        copy.wait()


def ring_kernel(seeds_ref, main_ref, odd_in_ref, even_in_ref, rim_ref, phase_ref, odd_ref, even_ref):
    del seeds_ref
    lane = lanes()
    odd = is_odd("vert")

    def row(x, carry):
        above = [jnp.where(odd, odd_in_ref[t, x], even_in_ref[t, x]) for t in range(2)]
        below = [jnp.where(odd, even_in_ref[t, x], odd_in_ref[t, x]) for t in range(2)]
        even_group = lane // RIM % 2 == 0
        mixed = [
            (jnp.where(even_group, b, a), jnp.where(even_group, a, b)) for a, b in zip(above, below)
        ]
        sums = [None, None]
        for k in range(27):
            cells = main_ref[k, x]
            slot = k % 16
            rim = roll(mixed[k // 16][slot % 2], 120 - 8 * slot, 1)
            rim_ref[k, x] = rim
            if k < 7:
                sums = [a if b is None else a + b for a, b in zip((cells, rim), sums)]
        phase_ref[2 * x] = sums[0]
        phase_ref[2 * x + 1] = sums[1]
        return carry

    lax.fori_loop(0, 4, row, 0)

    def cells_of(k, row):
        return (main_ref[k, row], rim_ref[k, row])

    messages = []
    for edge, inner, crossing, out in ((3, 2, TO_RIGHT, 1), (0, 1, TO_LEFT, 2)):
        pops = [cells_of(7 + q, edge) for q in range(19)]
        g = [cells_of(q, edge) for q in range(7)]
        fluid = both(lambda a: a > 0.5, cells_of(FLUID, edge))
        phi = load_pair(phase_ref, edge)
        pressure = both(lambda *p: total(p), *pops)
        omega = both(lambda p: 1.0 / (0.6 + 0.3 * jnp.clip(p, 0.0, 1.0)), phi)
        fields = [
            both(
                lambda a, b, f, o, p: jnp.where(f, (1.0 - o) * a + W[q] * (o * p), b),
                pops[q], pops[BACK[q]], fluid, omega, pressure,
            )
            for q in crossing
        ]
        turn = lambda a, b, f: jnp.where(f, -0.25 * a, b)
        fields.append(both(turn, g[out], g[BACK[out]], fluid))
        parts = [both(turn, g[0], g[0], fluid)]
        for q in range(3, 7):
            parts.append(moved(both(turn, g[q], g[BACK[q]], fluid), -DIRS[q][1], -DIRS[q][2]))
        grads = gradients(*(load_pair(phase_ref, inner + d) for d in (-1, 0, 1)))
        inner_phi = load_pair(phase_ref, inner)
        inner_pops = [cells_of(7 + q, inner) for q in range(19)]
        crossing_phase = []
        for t in range(2):
            mom = [momentum_of([p[t] for p in inner_pops], 0)] + [jnp.zeros((16, 128), F32)] * 2
            s = state_of(inner_phi[t], mom, tuple(gr[t] for gr in grads[:3]), grads[3][t])
            equil = 0.15625 * inner_phi[t] + (0.625 if out == 1 else -0.625) * carried_of(s, 0)
            crossing_phase.append(
                jnp.where(
                    cells_of(FLUID, inner)[t] > 0.5,
                    equil - 0.25 * cells_of(out, inner)[t],
                    cells_of(BACK[out], inner)[t],
                )
            )
        parts.append(tuple(crossing_phase))
        fields.append(both(lambda *p: total(p), *parts))
        fields.append(phi)
        for axis in range(3):
            fields.append(both(lambda *p: momentum_of(p, axis), *pops))
        fields.append(cells_of(FLUID, edge))
        fields.append(inner_phi)
        messages.append(fields)
    pack(odd_ref, even_ref, *messages, wide=WIDE_FIRST)


SHIFTS = sorted({c[1:] for c in DIRS})
BF16 = jnp.bfloat16


def probe_kernel(probes_ref, weights_ref, out_ref, acc_ref, code_ref):
    first_x = lax.axis_index("tile") * 4
    first_z = lax.axis_index("vert") * 128
    acc_ref[...] = jnp.zeros_like(acc_ref)
    count = jnp.zeros((8, 128), jnp.int32)
    groups = probes_ref.shape[1] // 8
    for i in range(groups):
        at = slice(8 * i, 8 * i + 8)
        x = probes_ref[0, at, :] - (first_x - 1)
        y = probes_ref[1, at, :]
        z = probes_ref[2, at, :] - first_z
        here = (x >= 0) & (x < 6) & (z >= -RIM) & (z < 128 + RIM)
        ring = jnp.where(z >= 0, z, z + 144)
        code_ref[at, :] = jnp.where(here, (x * 16 + y) * 256 + ring, -1)
        count = count + here.astype(jnp.int32)
    passes = jnp.max(count)
    across = lax.broadcasted_iota(jnp.int32, (96, 128), 0).astype(F32).astype(BF16)
    height = lax.broadcasted_iota(jnp.int32, (144, 128), 0).astype(F32).astype(BF16)
    zero = jnp.zeros((), BF16)
    one = jnp.ones((), BF16)

    def one_pass(i, carry):
        code = jnp.full((8, 128), -1, jnp.int32)
        weight = jnp.zeros((8, 128), F32)
        for i in range(groups):
            at = slice(8 * i, 8 * i + 8)
            here = code_ref[at, :]
            take = (here >= 0) & (code < 0)
            code = jnp.where(take, here, code)
            weight = jnp.where(take, weights_ref[at, :], weight)
            code_ref[at, :] = jnp.where(take, -1, here)
        code_xy = (code >> 8).astype(F32)
        code_z = (code & 255).astype(F32)
        high = weight.astype(BF16).astype(F32)
        low = weight - high
        lhs, rhs = [], []
        for n in range(8):
            line = lambda v: v[n : n + 1, :].astype(BF16)
            hit = across == line(code_xy)
            lhs.append(
                jnp.concatenate([jnp.where(hit, line(high), zero), jnp.where(hit, line(low), zero)], axis=0)
            )
            rhs.append(jnp.where(height == line(code_z), one, zero))
        acc_ref[...] += lax.dot_general(
            jnp.concatenate(lhs, axis=1), jnp.concatenate(rhs, axis=1), (((1,), (1,)), ((), ())),
            preferred_element_type=F32,
        )
        return carry

    lax.fori_loop(0, passes, one_pass, 0)
    lane = lanes()
    for x in range(6):
        rows = pl.ds(16 * x, 16)
        lows = pl.ds(96 + 16 * x, 16)
        main = acc_ref[rows, 0:128] + acc_ref[lows, 0:128]
        rim = acc_ref[rows, 128:144] + acc_ref[lows, 128:144]
        rim = jnp.concatenate([rim, jnp.zeros((16, 112), F32)], axis=1)
        rim = jnp.where(lane < RIM, rim, jnp.where(lane >= 120, roll(rim, 112, 1), 0.0))
        for n, (cy, cz) in enumerate(SHIFTS):
            store_pair(out_ref, moved((main, rim), cy, cz), n, x)


N_FIRST = 13
WIDE_FIRST = (7,)
N_SECOND = 8
HALVES = (slice(0, 8), slice(8, 16))
M2_KEYS = ((0, 0), (0, 1), (0, 2), (1, 1), (1, 2), (2, 2))


def spot(refs, row):
    if row in (1, 2):
        return refs[0], row - 1
    return refs[1], {-1: 0, 0: 1, 3: 2, 4: 3}[row]


def prim_at(prims, row, t, h):
    ref, at = spot(prims, row)
    vals = [ref[k, 2 * at + t, h, :] for k in range(10)]
    return state_of(vals[0], vals[6:9], tuple(vals[1:4]), vals[4]), vals[5], vals[9] > 0.5


def put_gradients(prims, phase_pairs, row):
    ref, at = spot(prims, row)
    grads = gradients(*phase_pairs)
    store_pair(ref, phase_pairs[1], 0, at)
    for i in range(4):
        store_pair(ref, grads[i], 1 + i, at)


def forward(cells_ref, prims, posts, row, t):
    prim_ref, at = spot(prims, row)
    post_ref, _ = spot(posts, row)
    i = 2 * at + t
    for h in HALVES:
        g = [cells_ref[q, row, h, :] for q in range(7)]
        f = [cells_ref[7 + q, row, h, :] for q in range(19)]
        prim_ref[5, i, h, :] = total(f)
        for axis in range(3):
            prim_ref[6 + axis, i, h, :] = momentum_of(f, axis)
        prim_ref[9, i, h, :] = cells_ref[FLUID, row, h, :]
        s, pressure, fluid = prim_at(prims, row, t, h)
        for q, v in post_flow(f, fluid, pressure, s, range(19)).items():
            post_ref[7 + q, i, h, :] = v
        for q, v in post_phase(g, fluid, s, range(7)).items():
            post_ref[q, i, h, :] = v


def stream(posts, row):
    ref, at = spot(posts, row)
    for q in range(19):
        _, cy, cz = DIRS[q]
        if (cy or cz) and 0 <= row + DIRS[q][0] < 4:
            store_pair(ref, moved(load_pair(ref, 7 + q, at), -cy, -cz), 7 + q, at)


def inner_kernel(main_ref, rim_ref, phase_ref, seeds_ref, prim_ref, post_ref, moments_ref):
    prims, posts = (prim_ref, None), (post_ref, None)
    for row in (1, 2):
        put_gradients(prims, [load_pair(phase_ref, row + d) for d in (-1, 0, 1)], row)
        for t, cells_ref in enumerate((main_ref, rim_ref)):
            forward(cells_ref, prims, posts, row, t)
        stream(posts, row)

    def moments(i, carry):
        for h in HALVES:
            adj = {q: seeds_ref[SHIFTS.index(DIRS[q][1:]), i + 2 + 2 * DIRS[q][0], h, :] for q in range(19)}
            m0, m1, m2 = moments_of(adj)
            for k, v in enumerate([m0] + m1 + [m2[key] for key in M2_KEYS]):
                moments_ref[k, i, h, :] = v
        return carry

    lax.fori_loop(0, 8, moments, 0)


def middle_kernel(
    main_ref, rim_ref, phase_ref, odd_in_ref, even_in_ref, seeds_ref, moments_ref, prim_in_ref, post_in_ref,
    prim_ref, adj_ref, gamma_ref, edges_ref, odd_ref, even_ref,
    post_ref, phase_mid_ref, grad_mid_ref, back_ref, dphi_ref,
):
    prims, posts = (prim_in_ref, prim_ref), (post_in_ref, post_ref)
    from_left, from_right = received(odd_in_ref, even_in_ref, N_FIRST, WIDE_FIRST)
    sides = ((from_left, -1, TO_RIGHT, 1), (from_right, 4, TO_LEFT, 2))
    for got, row, crossing, out in sides:
        _, at = spot(prims, row)
        for i in range(3):
            store_pair(prim_ref, got[8 + i], 6 + i, at)
        store_pair(prim_ref, got[11], 9, at)
        for q, pair in zip(crossing, got[:5]):
            store_pair(post_ref, pair, 7 + q, at)
        store_pair(post_ref, got[5], out, at)
    phases = [from_left[12], from_left[7]] + [load_pair(phase_ref, r) for r in range(4)]
    phases += [from_right[7], from_right[12]]
    for row in (-1, 0, 3, 4):
        put_gradients(prims, phases[row + 1 : row + 4], row)
    for row in (0, 3):
        for t, cells_ref in enumerate((main_ref, rim_ref)):
            forward(cells_ref, prims, posts, row, t)
        stream(posts, row)

    mid_parts = {}
    for got, row, crossing, out in sides:
        _, at = spot(posts, row)
        spread = [[], [], []]
        for t in range(2):
            i = 2 * at + t
            halves = [[], [], []]
            for h in HALVES:
                vals = [prim_ref[k, i, h, :] for k in range(10) if k != 5]
                s = state_of(vals[0], vals[5:8], tuple(vals[1:4]), vals[4])
                fluid = vals[8] > 0.5
                vel, force, omega, kappa = s["vel"], s["force"], s["omega"], s["kappa"]
                base = -1.5 * omega * dot(vel, vel) - 3.0 * kappa * dot(vel, force)
                odd_vec = tuple(3.0 * (omega * v + kappa * f) for v, f in zip(vel, force))
                even_vec = tuple(4.5 * omega * v + 9.0 * kappa * f for v, f in zip(vel, force))
                for q in crossing:
                    step = DIRS[q]
                    gain = base + along(step, vel) * along(step, even_vec) + along(step, odd_vec)
                    kept = post_ref[7 + q, i, h, :]
                    post_ref[7 + q, i, h, :] = jnp.where(fluid, kept + W[q] * gain, kept)
                sharp, _ = sharpening(s)
                carried = tuple(s["phi"] * v + sharp * gr for v, gr in zip(vel, s["grad"]))
                kept = post_ref[out, i, h, :]
                gain = 0.15625 * s["phi"] + 0.625 * along(DIRS[out], carried)
                post_ref[out, i, h, :] = jnp.where(fluid, kept + gain, kept)
                halves[0].append(jnp.where(fluid, s["phi"], 0.0))
                halves[1].append(jnp.where(fluid, carried[1], 0.0))
                halves[2].append(jnp.where(fluid, carried[2], 0.0))
            for n in range(3):
                spread[n].append(jnp.concatenate(halves[n], axis=0))
        stream(posts, row)
        phi, cy, cz = (tuple(x) for x in spread)
        gain_y = lambda sign: both(lambda p, c: 0.15625 * p + sign * 0.625 * c, phi, cy)
        gain_z = lambda sign: both(lambda p, c: 0.15625 * p + sign * 0.625 * c, phi, cz)
        mid_parts[row] = [
            got[6], both(lambda p: 0.3125 * p, phi),
            moved(gain_y(1.0), -1, 0), moved(gain_y(-1.0), 1, 0),
            moved(gain_z(1.0), 0, -1), moved(gain_z(-1.0), 0, 1),
        ]
    def post_pair(q, row):
        ref, at = spot(posts, row)
        return load_pair(ref, q, at)

    for row in range(-1, 5):
        parts = mid_parts.get(row)
        if parts is None:
            parts = [post_pair(0, row)]
            for q in range(3, 7):
                parts.append(moved(post_pair(q, row), -DIRS[q][1], -DIRS[q][2]))
        if row > -1:
            parts.append(post_pair(1, row - 1))
        if row < 4:
            parts.append(post_pair(2, row + 1))
        store_pair(phase_mid_ref, both(lambda *p: total(p), *parts), row + 1)
    for row in range(4):
        grads = gradients(*(load_pair(phase_mid_ref, row + d) for d in (0, 1, 2)))
        for i in range(4):
            store_pair(grad_mid_ref, grads[i], i, row)
    def backward(row, t, h):
        i = 2 * row + t
        f = []
        for q in range(19):
            ref, at = spot(posts, row - DIRS[q][0])
            f.append(ref[7 + q, 2 * at + t, h, :])
        adj = {q: seeds_ref[SHIFTS.index(DIRS[q][1:]), i + 2 + 2 * DIRS[q][0], h, :] for q in range(19)}
        ref, at = spot(prims, row)
        fluid = ref[9, 2 * at + t, h, :] > 0.5
        phi = phase_mid_ref[i + 2, h, :]
        mom = [momentum_of(f, axis) for axis in range(3)]
        s = state_of(phi, mom, tuple(grad_mid_ref[k, i, h, :] for k in range(3)), grad_mid_ref[3, i, h, :])
        kept = total([adj[q] * f[q] for q in range(19)])
        m = [moments_ref[k, i, h, :] for k in range(10)]
        m2 = {}
        for key, value in zip(M2_KEYS, m[4:]):
            m2[key] = m2[key[::-1]] = value
        d_flow, d_phi, d_grad, d_lap = pull_all(s, total(f), adj, kept, m[0], m[1:4], m2, None, None)
        for q in range(19):
            adj_ref[q, i, h, :] = jnp.where(fluid, d_flow[q], adj[BACK[q]])
        dphi_ref[i, h, :] = jnp.where(fluid, d_phi, 0.0)
        for k in range(3):
            back_ref[k, i, h, :] = jnp.where(fluid, d_grad[k], 0.0)
        back_ref[3, i, h, :] = jnp.where(fluid, d_lap, 0.0)

    for row in range(4):
        for t in range(2):
            for h in HALVES:
                backward(row, t, h)

    for q in range(19):
        _, cy, cz = DIRS[q]
        if cy or cz:
            for row in range(4):
                store_pair(adj_ref, moved(load_pair(adj_ref, q, row), cy, cz), q, row)

    for row in range(4):
        store_pair(gamma_ref, stencil_back(back_ref, dphi_ref, row), row)
    edge_parts = []
    for row, part in ((0, ahead_part), (3, behind_part)):
        pair = both(part, load_pair(back_ref, 0, row), load_pair(back_ref, 3, row))
        store_pair(edges_ref, pair, 0 if row == 0 else 1)
        edge_parts.append(pair)

    messages = []
    for row, out_dirs, part, sign, edge_pair in (
        (3, TO_RIGHT, behind_part, -1.0, edge_parts[1]),
        (0, TO_LEFT, ahead_part, 1.0, edge_parts[0]),
    ):
        gamma = load_pair(gamma_ref, row)
        next_gamma = load_pair(gamma_ref, row - 1 if row == 3 else row + 1)
        n1 = turn_gamma(both(lambda a: sign * a, next_gamma), gamma)
        partial = []
        for t in range(2):
            s, _, fluid = prim_at(prims, row, t, slice(None))
            adj = {
                q: adj_ref[q, 2 * (row + DIRS[q][0]) + t] for q in range(19) if q not in out_dirs
            }
            m0, m1, m2 = moments_of(adj)
            d_grad, d_lap = pull_stencil(s, m0, m1, m2, [n[t] for n in n1])[:2]
            partial.append(jnp.where(fluid, part(d_grad[0], d_lap), 0.0))
        back_dirs = TO_LEFT if row == 3 else TO_RIGHT
        fields = [load_pair(adj_ref, q, row) for q in back_dirs]
        fields += [gamma, edge_pair, tuple(partial)]
        messages.append(fields)
    pack(odd_ref, even_ref, *messages)


def turn_gamma(along_x, centre):
    diff = lambda a, b: 0.125 * (a - b)
    return (
        both(lambda a: 0.125 * a, along_x),
        both(diff, moved(centre, 1, 0), moved(centre, -1, 0)),
        both(diff, moved(centre, 0, 1), moved(centre, 0, -1)),
    )


def stencil_back(back_ref, start_ref, row, first=None, last=None):
    gy, gz, lap = (load_pair(back_ref, k, row) for k in (1, 2, 3))
    fold = lambda l, gyb, gya, lyb, lya, gzb, gza, lzb, lza: (
        0.5 * (gyb - gya) + lyb + lya + 0.5 * (gzb - gza) + lzb + lza - 6.0 * l
    )
    out = both(
        fold, lap,
        moved(gy, -1, 0), moved(gy, 1, 0), moved(lap, -1, 0), moved(lap, 1, 0),
        moved(gz, 0, -1), moved(gz, 0, 1), moved(lap, 0, -1), moved(lap, 0, 1),
    )
    add = lambda a, b: a + b
    if start_ref is not None:
        out = both(add, out, load_pair(start_ref, row))
    if row > 0:
        out = both(add, out, both(behind_part, load_pair(back_ref, 0, row - 1), load_pair(back_ref, 3, row - 1)))
    elif first is not None:
        out = both(add, out, first)
    if row < 3:
        out = both(add, out, both(ahead_part, load_pair(back_ref, 0, row + 1), load_pair(back_ref, 3, row + 1)))
    elif last is not None:
        out = both(add, out, last)
    return out


def ahead_kernel(
    main_ref, prim_in_ref, prim_out_ref, adj_ref, gamma_ref,
    flow_ref, back_ref, dphi_ref,
    turned_ref,
):
    prims = (prim_in_ref, prim_out_ref)
    for row in (1, 2):
        centre = load_pair(gamma_ref, row)
        for n, (cy, cz) in enumerate(((1, 0), (-1, 0), (0, 1), (0, -1))):
            store_pair(turned_ref, moved(centre, cy, cz), n, row - 1)
    for row in range(4):
        for t in range(2):
            for h in HALVES:
                i = 2 * row + t
                s, pressure, fluid = prim_at(prims, row, t, h)
                adj = {
                    q: adj_ref[q, i + 2 * DIRS[q][0], h, :] for q in range(19) if 0 <= row + DIRS[q][0] < 4
                }
                m0, m1, m2 = moments_of(adj)
                n0 = n1 = None
                if row in (1, 2):
                    g = [gamma_ref[i + 2, h, :], gamma_ref[i - 2, h, :]]
                    g += [turned_ref[n, i - 2, h, :] for n in range(4)]
                    n1 = [0.125 * (g[a] - g[a + 1]) for a in (0, 2, 4)]
                if t == 1:
                    d_grad, d_lap = pull_stencil(s, m0, m1, m2, n1)[:2]
                else:
                    if row in (1, 2):
                        n0 = 0.25 * gamma_ref[i, h, :] + 0.125 * total(g)
                    kept = total([a * main_ref[7 + q, row, h, :] for q, a in adj.items()])
                    d_flow, d_phi, d_grad, d_lap = pull_all(s, pressure, adj, kept, m0, m1, m2, n0, n1)
                    for q in range(19):
                        flow_ref[q, row, h, :] = jnp.where(fluid, d_flow[q], adj.get(BACK[q], 0.0))
                    dphi_ref[row, h, :] = jnp.where(fluid, d_phi, 0.0)
                for k in range(3):
                    back_ref[k, i, h, :] = jnp.where(fluid, d_grad[k], 0.0)
                back_ref[3, i, h, :] = jnp.where(fluid, d_lap, 0.0)


def last_kernel(
    main_ref, prim_in_ref, prim_out_ref, adj_ref, gamma_ref, edges_ref, flow_ref, back_in_ref, dphi_in_ref,
    odd_in_ref, even_in_ref,
    out_g_ref, out_f_ref,
    gamma_wide_ref, turned_ref, back_ref, dphi_ref, g_ref, f_ref, sems,
):
    add = lambda a, b: a + b
    prims = (prim_in_ref, prim_out_ref)
    copies = []

    def send(src, dst):
        copies.append(pltpu.make_async_copy(src, dst, sems.at[len(copies)]))
        copies[-1].start()

    got_left, got_right = received(odd_in_ref, even_in_ref, N_SECOND)
    own_first = load_pair(edges_ref, 0)
    own_last = load_pair(edges_ref, 1)

    for row, more, sign in ((1, got_left[6], -0.125), (2, got_right[6], 0.125)):
        for t in range(2):
            for n, h in enumerate(HALVES):
                i = 2 * row + t
                s, _, fluid = prim_at(prims, row, t, h)
                delta = more[t][8 * n : 8 * n + 8]
                d_vel, d_phi, d_grad, d_lap = pull_along_x(s, 0.125 * delta, sign * delta)
                if t == 0:
                    lift = jnp.where(fluid, d_vel, 0.0)
                    for q in range(19):
                        base = flow_ref[q, row, h, :]
                        f_ref[q, row, h, :] = base + DIRS[q][0] * lift if DIRS[q][0] else base
                    dphi_ref[row, h, :] = dphi_in_ref[row, h, :] + jnp.where(fluid, d_phi, 0.0)
                for k in range(3):
                    back_ref[k, i, h, :] = back_in_ref[k, i, h, :] + jnp.where(fluid, d_grad[k], 0.0)
                back_ref[3, i, h, :] = back_in_ref[3, i, h, :] + jnp.where(fluid, d_lap, 0.0)
    send(f_ref.at[:, pl.ds(1, 2)], out_f_ref.at[:, pl.ds(1, 2)])

    for row in (1, 2):
        store_pair(gamma_wide_ref, load_pair(gamma_ref, row), row + 1)
    store_pair(gamma_wide_ref, both(add, load_pair(gamma_ref, 0), got_left[6]), 1)
    store_pair(gamma_wide_ref, both(add, load_pair(gamma_ref, 3), got_right[6]), 4)
    store_pair(gamma_wide_ref, both(add, got_left[5], own_first), 0)
    store_pair(gamma_wide_ref, both(add, got_right[5], own_last), 5)
    for row in range(4):
        centre = load_pair(gamma_wide_ref, row + 1)
        for n, (cy, cz) in enumerate(((1, 0), (-1, 0), (0, 1), (0, -1))):
            store_pair(turned_ref, moved(centre, cy, cz), n, row)

    def phase_adjoints(i, h):
        at = [gamma_wide_ref[i + 2, h, :], gamma_wide_ref[i + 4, h, :], gamma_wide_ref[i, h, :]]
        return at + [turned_ref[n, i, h, :] for n in range(4)]

    for row, got, dirs in ((0, got_left, TO_LEFT), (3, got_right, TO_RIGHT)):
        for t in range(2):
            for n, h in enumerate(HALVES):
                i = 2 * row + t
                s, pressure, fluid = prim_at(prims, row, t, h)
                adj = {q: pair[t][8 * n : 8 * n + 8] for q, pair in zip(dirs, got[:5])}
                g = phase_adjoints(i, h)
                n1 = [0.125 * (g[a] - g[a + 1]) for a in (1, 3, 5)]
                m0, m1, m2 = moments_of(adj)
                if t == 1:
                    d_grad, d_lap = pull_stencil(s, m0, m1, m2, n1)[:2]
                else:
                    n0 = 0.25 * g[0] + 0.125 * total(g[1:])
                    kept = total([a * main_ref[7 + q, row, h, :] for q, a in adj.items()])
                    d_flow, d_phi, d_grad, d_lap = pull_all(s, pressure, adj, kept, m0, m1, m2, n0, n1)
                    for q in range(19):
                        more = jnp.where(fluid, d_flow[q], adj.get(BACK[q], 0.0))
                        f_ref[q, row, h, :] = flow_ref[q, row, h, :] + more
                    dphi_ref[row, h, :] = dphi_in_ref[row, h, :] + jnp.where(fluid, d_phi, 0.0)
                for k in range(3):
                    back_ref[k, i, h, :] = back_in_ref[k, i, h, :] + jnp.where(fluid, d_grad[k], 0.0)
                back_ref[3, i, h, :] = back_in_ref[3, i, h, :] + jnp.where(fluid, d_lap, 0.0)
        send(f_ref.at[:, pl.ds(row, 1)], out_f_ref.at[:, pl.ds(row, 1)])

    edge_parts = []
    for got, prim_row, row, own, out_dirs, part, sign in (
        (got_left, -1, 0, own_first, TO_RIGHT, behind_part, 1.0),
        (got_right, 4, 3, own_last, TO_LEFT, ahead_part, -1.0),
    ):
        gamma = load_pair(gamma_wide_ref, row + 1)
        n1 = turn_gamma(both(lambda a: sign * a, gamma), own)
        pair = []
        for t in range(2):
            s, _, fluid = prim_at(prims, prim_row, t, slice(None))
            adj = {q: adj_ref[q, 2 * row + t] for q in out_dirs}
            m0, m1, m2 = moments_of(adj)
            d_grad, d_lap = pull_stencil(s, m0, m1, m2, [n[t] for n in n1])[:2]
            pair.append(got[7][t] + jnp.where(fluid, part(d_grad[0], d_lap), 0.0))
        edge_parts.append(tuple(pair))

    for row in range(4):
        rest = stencil_back(back_ref, None, row, edge_parts[0], edge_parts[1])[0]
        ref, at = spot(prims, row)
        fluid = ref[9, 2 * at] > 0.5
        base = rest + dphi_ref[row]
        phase_adj = phase_adjoints(2 * row, slice(None))
        for q in range(7):
            g_ref[q, row] = jnp.where(fluid, base - 0.25 * phase_adj[q], rest + phase_adj[BACK[q]])
    send(g_ref, out_g_ref)
    for copy in copies:
        copy.wait()


def call(kernel, outs, n_in, scratch=(), flops=0, name=None, any_in=0, any_out=False):
    vmem = pl.BlockSpec(memory_space=pltpu.VMEM)
    return pl.pallas_call(
        kernel,
        out_shape=[jax.ShapeDtypeStruct(x, F32) if isinstance(x, tuple) else x for x in outs],
        in_specs=[pl.BlockSpec(memory_space=pl.ANY)] * any_in + [vmem] * (n_in - any_in),
        out_specs=[pl.BlockSpec(memory_space=pl.ANY) if any_out else vmem] * len(outs),
        scratch_shapes=[pltpu.VMEM(x, F32) if isinstance(x, tuple) else x for x in scratch],
        compiler_params=pltpu.CompilerParams(vmem_limit_bytes=VMEM_LIMIT),
        cost_estimate=pl.CostEstimate(flops=flops, bytes_accessed=flops // 8, transcendentals=0),
        name=name,
    )


def swap(x, axis, first):
    pairs = []
    for i in range(first, lax.axis_size(axis) - 1, 2):
        pairs += [(i, i + 1), (i + 1, i)]
    return lax.ppermute(x, axis, pairs)


def pair_gather(x, axis, first):
    size = lax.axis_size(axis)
    groups = [[i, (i + 1) % size] for i in range(first, size, 2)]
    return lax.all_gather(x, axis, axis_index_groups=groups)


def shards(phase_init, flow_init, solid_mask, sensor_cells, sensor_weights):
    tile = (16, 128)
    cells = sensor_cells.reshape(3, -1, 128).transpose(1, 0, 2)
    weights = sensor_weights.reshape(-1, 128)
    main, probes, weights, odd, even = call(
        rim_kernel,
        [(27, 4) + tile, jax.ShapeDtypeStruct((3,) + weights.shape, jnp.int32), weights.shape] + [(2, 4) + tile] * 2,
        5, any_in=5, flops=10**6, name="rim",
        scratch=[pltpu.VMEM((4,) + tile, jnp.int32), pltpu.SemaphoreType.DMA((10,))],
    )(*(pltpu.with_memory_space_constraint(x, pltpu.HBM) for x in (phase_init, flow_init, solid_mask, cells, weights)))
    odd, even = swap(odd, "vert", 1), swap(even, "vert", 0)
    (seeds,) = call(probe_kernel, [(9, 12) + tile], 2, scratch=[(192, 144), pltpu.VMEM(weights.shape, jnp.int32)], flops=2 * 10**9, name="probes")(
        probes, weights
    )
    first = message_tiles(N_FIRST, WIDE_FIRST)
    rim, phase, odd, even = call(
        ring_kernel, [(27, 4) + tile, (8,) + tile] + [(first,) + tile] * 2, 4, any_in=1, flops=10**7, name="ring"
    )(seeds, main, odd, even)
    odd, even = pair_gather(odd, "tile", 1), pair_gather(even, "tile", 0)
    prim_in, post_in, moments = call(
        inner_kernel, [(10, 4) + tile, (26, 4) + tile, (10, 8) + tile], 4, flops=2 * 10**8, name="inner"
    )(main, rim, phase, seeds)
    second = message_tiles(N_SECOND)
    prim_out, adj, gamma, edges, odd, even = call(
        middle_kernel,
        [(10, 8) + tile, (19, 8) + tile, (8,) + tile, (4,) + tile] + [(second,) + tile] * 2,
        9,
        scratch=[(26, 8) + tile, (12,) + tile, (4, 8) + tile, (4, 8) + tile, (8,) + tile],
        flops=10**8, name="middle",
    )(main, rim, phase, odd, even, seeds, moments, prim_in, post_in)
    odd, even = pair_gather(odd, "tile", 1), pair_gather(even, "tile", 0)
    flow, back, dphi = call(
        ahead_kernel, [(19, 4) + tile, (4, 8) + tile, (4,) + tile], 5, scratch=[(4, 4) + tile], flops=2 * 10**8,
        name="ahead",
    )(main, prim_in, prim_out, adj, gamma)
    return tuple(
        call(
            last_kernel,
            [(7, 4) + tile, (19, 4) + tile],
            11,
            scratch=[
                (12,) + tile, (4, 8) + tile, (4, 8) + tile, (4,) + tile, (7, 4) + tile, (19, 4) + tile,
                pltpu.SemaphoreType.DMA((4,)),
            ],
            flops=10**8, name="last", any_out=True,
        )(main, prim_in, prim_out, adj, gamma, edges, flow, back, dphi, odd, even)
    )


def solution(mesh):
    return jax.shard_map(
        shards,
        mesh=mesh,
        in_specs=(
            P(None, "tile", None, "vert"),
            P(None, "tile", None, "vert"),
            P("tile", None, "vert"),
            P(),
            P(),
        ),
        out_specs=(P(None, "tile", None, "vert"), P(None, "tile", None, "vert")),
        check_vma=False,
    )
```

```python
import functools

import jax
import jax.numpy as jnp
import numpy as np
from jax import lax
from jax.experimental import pallas as pl
from jax.experimental.pallas import tpu as pltpu
from jax.sharding import PartitionSpec as P

DIRS = [
    (0, 0, 0), (1, 0, 0), (-1, 0, 0), (0, 1, 0), (0, -1, 0), (0, 0, 1), (0, 0, -1),
    (1, 1, 0), (-1, -1, 0), (1, -1, 0), (-1, 1, 0), (1, 0, 1), (-1, 0, -1), (1, 0, -1),
    (-1, 0, 1), (0, 1, 1), (0, -1, -1), (0, 1, -1), (0, -1, 1),
]
BACK = [0, 2, 1, 4, 3, 6, 5, 8, 7, 10, 9, 12, 11, 14, 13, 16, 15, 18, 17]
W = [1.0 / 3.0] + [1.0 / 18.0] * 6 + [1.0 / 36.0] * 12
W0, W1, W2 = 1.0 / 3.0, 1.0 / 18.0, 1.0 / 36.0
PAIRS = [(q, q + 1) for q in range(1, 19, 2)]
TO_RIGHT = [q for q in range(19) if DIRS[q][0] == 1]
TO_LEFT = [q for q in range(19) if DIRS[q][0] == -1]
RIM = 8
SHARP = 0.075
FLUID = 26
F32 = jnp.float32
VMEM_LIMIT = 40 * 2**20


def lanes():
    return lax.broadcasted_iota(jnp.int32, (16, 128), 1)


def roll(x, shift, axis):
    shift = shift % x.shape[axis]
    return x if shift == 0 else pltpu.roll(x, shift, axis)


def load_pair(ref, *at):
    *head, row = at
    return (ref[(*head, 2 * row)], ref[(*head, 2 * row + 1)])


def store_pair(ref, pair, *at):
    *head, row = at
    ref[(*head, 2 * row)] = pair[0]
    ref[(*head, 2 * row + 1)] = pair[1]


def both(fn, *pairs):
    return tuple(fn(*each) for each in zip(*pairs))


def moved(pair, step_y, step_z):
    if step_y:
        pair = both(lambda t: roll(t, -step_y, 0), pair)
    if step_z:
        a = roll(pair[0], -step_z, 1)
        b = roll(pair[1], -step_z, 1)
        edge = lanes() == (127 if step_z > 0 else 0)
        pair = (jnp.where(edge, b, a), jnp.where(edge, a, b))
    return pair


def is_odd(axis):
    return jnp.full((16, 128), lax.rem(lax.axis_index(axis), 2), jnp.int32) == 1


def rim_slots(count, wide):
    slots, at = [], 0
    for k in range(count):
        width = 8 if k in wide else 4
        if at % 128 + 2 * width > 128:
            at += 128 - at % 128
        slots.append((at // 128, at % 128, width))
        at += 2 * width
    return slots


def message_tiles(count, wide=()):
    return count + rim_slots(count, wide)[-1][0] + 1


def packed(fields, wide):
    lane = lanes()
    out = [main for main, _ in fields]
    slots = rim_slots(len(fields), wide)
    for tile in range(slots[-1][0] + 1):
        acc = jnp.zeros((16, 128), F32)
        for (at, first, width), (_, rim) in zip(slots, fields):
            if at == tile:
                mine = (lane >= first) & (lane < first + 2 * width)
                acc = jnp.where(mine, roll(rim, first + width, 1), acc)
        out.append(acc)
    return out


def pack(odd_ref, even_ref, right, left, wide=()):
    odd = is_odd("tile")
    for n, (r, l) in enumerate(zip(packed(right, wide), packed(left, wide))):
        odd_ref[n] = jnp.where(odd, r, l)
        even_ref[n] = jnp.where(odd, l, r)


def received(odd_ref, even_ref, count, wide=()):
    odd = is_odd("tile")
    slots = rim_slots(count, wide)
    tiles = message_tiles(count, wide)
    got_odd = [odd_ref[n] for n in range(tiles)]
    got_even = [even_ref[n] for n in range(tiles)]
    sides = []
    for one, two in ((got_even, got_odd), (got_odd, got_even)):
        msg = [jnp.where(odd, a, b) for a, b in zip(one, two)]
        sides.append(
            [(msg[k], roll(msg[count + at], -(first + width), 1)) for k, (at, first, width) in enumerate(slots)]
        )
    return sides


def total(values):
    out = values[0]
    for value in values[1:]:
        out = out + value
    return out


def along(step, vec):
    out = None
    for c, v in zip(step, vec):
        if c == 0:
            continue
        if out is None:
            out = v if c > 0 else -v
        else:
            out = out + v if c > 0 else out - v
    return out


def momentum_of(pops, axis):
    plus = [pops[q] for q in range(19) if DIRS[q][axis] == 1]
    minus = [pops[q] for q in range(19) if DIRS[q][axis] == -1]
    return total([a - b for a, b in zip(plus, minus)])


def state_of(phi, mom, grad, lap):
    clipped = jnp.clip(phi, 0.0, 1.0)
    rho = 0.05 + 0.95 * clipped
    omega = 1.0 / (0.6 + 0.3 * clipped)
    inv_rho = 1.0 / rho
    potential = 1.2 * phi * (phi - 1.0) * (phi - 0.5) - 0.6 * lap
    force = (
        potential * grad[0] - 0.01 * rho,
        potential * grad[1],
        potential * grad[2] - 0.02 * (rho - 0.05),
    )
    half = 0.5 * inv_rho
    vel = tuple(m + f * half for m, f in zip(mom, force))
    kappa = (1.0 - 0.5 * omega) * inv_rho
    return dict(
        phi=phi, grad=grad, omega=omega, inv_rho=inv_rho, potential=potential, force=force,
        half=half, vel=vel, kappa=kappa,
    )


def dot(a, b):
    return a[0] * b[0] + a[1] * b[1] + a[2] * b[2]


def sharpening(s):
    inv_len = lax.rsqrt(dot(s["grad"], s["grad"]) + 0.01)
    return SHARP * s["phi"] * (1.0 - s["phi"]) * inv_len, inv_len


def carried_of(s, axis):
    sharp, _ = sharpening(s)
    return s["phi"] * s["vel"][axis] + sharp * s["grad"][axis]


def post_flow(pops, fluid, pressure, s, wanted):
    vel, force, omega, kappa = s["vel"], s["force"], s["omega"], s["kappa"]
    base = omega * (pressure - 1.5 * dot(vel, vel)) - 3.0 * kappa * dot(vel, force)
    odd_vec = tuple(3.0 * (omega * v + kappa * f) for v, f in zip(vel, force))
    even_vec = tuple(4.5 * omega * v + 9.0 * kappa * f for v, f in zip(vel, force))
    keep = 1.0 - omega
    out = {}
    if 0 in wanted:
        out[0] = jnp.where(fluid, keep * pops[0] + W0 * base, pops[0])
    for q, r in PAIRS:
        if q not in wanted and r not in wanted:
            continue
        step = DIRS[q]
        even = base + along(step, vel) * along(step, even_vec)
        odd = along(step, odd_vec)
        if q in wanted:
            out[q] = jnp.where(fluid, keep * pops[q] + W[q] * (even + odd), pops[r])
        if r in wanted:
            out[r] = jnp.where(fluid, keep * pops[r] + W[q] * (even - odd), pops[q])
    return out


def post_phase(pops, fluid, s, wanted):
    sharp, _ = sharpening(s)
    carried = tuple(s["phi"] * v + sharp * g for v, g in zip(s["vel"], s["grad"]))
    out = {}
    for q in wanted:
        if q == 0:
            out[q] = jnp.where(fluid, 0.3125 * s["phi"] - 0.25 * pops[0], pops[0])
        else:
            equil = 0.15625 * s["phi"] + 0.625 * along(DIRS[q], carried)
            out[q] = jnp.where(fluid, equil - 0.25 * pops[q], pops[BACK[q]])
    return out


def moments_of(adj):
    zero = None
    m0, m1 = [], [[], [], []]
    m2 = {}
    if 0 in adj:
        m0.append(W0 * adj[0])
    groups = {W1: [], W2: []}
    for q in range(1, 19):
        if q not in adj:
            continue
        a = adj[q]
        w = W[q]
        groups[w].append(a)
    for w, items in groups.items():
        if items:
            m0.append(w * total(items))

    def weighted(terms):
        parts = []
        for w in (W1, W2):
            mine = [(sign, a) for ww, sign, a in terms if ww == w]
            if not mine:
                continue
            acc = None
            for sign, a in mine:
                if acc is None:
                    acc = a if sign > 0 else -a
                else:
                    acc = acc + a if sign > 0 else acc - a
            parts.append(w * acc)
        return total(parts) if parts else None

    for i in range(3):
        m1[i] = weighted([(W[q], DIRS[q][i], adj[q]) for q in range(1, 19) if q in adj and DIRS[q][i]])
    for i in range(3):
        for j in range(i, 3):
            m2[(i, j)] = weighted(
                [
                    (W[q], DIRS[q][i] * DIRS[q][j], adj[q])
                    for q in range(1, 19)
                    if q in adj and DIRS[q][i] and DIRS[q][j]
                ]
            )
            m2[(j, i)] = m2[(i, j)]
    return total(m0), m1, m2


def apply_m2(m2, vec):
    out = []
    for i in range(3):
        terms = [m2[(i, j)] * vec[j] for j in range(3) if m2[(i, j)] is not None]
        out.append(total(terms))
    return out


def pull_stencil(s, m0, m1, m2, n1):
    vel, force = s["vel"], s["force"]
    omega, kappa, half = s["omega"], s["kappa"], s["half"]
    m2v = apply_m2(m2, vel)
    m2f = apply_m2(m2, force)
    m0_3 = 3.0 * m0
    lean = []
    for i in range(3):
        term = 9.0 * m2v[i] - m0_3 * vel[i]
        lean.append(term if m1[i] is None else term + 3.0 * m1[i])
    push = [9.0 * m2f[i] - m0_3 * force[i] for i in range(3)]
    d_vel = [omega * a + kappa * b for a, b in zip(lean, push)]
    if n1 is not None:
        five_phi = 5.0 * s["phi"]
        d_vel = [d + five_phi * n for d, n in zip(d_vel, n1)]
    d_force = [kappa * a + half * d for a, d in zip(lean, d_vel)]
    d_potential = dot(d_force, s["grad"])
    d_grad = [s["potential"] * x for x in d_force]
    if n1 is not None:
        sharp, inv_len = sharpening(s)
        tilt = dot(s["grad"], n1) * inv_len * inv_len
        sharp5 = 5.0 * sharp
        d_grad = [d + sharp5 * (n - g * tilt) for d, n, g in zip(d_grad, n1, s["grad"])]
    d_lap = -0.6 * d_potential
    return d_grad, d_lap, d_potential, d_force, d_vel, m2v, m2f


def inside_clip(phi):
    return jnp.where((phi > 0.0) & (phi < 1.0), 1.0, jnp.where((phi == 0.0) | (phi == 1.0), 0.5, 0.0))


def pull_all(s, pressure, adj, kept, m0, m1, m2, n0, n1):
    d_grad, d_lap, d_potential, d_force, d_vel, m2v, m2f = pull_stencil(s, m0, m1, m2, n1)
    phi, vel, force = s["phi"], s["vel"], s["force"]
    omega, kappa, inv_rho, half = s["omega"], s["kappa"], s["inv_rho"], s["half"]
    relaxed = m0 * (pressure - 1.5 * dot(vel, vel)) + 3.0 * dot(m1, vel) + 4.5 * dot(m2v, vel)
    forced = 3.0 * dot(m1, force) - 3.0 * m0 * dot(vel, force) + 9.0 * dot(m2v, force)
    d_omega = relaxed - kept - 0.5 * inv_rho * forced
    d_rho = (
        -kappa * inv_rho * forced
        - 0.01 * d_force[0]
        - 0.02 * d_force[2]
        - dot(d_vel, force) * half * inv_rho
    )
    d_clip = 0.95 * d_rho - 0.3 * omega * omega * d_omega
    d_phi = d_potential * (1.2 * (3.0 * phi * (phi - 1.0) + 0.5)) + d_clip * inside_clip(phi)
    if n1 is not None:
        _, inv_len = sharpening(s)
        d_phi = d_phi + 1.25 * n0 + 5.0 * (
            dot(n1, vel) + SHARP * (1.0 - 2.0 * phi) * inv_len * dot(n1, s["grad"])
        )
    d_pressure = omega * m0
    keep = 1.0 - omega
    kept_part = lambda q, rest: keep * adj[q] + rest if q in adj else rest
    d_flow = {0: kept_part(0, d_pressure)}
    for q, r in PAIRS:
        lift = along(DIRS[q], d_vel)
        d_flow[q] = kept_part(q, d_pressure + lift)
        d_flow[r] = kept_part(r, d_pressure - lift)
    return d_flow, d_phi, d_grad, d_lap


def pull_along_x(s, n0, n):
    phi, grad = s["phi"], s["grad"]
    sharp, inv_len = sharpening(s)
    d_vel = 5.0 * phi * n
    d_force = s["half"] * d_vel
    d_potential = d_force * grad[0]
    sharp5 = 5.0 * sharp
    tilt = sharp5 * (grad[0] * n * inv_len * inv_len)
    d_grad = [s["potential"] * d_force + sharp5 * n - grad[0] * tilt, -grad[1] * tilt, -grad[2] * tilt]
    d_rho = -0.01 * d_force - d_force * s["force"][0] * s["inv_rho"]
    d_phi = (
        d_potential * (1.2 * (3.0 * phi * (phi - 1.0) + 0.5))
        + 0.95 * d_rho * inside_clip(phi)
        + 1.25 * n0
        + 5.0 * n * (s["vel"][0] + SHARP * (1.0 - 2.0 * phi) * inv_len * grad[0])
    )
    return d_vel, d_phi, d_grad, -0.6 * d_potential


def gradients(behind, centre, ahead):
    ahead_y, behind_y = moved(centre, 1, 0), moved(centre, -1, 0)
    ahead_z, behind_z = moved(centre, 0, 1), moved(centre, 0, -1)
    diff = lambda a, b: 0.5 * (a - b)
    lap = both(
        lambda a, b, c, d, e, f, m: a + b + c + d + e + f - 6.0 * m,
        ahead, behind, ahead_y, behind_y, ahead_z, behind_z, centre,
    )
    return both(diff, ahead, behind), both(diff, ahead_y, behind_y), both(diff, ahead_z, behind_z), lap


def behind_part(d_grad, d_lap):
    return 0.5 * d_grad + d_lap


def ahead_part(d_grad, d_lap):
    return d_lap - 0.5 * d_grad


def rim_kernel(
    g_ref, f_ref, solid_ref, cells_ref, weights_ref,
    main_ref, probes_ref, probe_weights_ref, odd_ref, even_ref, mask_ref, sems,
):
    parts = [(range(0, 7), pltpu.make_async_copy(g_ref, main_ref.at[pl.ds(0, 7)], sems.at[1]))]
    for n, (first, count) in enumerate(((0, 5), (5, 5), (10, 5), (15, 4))):
        copy = pltpu.make_async_copy(
            f_ref.at[pl.ds(first, count)], main_ref.at[pl.ds(7 + first, count)], sems.at[2 + n]
        )
        parts.append((range(7 + first, 7 + first + count), copy))
    parts.append((range(FLUID, FLUID + 1), pltpu.make_async_copy(solid_ref, mask_ref, sems.at[0])))
    later = [pltpu.make_async_copy(weights_ref, probe_weights_ref, sems.at[6])]
    for i in range(3):
        later.append(pltpu.make_async_copy(cells_ref.at[:, i, :], probes_ref.at[i], sems.at[7 + i]))
    for _, copy in parts:
        copy.start()
    for copy in later:
        copy.start()
    lane = lanes()
    odd = is_odd("vert")
    up = [[jnp.zeros((16, 128), F32)] * 4 for _ in range(2)]
    down = [[jnp.zeros((16, 128), F32)] * 4 for _ in range(2)]
    for fields, copy in parts:
        copy.wait()
        for k in fields:
            tile, slot = k // 16, k % 16
            for x in range(4):
                if k == FLUID:
                    main_ref[FLUID, x] = 1.0 - mask_ref[x].astype(F32)
                turned = roll(main_ref[k, x], 8 * slot + 8, 1)
                up[tile][x] = jnp.where(lane // RIM == slot, turned, up[tile][x])
                down[tile][x] = jnp.where(lane // RIM == (slot + 1) % 16, turned, down[tile][x])
    for tile in range(2):
        for x in range(4):
            odd_ref[tile, x] = jnp.where(odd, up[tile][x], down[tile][x])
            even_ref[tile, x] = jnp.where(odd, down[tile][x], up[tile][x])
    for copy in later:
        copy.wait()


def ring_kernel(seeds_ref, main_ref, odd_in_ref, even_in_ref, rim_ref, phase_ref, odd_ref, even_ref):
    del seeds_ref
    lane = lanes()
    odd = is_odd("vert")

    def row(x):
        above = [jnp.where(odd, odd_in_ref[t, x], even_in_ref[t, x]) for t in range(2)]
        below = [jnp.where(odd, even_in_ref[t, x], odd_in_ref[t, x]) for t in range(2)]
        even_group = lane // RIM % 2 == 0
        mixed = [
            (jnp.where(even_group, b, a), jnp.where(even_group, a, b)) for a, b in zip(above, below)
        ]
        sums = [None, None]
        for k in range(27):
            cells = main_ref[k, x]
            slot = k % 16
            rim = roll(mixed[k // 16][slot % 2], 120 - 8 * slot, 1)
            rim_ref[k, x] = rim
            if k < 7:
                sums = [a if b is None else a + b for a, b in zip((cells, rim), sums)]
        phase_ref[2 * x] = sums[0]
        phase_ref[2 * x + 1] = sums[1]

    for x in (3, 2, 1, 0):
        row(x)

    def cells_of(k, row):
        return (main_ref[k, row], rim_ref[k, row])

    messages = []
    for edge, inner, crossing, out in ((3, 2, TO_RIGHT, 1), (0, 1, TO_LEFT, 2)):
        pops = [cells_of(7 + q, edge) for q in range(19)]
        g = [cells_of(q, edge) for q in range(7)]
        fluid = both(lambda a: a > 0.5, cells_of(FLUID, edge))
        phi = load_pair(phase_ref, edge)
        pressure = both(lambda *p: total(p), *pops)
        omega = both(lambda p: 1.0 / (0.6 + 0.3 * jnp.clip(p, 0.0, 1.0)), phi)
        fields = [
            both(
                lambda a, b, f, o, p: jnp.where(f, (1.0 - o) * a + W[q] * (o * p), b),
                pops[q], pops[BACK[q]], fluid, omega, pressure,
            )
            for q in crossing
        ]
        turn = lambda a, b, f: jnp.where(f, -0.25 * a, b)
        fields.append(both(turn, g[out], g[BACK[out]], fluid))
        parts = [both(turn, g[0], g[0], fluid)]
        for q in range(3, 7):
            parts.append(moved(both(turn, g[q], g[BACK[q]], fluid), -DIRS[q][1], -DIRS[q][2]))
        grads = gradients(*(load_pair(phase_ref, inner + d) for d in (-1, 0, 1)))
        inner_phi = load_pair(phase_ref, inner)
        inner_pops = [cells_of(7 + q, inner) for q in range(19)]
        crossing_phase = []
        for t in range(2):
            mom = [momentum_of([p[t] for p in inner_pops], 0)] + [jnp.zeros((16, 128), F32)] * 2
            s = state_of(inner_phi[t], mom, tuple(gr[t] for gr in grads[:3]), grads[3][t])
            equil = 0.15625 * inner_phi[t] + (0.625 if out == 1 else -0.625) * carried_of(s, 0)
            crossing_phase.append(
                jnp.where(
                    cells_of(FLUID, inner)[t] > 0.5,
                    equil - 0.25 * cells_of(out, inner)[t],
                    cells_of(BACK[out], inner)[t],
                )
            )
        parts.append(tuple(crossing_phase))
        fields.append(both(lambda *p: total(p), *parts))
        fields.append(phi)
        for axis in range(3):
            fields.append(both(lambda *p: momentum_of(p, axis), *pops))
        fields.append(cells_of(FLUID, edge))
        fields.append(inner_phi)
        messages.append(fields)
    pack(odd_ref, even_ref, *messages, wide=WIDE_FIRST)


SHIFTS = sorted({c[1:] for c in DIRS})
BF16 = jnp.bfloat16


def probe_kernel(probes_ref, weights_ref, out_ref, acc_ref, code_ref):
    first_x = lax.axis_index("tile") * 4
    first_z = lax.axis_index("vert") * 128
    acc_ref[...] = jnp.zeros_like(acc_ref)
    count = jnp.zeros((8, 128), jnp.int32)
    groups = probes_ref.shape[1] // 8
    for i in range(groups):
        at = slice(8 * i, 8 * i + 8)
        x = probes_ref[0, at, :] - (first_x - 1)
        y = probes_ref[1, at, :]
        z = probes_ref[2, at, :] - first_z
        here = (x >= 0) & (x < 6) & (z >= -RIM) & (z < 128 + RIM)
        ring = jnp.where(z >= 0, z, z + 144)
        code_ref[at, :] = jnp.where(here, (x * 16 + y) * 256 + ring, -1)
        count = count + here.astype(jnp.int32)
    passes = jnp.max(count)
    across = lax.broadcasted_iota(jnp.int32, (96, 128), 0).astype(F32).astype(BF16)
    height = lax.broadcasted_iota(jnp.int32, (144, 128), 0).astype(F32).astype(BF16)
    zero = jnp.zeros((), BF16)
    one = jnp.ones((), BF16)

    def one_pass(i, carry):
        code = jnp.full((8, 128), -1, jnp.int32)
        weight = jnp.zeros((8, 128), F32)
        for i in range(groups):
            at = slice(8 * i, 8 * i + 8)
            here = code_ref[at, :]
            take = (here >= 0) & (code < 0)
            code = jnp.where(take, here, code)
            weight = jnp.where(take, weights_ref[at, :], weight)
            code_ref[at, :] = jnp.where(take, -1, here)
        code_xy = (code >> 8).astype(F32)
        code_z = (code & 255).astype(F32)
        high = weight.astype(BF16).astype(F32)
        low = weight - high
        lhs, rhs = [], []
        for n in range(8):
            line = lambda v: v[n : n + 1, :].astype(BF16)
            hit = across == line(code_xy)
            lhs.append(
                jnp.concatenate([jnp.where(hit, line(high), zero), jnp.where(hit, line(low), zero)], axis=0)
            )
            rhs.append(jnp.where(height == line(code_z), one, zero))
        acc_ref[...] += lax.dot_general(
            jnp.concatenate(lhs, axis=1), jnp.concatenate(rhs, axis=1), (((1,), (1,)), ((), ())),
            preferred_element_type=F32,
        )
        return carry

    lax.fori_loop(0, passes, one_pass, 0)
    lane = lanes()
    for x in range(6):
        rows = pl.ds(16 * x, 16)
        lows = pl.ds(96 + 16 * x, 16)
        main = acc_ref[rows, 0:128] + acc_ref[lows, 0:128]
        rim = acc_ref[rows, 128:144] + acc_ref[lows, 128:144]
        rim = jnp.concatenate([rim, jnp.zeros((16, 112), F32)], axis=1)
        rim = jnp.where(lane < RIM, rim, jnp.where(lane >= 120, roll(rim, 112, 1), 0.0))
        for n, (cy, cz) in enumerate(SHIFTS):
            store_pair(out_ref, moved((main, rim), cy, cz), n, x)


N_FIRST = 13
WIDE_FIRST = (7,)
N_SECOND = 8
HALVES = (slice(0, 8), slice(8, 16))
SENT_ROWS = ((0, 1), (1,), (-1,), (0, -1))
M2_KEYS = ((0, 0), (0, 1), (0, 2), (1, 1), (1, 2), (2, 2))


def spot(refs, row):
    if row in (1, 2):
        return refs[0], row - 1
    return refs[1], {-1: 0, 0: 1, 3: 2, 4: 3}[row]


def prim_at(prims, row, t, h):
    ref, at = spot(prims, row)
    vals = [ref[k, 2 * at + t, h, :] for k in range(10)]
    return state_of(vals[0], vals[6:9], tuple(vals[1:4]), vals[4]), vals[5], vals[9] > 0.5


def put_gradients(prims, phase_pairs, row):
    ref, at = spot(prims, row)
    grads = gradients(*phase_pairs)
    store_pair(ref, phase_pairs[1], 0, at)
    for i in range(4):
        store_pair(ref, grads[i], 1 + i, at)


def forward(cells_ref, prims, posts, row, t):
    prim_ref, at = spot(prims, row)
    post_ref, _ = spot(posts, row)
    i = 2 * at + t
    for h in HALVES:
        g = [cells_ref[q, row, h, :] for q in range(7)]
        f = [cells_ref[7 + q, row, h, :] for q in range(19)]
        prim_ref[5, i, h, :] = total(f)
        for axis in range(3):
            prim_ref[6 + axis, i, h, :] = momentum_of(f, axis)
        prim_ref[9, i, h, :] = cells_ref[FLUID, row, h, :]
        s, pressure, fluid = prim_at(prims, row, t, h)
        for q, v in post_flow(f, fluid, pressure, s, range(19)).items():
            post_ref[7 + q, i, h, :] = v
        for q, v in post_phase(g, fluid, s, range(7)).items():
            post_ref[q, i, h, :] = v


def stream(posts, row):
    ref, at = spot(posts, row)
    for q in range(19):
        _, cy, cz = DIRS[q]
        if (cy or cz) and 0 <= row + DIRS[q][0] < 4:
            store_pair(ref, moved(load_pair(ref, 7 + q, at), -cy, -cz), 7 + q, at)


def inner_kernel(main_ref, rim_ref, phase_ref, seeds_ref, prim_ref, post_ref, moments_ref):
    prims, posts = (prim_ref, None), (post_ref, None)
    for row in (1, 2):
        put_gradients(prims, [load_pair(phase_ref, row + d) for d in (-1, 0, 1)], row)
        for t, cells_ref in enumerate((main_ref, rim_ref)):
            forward(cells_ref, prims, posts, row, t)
        stream(posts, row)

    def moments(i, carry):
        for h in HALVES:
            adj = {q: seeds_ref[SHIFTS.index(DIRS[q][1:]), i + 2 + 2 * DIRS[q][0], h, :] for q in range(19)}
            m0, m1, m2 = moments_of(adj)
            for k, v in enumerate([m0] + m1 + [m2[key] for key in M2_KEYS]):
                moments_ref[k, i, h, :] = v
        return carry

    lax.fori_loop(0, 8, moments, 0)


def middle_kernel(
    main_ref, rim_ref, phase_ref, odd_in_ref, even_in_ref, seeds_ref, moments_ref, prim_in_ref, post_in_ref,
    prim_ref, adj_ref, gamma_ref, edges_ref, odd_ref, even_ref,
    post_ref, phase_mid_ref, grad_mid_ref, back_ref, dphi_ref,
):
    prims, posts = (prim_in_ref, prim_ref), (post_in_ref, post_ref)
    from_left, from_right = received(odd_in_ref, even_in_ref, N_FIRST, WIDE_FIRST)
    sides = ((from_left, -1, TO_RIGHT, 1), (from_right, 4, TO_LEFT, 2))
    for got, row, crossing, out in sides:
        _, at = spot(prims, row)
        for i in range(3):
            store_pair(prim_ref, got[8 + i], 6 + i, at)
        store_pair(prim_ref, got[11], 9, at)
        for q, pair in zip(crossing, got[:5]):
            store_pair(post_ref, pair, 7 + q, at)
        store_pair(post_ref, got[5], out, at)
    phases = [from_left[12], from_left[7]] + [load_pair(phase_ref, r) for r in range(4)]
    phases += [from_right[7], from_right[12]]
    for row in (-1, 0, 3, 4):
        put_gradients(prims, phases[row + 1 : row + 4], row)
    for row in (0, 3):
        for t, cells_ref in enumerate((main_ref, rim_ref)):
            forward(cells_ref, prims, posts, row, t)
        stream(posts, row)

    mid_parts = {}
    for got, row, crossing, out in sides:
        _, at = spot(posts, row)
        spread = [[], [], []]
        for t in range(2):
            i = 2 * at + t
            halves = [[], [], []]
            for h in HALVES:
                vals = [prim_ref[k, i, h, :] for k in range(10) if k != 5]
                s = state_of(vals[0], vals[5:8], tuple(vals[1:4]), vals[4])
                fluid = vals[8] > 0.5
                vel, force, omega, kappa = s["vel"], s["force"], s["omega"], s["kappa"]
                base = -1.5 * omega * dot(vel, vel) - 3.0 * kappa * dot(vel, force)
                odd_vec = tuple(3.0 * (omega * v + kappa * f) for v, f in zip(vel, force))
                even_vec = tuple(4.5 * omega * v + 9.0 * kappa * f for v, f in zip(vel, force))
                for q in crossing:
                    step = DIRS[q]
                    gain = base + along(step, vel) * along(step, even_vec) + along(step, odd_vec)
                    kept = post_ref[7 + q, i, h, :]
                    post_ref[7 + q, i, h, :] = jnp.where(fluid, kept + W[q] * gain, kept)
                sharp, _ = sharpening(s)
                carried = tuple(s["phi"] * v + sharp * gr for v, gr in zip(vel, s["grad"]))
                kept = post_ref[out, i, h, :]
                gain = 0.15625 * s["phi"] + 0.625 * along(DIRS[out], carried)
                post_ref[out, i, h, :] = jnp.where(fluid, kept + gain, kept)
                halves[0].append(jnp.where(fluid, s["phi"], 0.0))
                halves[1].append(jnp.where(fluid, carried[1], 0.0))
                halves[2].append(jnp.where(fluid, carried[2], 0.0))
            for n in range(3):
                spread[n].append(jnp.concatenate(halves[n], axis=0))
        stream(posts, row)
        phi, cy, cz = (tuple(x) for x in spread)
        gain_y = lambda sign: both(lambda p, c: 0.15625 * p + sign * 0.625 * c, phi, cy)
        gain_z = lambda sign: both(lambda p, c: 0.15625 * p + sign * 0.625 * c, phi, cz)
        mid_parts[row] = [
            got[6], both(lambda p: 0.3125 * p, phi),
            moved(gain_y(1.0), -1, 0), moved(gain_y(-1.0), 1, 0),
            moved(gain_z(1.0), 0, -1), moved(gain_z(-1.0), 0, 1),
        ]
    def post_pair(q, row):
        ref, at = spot(posts, row)
        return load_pair(ref, q, at)

    for row in range(-1, 5):
        parts = mid_parts.get(row)
        if parts is None:
            parts = [post_pair(0, row)]
            for q in range(3, 7):
                parts.append(moved(post_pair(q, row), -DIRS[q][1], -DIRS[q][2]))
        if row > -1:
            parts.append(post_pair(1, row - 1))
        if row < 4:
            parts.append(post_pair(2, row + 1))
        store_pair(phase_mid_ref, both(lambda *p: total(p), *parts), row + 1)
    for row in range(4):
        grads = gradients(*(load_pair(phase_mid_ref, row + d) for d in (0, 1, 2)))
        for i in range(4):
            store_pair(grad_mid_ref, grads[i], i, row)
    def backward(row, t, h):
        i = 2 * row + t
        f = []
        for q in range(19):
            ref, at = spot(posts, row - DIRS[q][0])
            f.append(ref[7 + q, 2 * at + t, h, :])
        adj = {q: seeds_ref[SHIFTS.index(DIRS[q][1:]), i + 2 + 2 * DIRS[q][0], h, :] for q in range(19)}
        ref, at = spot(prims, row)
        fluid = ref[9, 2 * at + t, h, :] > 0.5
        phi = phase_mid_ref[i + 2, h, :]
        mom = [momentum_of(f, axis) for axis in range(3)]
        s = state_of(phi, mom, tuple(grad_mid_ref[k, i, h, :] for k in range(3)), grad_mid_ref[3, i, h, :])
        kept = total([adj[q] * f[q] for q in range(19)])
        m = [moments_ref[k, i, h, :] for k in range(10)]
        m2 = {}
        for key, value in zip(M2_KEYS, m[4:]):
            m2[key] = m2[key[::-1]] = value
        d_flow, d_phi, d_grad, d_lap = pull_all(s, total(f), adj, kept, m[0], m[1:4], m2, None, None)
        for q in range(19):
            adj_ref[q, i, h, :] = jnp.where(fluid, d_flow[q], adj[BACK[q]])
        dphi_ref[i, h, :] = jnp.where(fluid, d_phi, 0.0)
        for k in range(3):
            back_ref[k, i, h, :] = jnp.where(fluid, d_grad[k], 0.0)
        back_ref[3, i, h, :] = jnp.where(fluid, d_lap, 0.0)

    for row in range(4):
        for t in range(2):
            for h in HALVES:
                backward(row, t, h)

    for row in range(4):
        for q in range(19):
            if DIRS[q][1:] != (0, 0) and DIRS[q][0] in SENT_ROWS[row]:
                store_pair(adj_ref, moved(load_pair(adj_ref, q, row), *DIRS[q][1:]), q, row)

    for row in range(4):
        store_pair(gamma_ref, stencil_back(back_ref, dphi_ref, row), row)
    edge_parts = []
    for row, part in ((0, ahead_part), (3, behind_part)):
        pair = both(part, load_pair(back_ref, 0, row), load_pair(back_ref, 3, row))
        store_pair(edges_ref, pair, 0 if row == 0 else 1)
        edge_parts.append(pair)

    messages = []
    for row, out_dirs, part, sign, edge_pair in (
        (3, TO_RIGHT, behind_part, -1.0, edge_parts[1]),
        (0, TO_LEFT, ahead_part, 1.0, edge_parts[0]),
    ):
        gamma = load_pair(gamma_ref, row)
        next_gamma = load_pair(gamma_ref, row - 1 if row == 3 else row + 1)
        n1 = turn_gamma(both(lambda a: sign * a, next_gamma), gamma)
        partial = []
        for t in range(2):
            s, _, fluid = prim_at(prims, row, t, slice(None))
            adj = {
                q: adj_ref[q, 2 * (row + DIRS[q][0]) + t] for q in range(19) if q not in out_dirs
            }
            m0, m1, m2 = moments_of(adj)
            d_grad, d_lap = pull_stencil(s, m0, m1, m2, [n[t] for n in n1])[:2]
            partial.append(jnp.where(fluid, part(d_grad[0], d_lap), 0.0))
        back_dirs = TO_LEFT if row == 3 else TO_RIGHT
        fields = [load_pair(adj_ref, q, row) for q in back_dirs]
        fields += [gamma, edge_pair, tuple(partial)]
        messages.append(fields)
    pack(odd_ref, even_ref, *messages)


def turn_gamma(along_x, centre):
    diff = lambda a, b: 0.125 * (a - b)
    return (
        both(lambda a: 0.125 * a, along_x),
        both(diff, moved(centre, 1, 0), moved(centre, -1, 0)),
        both(diff, moved(centre, 0, 1), moved(centre, 0, -1)),
    )


def stencil_back(back_ref, start_ref, row, first=None, last=None):
    gy, gz, lap = (load_pair(back_ref, k, row) for k in (1, 2, 3))
    fold = lambda l, gyb, gya, lyb, lya, gzb, gza, lzb, lza: (
        0.5 * (gyb - gya) + lyb + lya + 0.5 * (gzb - gza) + lzb + lza - 6.0 * l
    )
    out = both(
        fold, lap,
        moved(gy, -1, 0), moved(gy, 1, 0), moved(lap, -1, 0), moved(lap, 1, 0),
        moved(gz, 0, -1), moved(gz, 0, 1), moved(lap, 0, -1), moved(lap, 0, 1),
    )
    add = lambda a, b: a + b
    if start_ref is not None:
        out = both(add, out, load_pair(start_ref, row))
    if row > 0:
        out = both(add, out, both(behind_part, load_pair(back_ref, 0, row - 1), load_pair(back_ref, 3, row - 1)))
    elif first is not None:
        out = both(add, out, first)
    if row < 3:
        out = both(add, out, both(ahead_part, load_pair(back_ref, 0, row + 1), load_pair(back_ref, 3, row + 1)))
    elif last is not None:
        out = both(add, out, last)
    return out


def ahead_kernel(
    main_ref, prim_in_ref, prim_out_ref, adj_ref, gamma_ref,
    flow_ref, back_ref, dphi_ref,
    turned_ref, shifted_ref,
):
    prims = (prim_in_ref, prim_out_ref)
    for row in range(4):
        for q in range(19):
            if DIRS[q][1:] != (0, 0) and DIRS[q][0] not in SENT_ROWS[row]:
                store_pair(shifted_ref, moved(load_pair(adj_ref, q, row), *DIRS[q][1:]), q, row)

    def adjoint(q, row, t, h):
        step = DIRS[q]
        at = row + step[0]
        ref = adj_ref if step[1:] == (0, 0) or step[0] in SENT_ROWS[at] else shifted_ref
        return ref[q, 2 * at + t, h, :]

    for row in (1, 2):
        centre = load_pair(gamma_ref, row)
        for n, (cy, cz) in enumerate(((1, 0), (-1, 0), (0, 1), (0, -1))):
            store_pair(turned_ref, moved(centre, cy, cz), n, row - 1)
    for row in range(4):
        for t in range(2):
            for h in HALVES:
                i = 2 * row + t
                s, pressure, fluid = prim_at(prims, row, t, h)
                adj = {q: adjoint(q, row, t, h) for q in range(19) if 0 <= row + DIRS[q][0] < 4}
                m0, m1, m2 = moments_of(adj)
                n0 = n1 = None
                if row in (1, 2):
                    g = [gamma_ref[i + 2, h, :], gamma_ref[i - 2, h, :]]
                    g += [turned_ref[n, i - 2, h, :] for n in range(4)]
                    n1 = [0.125 * (g[a] - g[a + 1]) for a in (0, 2, 4)]
                if t == 1:
                    d_grad, d_lap = pull_stencil(s, m0, m1, m2, n1)[:2]
                else:
                    if row in (1, 2):
                        n0 = 0.25 * gamma_ref[i, h, :] + 0.125 * total(g)
                    kept = total([a * main_ref[7 + q, row, h, :] for q, a in adj.items()])
                    d_flow, d_phi, d_grad, d_lap = pull_all(s, pressure, adj, kept, m0, m1, m2, n0, n1)
                    for q in range(19):
                        flow_ref[q, row, h, :] = jnp.where(fluid, d_flow[q], adj.get(BACK[q], 0.0))
                    dphi_ref[row, h, :] = jnp.where(fluid, d_phi, 0.0)
                for k in range(3):
                    back_ref[k, i, h, :] = jnp.where(fluid, d_grad[k], 0.0)
                back_ref[3, i, h, :] = jnp.where(fluid, d_lap, 0.0)


def last_kernel(
    main_ref, prim_in_ref, prim_out_ref, adj_ref, gamma_ref, edges_ref, flow_ref, back_in_ref, dphi_in_ref,
    odd_in_ref, even_in_ref,
    out_g_ref, out_f_ref,
    gamma_wide_ref, turned_ref, back_ref, dphi_ref, g_ref, f_ref, sems,
):
    add = lambda a, b: a + b
    prims = (prim_in_ref, prim_out_ref)
    copies = []

    def send(src, dst):
        copies.append(pltpu.make_async_copy(src, dst, sems.at[len(copies)]))
        copies[-1].start()

    got_left, got_right = received(odd_in_ref, even_in_ref, N_SECOND)
    own_first = load_pair(edges_ref, 0)
    own_last = load_pair(edges_ref, 1)

    for row, more, sign in ((1, got_left[6], -0.125), (2, got_right[6], 0.125)):
        for t in range(2):
            for n, h in enumerate(HALVES):
                i = 2 * row + t
                s, _, fluid = prim_at(prims, row, t, h)
                delta = more[t][8 * n : 8 * n + 8]
                d_vel, d_phi, d_grad, d_lap = pull_along_x(s, 0.125 * delta, sign * delta)
                if t == 0:
                    lift = jnp.where(fluid, d_vel, 0.0)
                    for q in range(19):
                        base = flow_ref[q, row, h, :]
                        f_ref[q, row, h, :] = base + DIRS[q][0] * lift if DIRS[q][0] else base
                    dphi_ref[row, h, :] = dphi_in_ref[row, h, :] + jnp.where(fluid, d_phi, 0.0)
                for k in range(3):
                    back_ref[k, i, h, :] = back_in_ref[k, i, h, :] + jnp.where(fluid, d_grad[k], 0.0)
                back_ref[3, i, h, :] = back_in_ref[3, i, h, :] + jnp.where(fluid, d_lap, 0.0)
    send(f_ref.at[:, pl.ds(1, 2)], out_f_ref.at[:, pl.ds(1, 2)])

    for row in (1, 2):
        store_pair(gamma_wide_ref, load_pair(gamma_ref, row), row + 1)
    store_pair(gamma_wide_ref, both(add, load_pair(gamma_ref, 0), got_left[6]), 1)
    store_pair(gamma_wide_ref, both(add, load_pair(gamma_ref, 3), got_right[6]), 4)
    store_pair(gamma_wide_ref, both(add, got_left[5], own_first), 0)
    store_pair(gamma_wide_ref, both(add, got_right[5], own_last), 5)
    for row in range(4):
        centre = load_pair(gamma_wide_ref, row + 1)
        for n, (cy, cz) in enumerate(((1, 0), (-1, 0), (0, 1), (0, -1))):
            store_pair(turned_ref, moved(centre, cy, cz), n, row)

    def phase_adjoints(i, h):
        at = [gamma_wide_ref[i + 2, h, :], gamma_wide_ref[i + 4, h, :], gamma_wide_ref[i, h, :]]
        return at + [turned_ref[n, i, h, :] for n in range(4)]

    for row, got, dirs in ((0, got_left, TO_LEFT), (3, got_right, TO_RIGHT)):
        for t in range(2):
            for n, h in enumerate(HALVES):
                i = 2 * row + t
                s, pressure, fluid = prim_at(prims, row, t, h)
                adj = {q: pair[t][8 * n : 8 * n + 8] for q, pair in zip(dirs, got[:5])}
                g = phase_adjoints(i, h)
                n1 = [0.125 * (g[a] - g[a + 1]) for a in (1, 3, 5)]
                m0, m1, m2 = moments_of(adj)
                if t == 1:
                    d_grad, d_lap = pull_stencil(s, m0, m1, m2, n1)[:2]
                else:
                    n0 = 0.25 * g[0] + 0.125 * total(g[1:])
                    kept = total([a * main_ref[7 + q, row, h, :] for q, a in adj.items()])
                    d_flow, d_phi, d_grad, d_lap = pull_all(s, pressure, adj, kept, m0, m1, m2, n0, n1)
                    for q in range(19):
                        more = jnp.where(fluid, d_flow[q], adj.get(BACK[q], 0.0))
                        f_ref[q, row, h, :] = flow_ref[q, row, h, :] + more
                    dphi_ref[row, h, :] = dphi_in_ref[row, h, :] + jnp.where(fluid, d_phi, 0.0)
                for k in range(3):
                    back_ref[k, i, h, :] = back_in_ref[k, i, h, :] + jnp.where(fluid, d_grad[k], 0.0)
                back_ref[3, i, h, :] = back_in_ref[3, i, h, :] + jnp.where(fluid, d_lap, 0.0)
        send(f_ref.at[:, pl.ds(row, 1)], out_f_ref.at[:, pl.ds(row, 1)])

    edge_parts = []
    for got, prim_row, row, own, out_dirs, part, sign in (
        (got_left, -1, 0, own_first, TO_RIGHT, behind_part, 1.0),
        (got_right, 4, 3, own_last, TO_LEFT, ahead_part, -1.0),
    ):
        gamma = load_pair(gamma_wide_ref, row + 1)
        n1 = turn_gamma(both(lambda a: sign * a, gamma), own)
        pair = []
        for t in range(2):
            s, _, fluid = prim_at(prims, prim_row, t, slice(None))
            adj = {q: adj_ref[q, 2 * row + t] for q in out_dirs}
            m0, m1, m2 = moments_of(adj)
            d_grad, d_lap = pull_stencil(s, m0, m1, m2, [n[t] for n in n1])[:2]
            pair.append(got[7][t] + jnp.where(fluid, part(d_grad[0], d_lap), 0.0))
        edge_parts.append(tuple(pair))

    for row in range(4):
        rest = stencil_back(back_ref, None, row, edge_parts[0], edge_parts[1])[0]
        ref, at = spot(prims, row)
        fluid = ref[9, 2 * at] > 0.5
        base = rest + dphi_ref[row]
        phase_adj = phase_adjoints(2 * row, slice(None))
        for q in range(7):
            g_ref[q, row] = jnp.where(fluid, base - 0.25 * phase_adj[q], rest + phase_adj[BACK[q]])
        send(g_ref.at[:, pl.ds(row, 1)], out_g_ref.at[:, pl.ds(row, 1)])
    for copy in copies:
        copy.wait()


def call(kernel, outs, n_in, scratch=(), flops=0, name=None, any_in=0, any_out=False):
    vmem = pl.BlockSpec(memory_space=pltpu.VMEM)
    return pl.pallas_call(
        kernel,
        out_shape=[jax.ShapeDtypeStruct(x, F32) if isinstance(x, tuple) else x for x in outs],
        in_specs=[pl.BlockSpec(memory_space=pl.ANY)] * any_in + [vmem] * (n_in - any_in),
        out_specs=[pl.BlockSpec(memory_space=pl.ANY) if any_out else vmem] * len(outs),
        scratch_shapes=[pltpu.VMEM(x, F32) if isinstance(x, tuple) else x for x in scratch],
        compiler_params=pltpu.CompilerParams(vmem_limit_bytes=VMEM_LIMIT),
        cost_estimate=pl.CostEstimate(flops=flops, bytes_accessed=flops // 8, transcendentals=0),
        name=name,
    )


def swap(x, axis, first):
    pairs = []
    for i in range(first, lax.axis_size(axis) - 1, 2):
        pairs += [(i, i + 1), (i + 1, i)]
    return lax.ppermute(x, axis, pairs)


def shards(phase_init, flow_init, solid_mask, sensor_cells, sensor_weights):
    tile = (16, 128)
    cells = sensor_cells.reshape(3, -1, 128).transpose(1, 0, 2)
    weights = sensor_weights.reshape(-1, 128)
    main, probes, weights, odd, even = call(
        rim_kernel,
        [(27, 4) + tile, jax.ShapeDtypeStruct((3,) + weights.shape, jnp.int32), weights.shape] + [(2, 4) + tile] * 2,
        5, any_in=5, flops=10**6, name="rim",
        scratch=[pltpu.VMEM((4,) + tile, jnp.int32), pltpu.SemaphoreType.DMA((10,))],
    )(*(pltpu.with_memory_space_constraint(x, pltpu.HBM) for x in (phase_init, flow_init, solid_mask, cells, weights)))
    odd, even = swap(odd, "vert", 1), swap(even, "vert", 0)
    (seeds,) = call(probe_kernel, [(9, 12) + tile], 2, scratch=[(192, 144), pltpu.VMEM(weights.shape, jnp.int32)], flops=2 * 10**9, name="probes")(
        probes, weights
    )
    first = message_tiles(N_FIRST, WIDE_FIRST)
    rim, phase, odd, even = call(
        ring_kernel, [(27, 4) + tile, (8,) + tile] + [(first,) + tile] * 2, 4, any_in=1, flops=10**7, name="ring"
    )(seeds, main, odd, even)
    odd, even = swap(odd, "tile", 1), swap(even, "tile", 0)
    prim_in, post_in, moments = call(
        inner_kernel, [(10, 4) + tile, (26, 4) + tile, (10, 8) + tile], 4, flops=2 * 10**8, name="inner"
    )(main, rim, phase, seeds)
    second = message_tiles(N_SECOND)
    prim_out, adj, gamma, edges, odd, even = call(
        middle_kernel,
        [(10, 8) + tile, (19, 8) + tile, (8,) + tile, (4,) + tile] + [(second,) + tile] * 2,
        9,
        scratch=[(26, 8) + tile, (12,) + tile, (4, 8) + tile, (4, 8) + tile, (8,) + tile],
        flops=10**8, name="middle",
    )(main, rim, phase, odd, even, seeds, moments, prim_in, post_in)
    odd, even = swap(odd, "tile", 1), swap(even, "tile", 0)
    flow, back, dphi = call(
        ahead_kernel, [(19, 4) + tile, (4, 8) + tile, (4,) + tile], 5, scratch=[(4, 4) + tile, (19, 8) + tile],
        flops=2 * 10**8, name="ahead",
    )(main, prim_in, prim_out, adj, gamma)
    return tuple(
        call(
            last_kernel,
            [(7, 4) + tile, (19, 4) + tile],
            11,
            scratch=[
                (12,) + tile, (4, 8) + tile, (4, 8) + tile, (4,) + tile, (7, 4) + tile, (19, 4) + tile,
                pltpu.SemaphoreType.DMA((7,)),
            ],
            flops=10**8, name="last", any_out=True,
        )(main, prim_in, prim_out, adj, gamma, edges, flow, back, dphi, odd, even)
    )


def solution(mesh):
    return jax.shard_map(
        shards,
        mesh=mesh,
        in_specs=(
            P(None, "tile", None, "vert"),
            P(None, "tile", None, "vert"),
            P("tile", None, "vert"),
            P(),
            P(),
        ),
        out_specs=(P(None, "tile", None, "vert"), P(None, "tile", None, "vert")),
        check_vma=False,
    )
```

```python
import functools

import jax
import jax.numpy as jnp
import numpy as np
from jax import lax
from jax.experimental import pallas as pl
from jax.experimental.pallas import tpu as pltpu
from jax.sharding import PartitionSpec as P

DIRS = [
    (0, 0, 0), (1, 0, 0), (-1, 0, 0), (0, 1, 0), (0, -1, 0), (0, 0, 1), (0, 0, -1),
    (1, 1, 0), (-1, -1, 0), (1, -1, 0), (-1, 1, 0), (1, 0, 1), (-1, 0, -1), (1, 0, -1),
    (-1, 0, 1), (0, 1, 1), (0, -1, -1), (0, 1, -1), (0, -1, 1),
]
BACK = [0, 2, 1, 4, 3, 6, 5, 8, 7, 10, 9, 12, 11, 14, 13, 16, 15, 18, 17]
W = [1.0 / 3.0] + [1.0 / 18.0] * 6 + [1.0 / 36.0] * 12
W0, W1, W2 = 1.0 / 3.0, 1.0 / 18.0, 1.0 / 36.0
PAIRS = [(q, q + 1) for q in range(1, 19, 2)]
TO_RIGHT = [q for q in range(19) if DIRS[q][0] == 1]
TO_LEFT = [q for q in range(19) if DIRS[q][0] == -1]
RIM = 8
SHARP = 0.075
FLUID = 26
F32 = jnp.float32
VMEM_LIMIT = 40 * 2**20


def lanes():
    return lax.broadcasted_iota(jnp.int32, (16, 128), 1)


def roll(x, shift, axis):
    shift = shift % x.shape[axis]
    return x if shift == 0 else pltpu.roll(x, shift, axis)


def load_pair(ref, *at):
    *head, row = at
    return (ref[(*head, 2 * row)], ref[(*head, 2 * row + 1)])


def store_pair(ref, pair, *at):
    *head, row = at
    ref[(*head, 2 * row)] = pair[0]
    ref[(*head, 2 * row + 1)] = pair[1]


def both(fn, *pairs):
    return tuple(fn(*each) for each in zip(*pairs))


def moved(pair, step_y, step_z):
    if step_y:
        pair = both(lambda t: roll(t, -step_y, 0), pair)
    if step_z:
        a = roll(pair[0], -step_z, 1)
        b = roll(pair[1], -step_z, 1)
        edge = lanes() == (127 if step_z > 0 else 0)
        pair = (jnp.where(edge, b, a), jnp.where(edge, a, b))
    return pair


def is_odd(axis):
    return jnp.full((16, 128), lax.rem(lax.axis_index(axis), 2), jnp.int32) == 1


def rim_slots(count, wide):
    slots, at = [], 0
    for k in range(count):
        width = 8 if k in wide else 4
        if at % 128 + 2 * width > 128:
            at += 128 - at % 128
        slots.append((at // 128, at % 128, width))
        at += 2 * width
    return slots


def message_tiles(count, wide=()):
    return count + rim_slots(count, wide)[-1][0] + 1


def packed(fields, wide):
    lane = lanes()
    out = [main for main, _ in fields]
    slots = rim_slots(len(fields), wide)
    for tile in range(slots[-1][0] + 1):
        acc = jnp.zeros((16, 128), F32)
        for (at, first, width), (_, rim) in zip(slots, fields):
            if at == tile:
                mine = (lane >= first) & (lane < first + 2 * width)
                acc = jnp.where(mine, roll(rim, first + width, 1), acc)
        out.append(acc)
    return out


def pack(odd_ref, even_ref, right, left, wide=()):
    odd = is_odd("tile")
    for n, (r, l) in enumerate(zip(packed(right, wide), packed(left, wide))):
        odd_ref[n] = jnp.where(odd, r, l)
        even_ref[n] = jnp.where(odd, l, r)


def received(odd_ref, even_refs, count, wide=()):
    odd = is_odd("tile")
    slots = rim_slots(count, wide)
    tiles = message_tiles(count, wide)
    got_odd = [odd_ref[n] for n in range(tiles)]
    got_even = [total([ref[n] for ref in even_refs]) for n in range(tiles)]
    sides = []
    for one, two in ((got_even, got_odd), (got_odd, got_even)):
        msg = [jnp.where(odd, a, b) for a, b in zip(one, two)]
        sides.append(
            [(msg[k], roll(msg[count + at], -(first + width), 1)) for k, (at, first, width) in enumerate(slots)]
        )
    return sides


def total(values):
    out = values[0]
    for value in values[1:]:
        out = out + value
    return out


def along(step, vec):
    out = None
    for c, v in zip(step, vec):
        if c == 0:
            continue
        if out is None:
            out = v if c > 0 else -v
        else:
            out = out + v if c > 0 else out - v
    return out


def momentum_of(pops, axis):
    plus = [pops[q] for q in range(19) if DIRS[q][axis] == 1]
    minus = [pops[q] for q in range(19) if DIRS[q][axis] == -1]
    return total([a - b for a, b in zip(plus, minus)])


def state_of(phi, mom, grad, lap):
    clipped = jnp.clip(phi, 0.0, 1.0)
    rho = 0.05 + 0.95 * clipped
    omega = 1.0 / (0.6 + 0.3 * clipped)
    inv_rho = 1.0 / rho
    potential = 1.2 * phi * (phi - 1.0) * (phi - 0.5) - 0.6 * lap
    force = (
        potential * grad[0] - 0.01 * rho,
        potential * grad[1],
        potential * grad[2] - 0.02 * (rho - 0.05),
    )
    half = 0.5 * inv_rho
    vel = tuple(m + f * half for m, f in zip(mom, force))
    kappa = (1.0 - 0.5 * omega) * inv_rho
    return dict(
        phi=phi, grad=grad, omega=omega, inv_rho=inv_rho, potential=potential, force=force,
        half=half, vel=vel, kappa=kappa,
    )


def dot(a, b):
    return a[0] * b[0] + a[1] * b[1] + a[2] * b[2]


def sharpening(s):
    inv_len = lax.rsqrt(dot(s["grad"], s["grad"]) + 0.01)
    return SHARP * s["phi"] * (1.0 - s["phi"]) * inv_len, inv_len


def carried_of(s, axis):
    sharp, _ = sharpening(s)
    return s["phi"] * s["vel"][axis] + sharp * s["grad"][axis]


def post_flow(pops, fluid, pressure, s, wanted):
    vel, force, omega, kappa = s["vel"], s["force"], s["omega"], s["kappa"]
    base = omega * (pressure - 1.5 * dot(vel, vel)) - 3.0 * kappa * dot(vel, force)
    odd_vec = tuple(3.0 * (omega * v + kappa * f) for v, f in zip(vel, force))
    even_vec = tuple(4.5 * omega * v + 9.0 * kappa * f for v, f in zip(vel, force))
    keep = 1.0 - omega
    out = {}
    if 0 in wanted:
        out[0] = jnp.where(fluid, keep * pops[0] + W0 * base, pops[0])
    for q, r in PAIRS:
        if q not in wanted and r not in wanted:
            continue
        step = DIRS[q]
        even = base + along(step, vel) * along(step, even_vec)
        odd = along(step, odd_vec)
        if q in wanted:
            out[q] = jnp.where(fluid, keep * pops[q] + W[q] * (even + odd), pops[r])
        if r in wanted:
            out[r] = jnp.where(fluid, keep * pops[r] + W[q] * (even - odd), pops[q])
    return out


def post_phase(pops, fluid, s, wanted):
    sharp, _ = sharpening(s)
    carried = tuple(s["phi"] * v + sharp * g for v, g in zip(s["vel"], s["grad"]))
    out = {}
    for q in wanted:
        if q == 0:
            out[q] = jnp.where(fluid, 0.3125 * s["phi"] - 0.25 * pops[0], pops[0])
        else:
            equil = 0.15625 * s["phi"] + 0.625 * along(DIRS[q], carried)
            out[q] = jnp.where(fluid, equil - 0.25 * pops[q], pops[BACK[q]])
    return out


def moments_of(adj):
    zero = None
    m0, m1 = [], [[], [], []]
    m2 = {}
    if 0 in adj:
        m0.append(W0 * adj[0])
    groups = {W1: [], W2: []}
    for q in range(1, 19):
        if q not in adj:
            continue
        a = adj[q]
        w = W[q]
        groups[w].append(a)
    for w, items in groups.items():
        if items:
            m0.append(w * total(items))

    def weighted(terms):
        parts = []
        for w in (W1, W2):
            mine = [(sign, a) for ww, sign, a in terms if ww == w]
            if not mine:
                continue
            acc = None
            for sign, a in mine:
                if acc is None:
                    acc = a if sign > 0 else -a
                else:
                    acc = acc + a if sign > 0 else acc - a
            parts.append(w * acc)
        return total(parts) if parts else None

    for i in range(3):
        m1[i] = weighted([(W[q], DIRS[q][i], adj[q]) for q in range(1, 19) if q in adj and DIRS[q][i]])
    for i in range(3):
        for j in range(i, 3):
            m2[(i, j)] = weighted(
                [
                    (W[q], DIRS[q][i] * DIRS[q][j], adj[q])
                    for q in range(1, 19)
                    if q in adj and DIRS[q][i] and DIRS[q][j]
                ]
            )
            m2[(j, i)] = m2[(i, j)]
    return total(m0), m1, m2


def apply_m2(m2, vec):
    out = []
    for i in range(3):
        terms = [m2[(i, j)] * vec[j] for j in range(3) if m2[(i, j)] is not None]
        out.append(total(terms))
    return out


def pull_stencil(s, m0, m1, m2, n1):
    vel, force = s["vel"], s["force"]
    omega, kappa, half = s["omega"], s["kappa"], s["half"]
    m2v = apply_m2(m2, vel)
    m2f = apply_m2(m2, force)
    m0_3 = 3.0 * m0
    lean = []
    for i in range(3):
        term = 9.0 * m2v[i] - m0_3 * vel[i]
        lean.append(term if m1[i] is None else term + 3.0 * m1[i])
    push = [9.0 * m2f[i] - m0_3 * force[i] for i in range(3)]
    d_vel = [omega * a + kappa * b for a, b in zip(lean, push)]
    if n1 is not None:
        five_phi = 5.0 * s["phi"]
        d_vel = [d + five_phi * n for d, n in zip(d_vel, n1)]
    d_force = [kappa * a + half * d for a, d in zip(lean, d_vel)]
    d_potential = dot(d_force, s["grad"])
    d_grad = [s["potential"] * x for x in d_force]
    if n1 is not None:
        sharp, inv_len = sharpening(s)
        tilt = dot(s["grad"], n1) * inv_len * inv_len
        sharp5 = 5.0 * sharp
        d_grad = [d + sharp5 * (n - g * tilt) for d, n, g in zip(d_grad, n1, s["grad"])]
    d_lap = -0.6 * d_potential
    return d_grad, d_lap, d_potential, d_force, d_vel, m2v, m2f


def inside_clip(phi):
    return jnp.where((phi > 0.0) & (phi < 1.0), 1.0, jnp.where((phi == 0.0) | (phi == 1.0), 0.5, 0.0))


def pull_all(s, pressure, adj, kept, m0, m1, m2, n0, n1):
    d_grad, d_lap, d_potential, d_force, d_vel, m2v, m2f = pull_stencil(s, m0, m1, m2, n1)
    phi, vel, force = s["phi"], s["vel"], s["force"]
    omega, kappa, inv_rho, half = s["omega"], s["kappa"], s["inv_rho"], s["half"]
    relaxed = m0 * (pressure - 1.5 * dot(vel, vel)) + 3.0 * dot(m1, vel) + 4.5 * dot(m2v, vel)
    forced = 3.0 * dot(m1, force) - 3.0 * m0 * dot(vel, force) + 9.0 * dot(m2v, force)
    d_omega = relaxed - kept - 0.5 * inv_rho * forced
    d_rho = (
        -kappa * inv_rho * forced
        - 0.01 * d_force[0]
        - 0.02 * d_force[2]
        - dot(d_vel, force) * half * inv_rho
    )
    d_clip = 0.95 * d_rho - 0.3 * omega * omega * d_omega
    d_phi = d_potential * (1.2 * (3.0 * phi * (phi - 1.0) + 0.5)) + d_clip * inside_clip(phi)
    if n1 is not None:
        _, inv_len = sharpening(s)
        d_phi = d_phi + 1.25 * n0 + 5.0 * (
            dot(n1, vel) + SHARP * (1.0 - 2.0 * phi) * inv_len * dot(n1, s["grad"])
        )
    d_pressure = omega * m0
    keep = 1.0 - omega
    kept_part = lambda q, rest: keep * adj[q] + rest if q in adj else rest
    d_flow = {0: kept_part(0, d_pressure)}
    for q, r in PAIRS:
        lift = along(DIRS[q], d_vel)
        d_flow[q] = kept_part(q, d_pressure + lift)
        d_flow[r] = kept_part(r, d_pressure - lift)
    return d_flow, d_phi, d_grad, d_lap


def pull_along_x(s, n0, n):
    phi, grad = s["phi"], s["grad"]
    sharp, inv_len = sharpening(s)
    d_vel = 5.0 * phi * n
    d_force = s["half"] * d_vel
    d_potential = d_force * grad[0]
    sharp5 = 5.0 * sharp
    tilt = sharp5 * (grad[0] * n * inv_len * inv_len)
    d_grad = [s["potential"] * d_force + sharp5 * n - grad[0] * tilt, -grad[1] * tilt, -grad[2] * tilt]
    d_rho = -0.01 * d_force - d_force * s["force"][0] * s["inv_rho"]
    d_phi = (
        d_potential * (1.2 * (3.0 * phi * (phi - 1.0) + 0.5))
        + 0.95 * d_rho * inside_clip(phi)
        + 1.25 * n0
        + 5.0 * n * (s["vel"][0] + SHARP * (1.0 - 2.0 * phi) * inv_len * grad[0])
    )
    return d_vel, d_phi, d_grad, -0.6 * d_potential


def gradients(behind, centre, ahead):
    ahead_y, behind_y = moved(centre, 1, 0), moved(centre, -1, 0)
    ahead_z, behind_z = moved(centre, 0, 1), moved(centre, 0, -1)
    diff = lambda a, b: 0.5 * (a - b)
    lap = both(
        lambda a, b, c, d, e, f, m: a + b + c + d + e + f - 6.0 * m,
        ahead, behind, ahead_y, behind_y, ahead_z, behind_z, centre,
    )
    return both(diff, ahead, behind), both(diff, ahead_y, behind_y), both(diff, ahead_z, behind_z), lap


def behind_part(d_grad, d_lap):
    return 0.5 * d_grad + d_lap


def ahead_part(d_grad, d_lap):
    return d_lap - 0.5 * d_grad


def rim_kernel(
    g_ref, f_ref, solid_ref, cells_ref, weights_ref,
    main_ref, probes_ref, probe_weights_ref, odd_ref, even_ref, mask_ref, sems,
):
    parts = [(range(0, 7), pltpu.make_async_copy(g_ref, main_ref.at[pl.ds(0, 7)], sems.at[1]))]
    for n, (first, count) in enumerate(((0, 5), (5, 5), (10, 5), (15, 4))):
        copy = pltpu.make_async_copy(
            f_ref.at[pl.ds(first, count)], main_ref.at[pl.ds(7 + first, count)], sems.at[2 + n]
        )
        parts.append((range(7 + first, 7 + first + count), copy))
    parts.append((range(FLUID, FLUID + 1), pltpu.make_async_copy(solid_ref, mask_ref, sems.at[0])))
    later = [pltpu.make_async_copy(weights_ref, probe_weights_ref, sems.at[6])]
    for i in range(3):
        later.append(pltpu.make_async_copy(cells_ref.at[:, i, :], probes_ref.at[i], sems.at[7 + i]))
    for _, copy in parts:
        copy.start()
    for copy in later:
        copy.start()
    lane = lanes()
    odd = is_odd("vert")
    up = [[jnp.zeros((16, 128), F32)] * 4 for _ in range(2)]
    down = [[jnp.zeros((16, 128), F32)] * 4 for _ in range(2)]
    for fields, copy in parts:
        copy.wait()
        for k in fields:
            tile, slot = k // 16, k % 16
            for x in range(4):
                if k == FLUID:
                    main_ref[FLUID, x] = 1.0 - mask_ref[x].astype(F32)
                turned = roll(main_ref[k, x], 8 * slot + 8, 1)
                up[tile][x] = jnp.where(lane // RIM == slot, turned, up[tile][x])
                down[tile][x] = jnp.where(lane // RIM == (slot + 1) % 16, turned, down[tile][x])
    for tile in range(2):
        for x in range(4):
            odd_ref[tile, x] = jnp.where(odd, up[tile][x], down[tile][x])
            even_ref[tile, x] = jnp.where(odd, down[tile][x], up[tile][x])
    for copy in later:
        copy.wait()


def ring_kernel(seeds_ref, main_ref, odd_in_ref, even_in_ref, rim_ref, phase_ref, odd_ref, even_ref, rest_ref):
    del seeds_ref
    lane = lanes()
    odd = is_odd("vert")

    def row(x):
        above = [jnp.where(odd, odd_in_ref[t, x], even_in_ref[t, x]) for t in range(2)]
        below = [jnp.where(odd, even_in_ref[t, x], odd_in_ref[t, x]) for t in range(2)]
        even_group = lane // RIM % 2 == 0
        mixed = [
            (jnp.where(even_group, b, a), jnp.where(even_group, a, b)) for a, b in zip(above, below)
        ]
        sums = [None, None]
        for k in range(27):
            cells = main_ref[k, x]
            slot = k % 16
            rim = roll(mixed[k // 16][slot % 2], 120 - 8 * slot, 1)
            rim_ref[k, x] = rim
            if k < 7:
                sums = [a if b is None else a + b for a, b in zip((cells, rim), sums)]
        phase_ref[2 * x] = sums[0]
        phase_ref[2 * x + 1] = sums[1]

    for x in (3, 2, 1, 0):
        row(x)

    def cells_of(k, row):
        return (main_ref[k, row], rim_ref[k, row])

    messages = []
    for edge, inner, crossing, out in ((3, 2, TO_RIGHT, 1), (0, 1, TO_LEFT, 2)):
        pops = [cells_of(7 + q, edge) for q in range(19)]
        g = [cells_of(q, edge) for q in range(7)]
        fluid = both(lambda a: a > 0.5, cells_of(FLUID, edge))
        phi = load_pair(phase_ref, edge)
        pressure = both(lambda *p: total(p), *pops)
        omega = both(lambda p: 1.0 / (0.6 + 0.3 * jnp.clip(p, 0.0, 1.0)), phi)
        fields = [
            both(
                lambda a, b, f, o, p: jnp.where(f, (1.0 - o) * a + W[q] * (o * p), b),
                pops[q], pops[BACK[q]], fluid, omega, pressure,
            )
            for q in crossing
        ]
        turn = lambda a, b, f: jnp.where(f, -0.25 * a, b)
        fields.append(both(turn, g[out], g[BACK[out]], fluid))
        parts = [both(turn, g[0], g[0], fluid)]
        for q in range(3, 7):
            parts.append(moved(both(turn, g[q], g[BACK[q]], fluid), -DIRS[q][1], -DIRS[q][2]))
        grads = gradients(*(load_pair(phase_ref, inner + d) for d in (-1, 0, 1)))
        inner_phi = load_pair(phase_ref, inner)
        inner_pops = [cells_of(7 + q, inner) for q in range(19)]
        crossing_phase = []
        for t in range(2):
            mom = [momentum_of([p[t] for p in inner_pops], 0)] + [jnp.zeros((16, 128), F32)] * 2
            s = state_of(inner_phi[t], mom, tuple(gr[t] for gr in grads[:3]), grads[3][t])
            equil = 0.15625 * inner_phi[t] + (0.625 if out == 1 else -0.625) * carried_of(s, 0)
            crossing_phase.append(
                jnp.where(
                    cells_of(FLUID, inner)[t] > 0.5,
                    equil - 0.25 * cells_of(out, inner)[t],
                    cells_of(BACK[out], inner)[t],
                )
            )
        parts.append(tuple(crossing_phase))
        fields.append(both(lambda *p: total(p), *parts))
        fields.append(phi)
        for axis in range(3):
            fields.append(both(lambda *p: momentum_of(p, axis), *pops))
        fields.append(cells_of(FLUID, edge))
        fields.append(inner_phi)
        messages.append(fields)
    pack(odd_ref, even_ref, *messages, wide=WIDE_FIRST)
    for n in range(message_tiles(N_FIRST, WIDE_FIRST)):
        rest_ref[n] = even_ref[n]


SHIFTS = sorted({c[1:] for c in DIRS})
BF16 = jnp.bfloat16


def probe_kernel(probes_ref, weights_ref, out_ref, acc_ref, code_ref):
    first_x = lax.axis_index("tile") * 4
    first_z = lax.axis_index("vert") * 128
    acc_ref[...] = jnp.zeros_like(acc_ref)
    count = jnp.zeros((8, 128), jnp.int32)
    groups = probes_ref.shape[1] // 8
    for i in range(groups):
        at = slice(8 * i, 8 * i + 8)
        x = probes_ref[0, at, :] - (first_x - 1)
        y = probes_ref[1, at, :]
        z = probes_ref[2, at, :] - first_z
        here = (x >= 0) & (x < 6) & (z >= -RIM) & (z < 128 + RIM)
        ring = jnp.where(z >= 0, z, z + 144)
        code_ref[at, :] = jnp.where(here, (x * 16 + y) * 256 + ring, -1)
        count = count + here.astype(jnp.int32)
    passes = jnp.max(count)
    across = lax.broadcasted_iota(jnp.int32, (96, 128), 0).astype(F32).astype(BF16)
    height = lax.broadcasted_iota(jnp.int32, (144, 128), 0).astype(F32).astype(BF16)
    zero = jnp.zeros((), BF16)
    one = jnp.ones((), BF16)

    def one_pass(i, carry):
        code = jnp.full((8, 128), -1, jnp.int32)
        weight = jnp.zeros((8, 128), F32)
        for i in range(groups):
            at = slice(8 * i, 8 * i + 8)
            here = code_ref[at, :]
            take = (here >= 0) & (code < 0)
            code = jnp.where(take, here, code)
            weight = jnp.where(take, weights_ref[at, :], weight)
            code_ref[at, :] = jnp.where(take, -1, here)
        code_xy = (code >> 8).astype(F32)
        code_z = (code & 255).astype(F32)
        high = weight.astype(BF16).astype(F32)
        low = weight - high
        lhs, rhs = [], []
        for n in range(8):
            line = lambda v: v[n : n + 1, :].astype(BF16)
            hit = across == line(code_xy)
            lhs.append(
                jnp.concatenate([jnp.where(hit, line(high), zero), jnp.where(hit, line(low), zero)], axis=0)
            )
            rhs.append(jnp.where(height == line(code_z), one, zero))
        acc_ref[...] += lax.dot_general(
            jnp.concatenate(lhs, axis=1), jnp.concatenate(rhs, axis=1), (((1,), (1,)), ((), ())),
            preferred_element_type=F32,
        )
        return carry

    lax.fori_loop(0, passes, one_pass, 0)
    lane = lanes()
    for x in range(6):
        rows = pl.ds(16 * x, 16)
        lows = pl.ds(96 + 16 * x, 16)
        main = acc_ref[rows, 0:128] + acc_ref[lows, 0:128]
        rim = acc_ref[rows, 128:144] + acc_ref[lows, 128:144]
        rim = jnp.concatenate([rim, jnp.zeros((16, 112), F32)], axis=1)
        rim = jnp.where(lane < RIM, rim, jnp.where(lane >= 120, roll(rim, 112, 1), 0.0))
        for n, (cy, cz) in enumerate(SHIFTS):
            store_pair(out_ref, moved((main, rim), cy, cz), n, x)


N_FIRST = 13
WIDE_FIRST = (7,)
N_SECOND = 8
HALVES = (slice(0, 8), slice(8, 16))
SENT_ROWS = ((0, 1), (1,), (-1,), (0, -1))
M2_KEYS = ((0, 0), (0, 1), (0, 2), (1, 1), (1, 2), (2, 2))


def spot(refs, row):
    if row in (1, 2):
        return refs[0], row - 1
    return refs[1], {-1: 0, 0: 1, 3: 2, 4: 3}[row]


def prim_at(prims, row, t, h):
    ref, at = spot(prims, row)
    vals = [ref[k, 2 * at + t, h, :] for k in range(10)]
    return state_of(vals[0], vals[6:9], tuple(vals[1:4]), vals[4]), vals[5], vals[9] > 0.5


def put_gradients(prims, phase_pairs, row):
    ref, at = spot(prims, row)
    grads = gradients(*phase_pairs)
    store_pair(ref, phase_pairs[1], 0, at)
    for i in range(4):
        store_pair(ref, grads[i], 1 + i, at)


def forward(cells_ref, prims, posts, row, t):
    prim_ref, at = spot(prims, row)
    post_ref, _ = spot(posts, row)
    i = 2 * at + t
    for h in HALVES:
        g = [cells_ref[q, row, h, :] for q in range(7)]
        f = [cells_ref[7 + q, row, h, :] for q in range(19)]
        prim_ref[5, i, h, :] = total(f)
        for axis in range(3):
            prim_ref[6 + axis, i, h, :] = momentum_of(f, axis)
        prim_ref[9, i, h, :] = cells_ref[FLUID, row, h, :]
        s, pressure, fluid = prim_at(prims, row, t, h)
        for q, v in post_flow(f, fluid, pressure, s, range(19)).items():
            post_ref[7 + q, i, h, :] = v
        for q, v in post_phase(g, fluid, s, range(7)).items():
            post_ref[q, i, h, :] = v


def stream(posts, row):
    ref, at = spot(posts, row)
    for q in range(19):
        _, cy, cz = DIRS[q]
        if (cy or cz) and 0 <= row + DIRS[q][0] < 4:
            store_pair(ref, moved(load_pair(ref, 7 + q, at), -cy, -cz), 7 + q, at)


def inner_kernel(main_ref, rim_ref, phase_ref, seeds_ref, prim_ref, post_ref, moments_ref):
    prims, posts = (prim_ref, None), (post_ref, None)
    for row in (1, 2):
        put_gradients(prims, [load_pair(phase_ref, row + d) for d in (-1, 0, 1)], row)
        for t, cells_ref in enumerate((main_ref, rim_ref)):
            forward(cells_ref, prims, posts, row, t)
        stream(posts, row)

    def moments(i, carry):
        for h in HALVES:
            adj = {q: seeds_ref[SHIFTS.index(DIRS[q][1:]), i + 2 + 2 * DIRS[q][0], h, :] for q in range(19)}
            m0, m1, m2 = moments_of(adj)
            for k, v in enumerate([m0] + m1 + [m2[key] for key in M2_KEYS]):
                moments_ref[k, i, h, :] = v
        return carry

    lax.fori_loop(0, 8, moments, 0)


def middle_kernel(
    main_ref, rim_ref, phase_ref, near_in_ref, odd_in_ref, rest_in_ref, seeds_ref, moments_ref, prim_in_ref, post_in_ref,
    prim_ref, adj_ref, gamma_ref, edges_ref, odd_ref, even_ref,
    post_ref, phase_mid_ref, grad_mid_ref, back_ref, dphi_ref,
):
    prims, posts = (prim_in_ref, prim_ref), (post_in_ref, post_ref)
    from_left, from_right = received(odd_in_ref, (near_in_ref, rest_in_ref), N_FIRST, WIDE_FIRST)
    sides = ((from_left, -1, TO_RIGHT, 1), (from_right, 4, TO_LEFT, 2))
    for got, row, crossing, out in sides:
        _, at = spot(prims, row)
        for i in range(3):
            store_pair(prim_ref, got[8 + i], 6 + i, at)
        store_pair(prim_ref, got[11], 9, at)
        for q, pair in zip(crossing, got[:5]):
            store_pair(post_ref, pair, 7 + q, at)
        store_pair(post_ref, got[5], out, at)
    phases = [from_left[12], from_left[7]] + [load_pair(phase_ref, r) for r in range(4)]
    phases += [from_right[7], from_right[12]]
    for row in (-1, 0, 3, 4):
        put_gradients(prims, phases[row + 1 : row + 4], row)
    for row in (0, 3):
        for t, cells_ref in enumerate((main_ref, rim_ref)):
            forward(cells_ref, prims, posts, row, t)
        stream(posts, row)

    mid_parts = {}
    for got, row, crossing, out in sides:
        _, at = spot(posts, row)
        spread = [[], [], []]
        for t in range(2):
            i = 2 * at + t
            halves = [[], [], []]
            for h in HALVES:
                vals = [prim_ref[k, i, h, :] for k in range(10) if k != 5]
                s = state_of(vals[0], vals[5:8], tuple(vals[1:4]), vals[4])
                fluid = vals[8] > 0.5
                vel, force, omega, kappa = s["vel"], s["force"], s["omega"], s["kappa"]
                base = -1.5 * omega * dot(vel, vel) - 3.0 * kappa * dot(vel, force)
                odd_vec = tuple(3.0 * (omega * v + kappa * f) for v, f in zip(vel, force))
                even_vec = tuple(4.5 * omega * v + 9.0 * kappa * f for v, f in zip(vel, force))
                for q in crossing:
                    step = DIRS[q]
                    gain = base + along(step, vel) * along(step, even_vec) + along(step, odd_vec)
                    kept = post_ref[7 + q, i, h, :]
                    post_ref[7 + q, i, h, :] = jnp.where(fluid, kept + W[q] * gain, kept)
                sharp, _ = sharpening(s)
                carried = tuple(s["phi"] * v + sharp * gr for v, gr in zip(vel, s["grad"]))
                kept = post_ref[out, i, h, :]
                gain = 0.15625 * s["phi"] + 0.625 * along(DIRS[out], carried)
                post_ref[out, i, h, :] = jnp.where(fluid, kept + gain, kept)
                halves[0].append(jnp.where(fluid, s["phi"], 0.0))
                halves[1].append(jnp.where(fluid, carried[1], 0.0))
                halves[2].append(jnp.where(fluid, carried[2], 0.0))
            for n in range(3):
                spread[n].append(jnp.concatenate(halves[n], axis=0))
        stream(posts, row)
        phi, cy, cz = (tuple(x) for x in spread)
        gain_y = lambda sign: both(lambda p, c: 0.15625 * p + sign * 0.625 * c, phi, cy)
        gain_z = lambda sign: both(lambda p, c: 0.15625 * p + sign * 0.625 * c, phi, cz)
        mid_parts[row] = [
            got[6], both(lambda p: 0.3125 * p, phi),
            moved(gain_y(1.0), -1, 0), moved(gain_y(-1.0), 1, 0),
            moved(gain_z(1.0), 0, -1), moved(gain_z(-1.0), 0, 1),
        ]
    def post_pair(q, row):
        ref, at = spot(posts, row)
        return load_pair(ref, q, at)

    for row in range(-1, 5):
        parts = mid_parts.get(row)
        if parts is None:
            parts = [post_pair(0, row)]
            for q in range(3, 7):
                parts.append(moved(post_pair(q, row), -DIRS[q][1], -DIRS[q][2]))
        if row > -1:
            parts.append(post_pair(1, row - 1))
        if row < 4:
            parts.append(post_pair(2, row + 1))
        store_pair(phase_mid_ref, both(lambda *p: total(p), *parts), row + 1)
    for row in range(4):
        grads = gradients(*(load_pair(phase_mid_ref, row + d) for d in (0, 1, 2)))
        for i in range(4):
            store_pair(grad_mid_ref, grads[i], i, row)
    def backward(row, t, h):
        i = 2 * row + t
        f = []
        for q in range(19):
            ref, at = spot(posts, row - DIRS[q][0])
            f.append(ref[7 + q, 2 * at + t, h, :])
        adj = {q: seeds_ref[SHIFTS.index(DIRS[q][1:]), i + 2 + 2 * DIRS[q][0], h, :] for q in range(19)}
        ref, at = spot(prims, row)
        fluid = ref[9, 2 * at + t, h, :] > 0.5
        phi = phase_mid_ref[i + 2, h, :]
        mom = [momentum_of(f, axis) for axis in range(3)]
        s = state_of(phi, mom, tuple(grad_mid_ref[k, i, h, :] for k in range(3)), grad_mid_ref[3, i, h, :])
        kept = total([adj[q] * f[q] for q in range(19)])
        m = [moments_ref[k, i, h, :] for k in range(10)]
        m2 = {}
        for key, value in zip(M2_KEYS, m[4:]):
            m2[key] = m2[key[::-1]] = value
        d_flow, d_phi, d_grad, d_lap = pull_all(s, total(f), adj, kept, m[0], m[1:4], m2, None, None)
        for q in range(19):
            adj_ref[q, i, h, :] = jnp.where(fluid, d_flow[q], adj[BACK[q]])
        dphi_ref[i, h, :] = jnp.where(fluid, d_phi, 0.0)
        for k in range(3):
            back_ref[k, i, h, :] = jnp.where(fluid, d_grad[k], 0.0)
        back_ref[3, i, h, :] = jnp.where(fluid, d_lap, 0.0)

    for row in range(4):
        for t in range(2):
            for h in HALVES:
                backward(row, t, h)

    for row in range(4):
        for q in range(19):
            if DIRS[q][1:] != (0, 0) and DIRS[q][0] in SENT_ROWS[row]:
                store_pair(adj_ref, moved(load_pair(adj_ref, q, row), *DIRS[q][1:]), q, row)

    for row in range(4):
        store_pair(gamma_ref, stencil_back(back_ref, dphi_ref, row), row)
    edge_parts = []
    for row, part in ((0, ahead_part), (3, behind_part)):
        pair = both(part, load_pair(back_ref, 0, row), load_pair(back_ref, 3, row))
        store_pair(edges_ref, pair, 0 if row == 0 else 1)
        edge_parts.append(pair)

    messages = []
    for row, out_dirs, part, sign, edge_pair in (
        (3, TO_RIGHT, behind_part, -1.0, edge_parts[1]),
        (0, TO_LEFT, ahead_part, 1.0, edge_parts[0]),
    ):
        gamma = load_pair(gamma_ref, row)
        next_gamma = load_pair(gamma_ref, row - 1 if row == 3 else row + 1)
        n1 = turn_gamma(both(lambda a: sign * a, next_gamma), gamma)
        partial = []
        for t in range(2):
            s, _, fluid = prim_at(prims, row, t, slice(None))
            adj = {
                q: adj_ref[q, 2 * (row + DIRS[q][0]) + t] for q in range(19) if q not in out_dirs
            }
            m0, m1, m2 = moments_of(adj)
            d_grad, d_lap = pull_stencil(s, m0, m1, m2, [n[t] for n in n1])[:2]
            partial.append(jnp.where(fluid, part(d_grad[0], d_lap), 0.0))
        back_dirs = TO_LEFT if row == 3 else TO_RIGHT
        fields = [load_pair(adj_ref, q, row) for q in back_dirs]
        fields += [gamma, edge_pair, tuple(partial)]
        messages.append(fields)
    pack(odd_ref, even_ref, *messages)


def turn_gamma(along_x, centre):
    diff = lambda a, b: 0.125 * (a - b)
    return (
        both(lambda a: 0.125 * a, along_x),
        both(diff, moved(centre, 1, 0), moved(centre, -1, 0)),
        both(diff, moved(centre, 0, 1), moved(centre, 0, -1)),
    )


def stencil_back(back_ref, start_ref, row, first=None, last=None):
    gy, gz, lap = (load_pair(back_ref, k, row) for k in (1, 2, 3))
    fold = lambda l, gyb, gya, lyb, lya, gzb, gza, lzb, lza: (
        0.5 * (gyb - gya) + lyb + lya + 0.5 * (gzb - gza) + lzb + lza - 6.0 * l
    )
    out = both(
        fold, lap,
        moved(gy, -1, 0), moved(gy, 1, 0), moved(lap, -1, 0), moved(lap, 1, 0),
        moved(gz, 0, -1), moved(gz, 0, 1), moved(lap, 0, -1), moved(lap, 0, 1),
    )
    add = lambda a, b: a + b
    if start_ref is not None:
        out = both(add, out, load_pair(start_ref, row))
    if row > 0:
        out = both(add, out, both(behind_part, load_pair(back_ref, 0, row - 1), load_pair(back_ref, 3, row - 1)))
    elif first is not None:
        out = both(add, out, first)
    if row < 3:
        out = both(add, out, both(ahead_part, load_pair(back_ref, 0, row + 1), load_pair(back_ref, 3, row + 1)))
    elif last is not None:
        out = both(add, out, last)
    return out


def ahead_kernel(
    main_ref, prim_in_ref, prim_out_ref, adj_ref, gamma_ref,
    flow_ref, back_ref, dphi_ref,
    turned_ref, shifted_ref,
):
    prims = (prim_in_ref, prim_out_ref)
    for row in range(4):
        for q in range(19):
            if DIRS[q][1:] != (0, 0) and DIRS[q][0] not in SENT_ROWS[row]:
                store_pair(shifted_ref, moved(load_pair(adj_ref, q, row), *DIRS[q][1:]), q, row)

    def adjoint(q, row, t, h):
        step = DIRS[q]
        at = row + step[0]
        ref = adj_ref if step[1:] == (0, 0) or step[0] in SENT_ROWS[at] else shifted_ref
        return ref[q, 2 * at + t, h, :]

    for row in (1, 2):
        centre = load_pair(gamma_ref, row)
        for n, (cy, cz) in enumerate(((1, 0), (-1, 0), (0, 1), (0, -1))):
            store_pair(turned_ref, moved(centre, cy, cz), n, row - 1)
    for row in range(4):
        for t in range(2):
            for h in HALVES:
                i = 2 * row + t
                s, pressure, fluid = prim_at(prims, row, t, h)
                adj = {q: adjoint(q, row, t, h) for q in range(19) if 0 <= row + DIRS[q][0] < 4}
                m0, m1, m2 = moments_of(adj)
                n0 = n1 = None
                if row in (1, 2):
                    g = [gamma_ref[i + 2, h, :], gamma_ref[i - 2, h, :]]
                    g += [turned_ref[n, i - 2, h, :] for n in range(4)]
                    n1 = [0.125 * (g[a] - g[a + 1]) for a in (0, 2, 4)]
                if t == 1:
                    d_grad, d_lap = pull_stencil(s, m0, m1, m2, n1)[:2]
                else:
                    if row in (1, 2):
                        n0 = 0.25 * gamma_ref[i, h, :] + 0.125 * total(g)
                    kept = total([a * main_ref[7 + q, row, h, :] for q, a in adj.items()])
                    d_flow, d_phi, d_grad, d_lap = pull_all(s, pressure, adj, kept, m0, m1, m2, n0, n1)
                    for q in range(19):
                        flow_ref[q, row, h, :] = jnp.where(fluid, d_flow[q], adj.get(BACK[q], 0.0))
                    dphi_ref[row, h, :] = jnp.where(fluid, d_phi, 0.0)
                for k in range(3):
                    back_ref[k, i, h, :] = jnp.where(fluid, d_grad[k], 0.0)
                back_ref[3, i, h, :] = jnp.where(fluid, d_lap, 0.0)


def last_kernel(
    main_ref, prim_in_ref, prim_out_ref, adj_ref, gamma_ref, edges_ref, flow_ref, back_in_ref, dphi_in_ref,
    even_in_ref, odd_in_ref,
    out_g_ref, out_f_ref,
    gamma_wide_ref, turned_ref, back_ref, dphi_ref, g_ref, f_ref, sems,
):
    add = lambda a, b: a + b
    prims = (prim_in_ref, prim_out_ref)
    copies = []

    def send(src, dst):
        copies.append(pltpu.make_async_copy(src, dst, sems.at[len(copies)]))
        copies[-1].start()

    got_left, got_right = received(odd_in_ref, (even_in_ref,), N_SECOND)
    own_first = load_pair(edges_ref, 0)
    own_last = load_pair(edges_ref, 1)

    for row, more, sign in ((1, got_left[6], -0.125), (2, got_right[6], 0.125)):
        for t in range(2):
            for n, h in enumerate(HALVES):
                i = 2 * row + t
                s, _, fluid = prim_at(prims, row, t, h)
                delta = more[t][8 * n : 8 * n + 8]
                d_vel, d_phi, d_grad, d_lap = pull_along_x(s, 0.125 * delta, sign * delta)
                if t == 0:
                    lift = jnp.where(fluid, d_vel, 0.0)
                    for q in range(19):
                        base = flow_ref[q, row, h, :]
                        f_ref[q, row, h, :] = base + DIRS[q][0] * lift if DIRS[q][0] else base
                    dphi_ref[row, h, :] = dphi_in_ref[row, h, :] + jnp.where(fluid, d_phi, 0.0)
                for k in range(3):
                    back_ref[k, i, h, :] = back_in_ref[k, i, h, :] + jnp.where(fluid, d_grad[k], 0.0)
                back_ref[3, i, h, :] = back_in_ref[3, i, h, :] + jnp.where(fluid, d_lap, 0.0)
    send(f_ref.at[:, pl.ds(1, 2)], out_f_ref.at[:, pl.ds(1, 2)])

    for row in (1, 2):
        store_pair(gamma_wide_ref, load_pair(gamma_ref, row), row + 1)
    store_pair(gamma_wide_ref, both(add, load_pair(gamma_ref, 0), got_left[6]), 1)
    store_pair(gamma_wide_ref, both(add, load_pair(gamma_ref, 3), got_right[6]), 4)
    store_pair(gamma_wide_ref, both(add, got_left[5], own_first), 0)
    store_pair(gamma_wide_ref, both(add, got_right[5], own_last), 5)
    for row in range(4):
        centre = load_pair(gamma_wide_ref, row + 1)
        for n, (cy, cz) in enumerate(((1, 0), (-1, 0), (0, 1), (0, -1))):
            store_pair(turned_ref, moved(centre, cy, cz), n, row)

    def phase_adjoints(i, h):
        at = [gamma_wide_ref[i + 2, h, :], gamma_wide_ref[i + 4, h, :], gamma_wide_ref[i, h, :]]
        return at + [turned_ref[n, i, h, :] for n in range(4)]

    for row, got, dirs in ((0, got_left, TO_LEFT), (3, got_right, TO_RIGHT)):
        for t in range(2):
            for n, h in enumerate(HALVES):
                i = 2 * row + t
                s, pressure, fluid = prim_at(prims, row, t, h)
                adj = {q: pair[t][8 * n : 8 * n + 8] for q, pair in zip(dirs, got[:5])}
                g = phase_adjoints(i, h)
                n1 = [0.125 * (g[a] - g[a + 1]) for a in (1, 3, 5)]
                m0, m1, m2 = moments_of(adj)
                if t == 1:
                    d_grad, d_lap = pull_stencil(s, m0, m1, m2, n1)[:2]
                else:
                    n0 = 0.25 * g[0] + 0.125 * total(g[1:])
                    kept = total([a * main_ref[7 + q, row, h, :] for q, a in adj.items()])
                    d_flow, d_phi, d_grad, d_lap = pull_all(s, pressure, adj, kept, m0, m1, m2, n0, n1)
                    for q in range(19):
                        more = jnp.where(fluid, d_flow[q], adj.get(BACK[q], 0.0))
                        f_ref[q, row, h, :] = flow_ref[q, row, h, :] + more
                    dphi_ref[row, h, :] = dphi_in_ref[row, h, :] + jnp.where(fluid, d_phi, 0.0)
                for k in range(3):
                    back_ref[k, i, h, :] = back_in_ref[k, i, h, :] + jnp.where(fluid, d_grad[k], 0.0)
                back_ref[3, i, h, :] = back_in_ref[3, i, h, :] + jnp.where(fluid, d_lap, 0.0)
        send(f_ref.at[:, pl.ds(row, 1)], out_f_ref.at[:, pl.ds(row, 1)])

    edge_parts = []
    for got, prim_row, row, own, out_dirs, part, sign in (
        (got_left, -1, 0, own_first, TO_RIGHT, behind_part, 1.0),
        (got_right, 4, 3, own_last, TO_LEFT, ahead_part, -1.0),
    ):
        gamma = load_pair(gamma_wide_ref, row + 1)
        n1 = turn_gamma(both(lambda a: sign * a, gamma), own)
        pair = []
        for t in range(2):
            s, _, fluid = prim_at(prims, prim_row, t, slice(None))
            adj = {q: adj_ref[q, 2 * row + t] for q in out_dirs}
            m0, m1, m2 = moments_of(adj)
            d_grad, d_lap = pull_stencil(s, m0, m1, m2, [n[t] for n in n1])[:2]
            pair.append(got[7][t] + jnp.where(fluid, part(d_grad[0], d_lap), 0.0))
        edge_parts.append(tuple(pair))

    for row in range(4):
        rest = stencil_back(back_ref, None, row, edge_parts[0], edge_parts[1])[0]
        ref, at = spot(prims, row)
        fluid = ref[9, 2 * at] > 0.5
        base = rest + dphi_ref[row]
        phase_adj = phase_adjoints(2 * row, slice(None))
        for q in range(7):
            g_ref[q, row] = jnp.where(fluid, base - 0.25 * phase_adj[q], rest + phase_adj[BACK[q]])
        send(g_ref.at[:, pl.ds(row, 1)], out_g_ref.at[:, pl.ds(row, 1)])
    for copy in copies:
        copy.wait()


def call(kernel, outs, n_in, scratch=(), flops=0, name=None, any_in=0, any_out=False):
    vmem = pl.BlockSpec(memory_space=pltpu.VMEM)
    return pl.pallas_call(
        kernel,
        out_shape=[jax.ShapeDtypeStruct(x, F32) if isinstance(x, tuple) else x for x in outs],
        in_specs=[pl.BlockSpec(memory_space=pl.ANY)] * any_in + [vmem] * (n_in - any_in),
        out_specs=[pl.BlockSpec(memory_space=pl.ANY) if any_out else vmem] * len(outs),
        scratch_shapes=[pltpu.VMEM(x, F32) if isinstance(x, tuple) else x for x in scratch],
        compiler_params=pltpu.CompilerParams(vmem_limit_bytes=VMEM_LIMIT),
        cost_estimate=pl.CostEstimate(flops=flops, bytes_accessed=flops // 8, transcendentals=0),
        name=name,
    )


def swap(x, axis, first, wanted=lambda i: True):
    pairs = []
    for i in range(first, lax.axis_size(axis) - 1, 2):
        if wanted(i):
            pairs += [(i, i + 1), (i + 1, i)]
    return lax.ppermute(x, axis, pairs)


LINE = 8


def before_long(i):
    return i % LINE == LINE - 2


def shards(phase_init, flow_init, solid_mask, sensor_cells, sensor_weights):
    tile = (16, 128)
    cells = sensor_cells.reshape(3, -1, 128).transpose(1, 0, 2)
    weights = sensor_weights.reshape(-1, 128)
    main, probes, weights, odd, even = call(
        rim_kernel,
        [(27, 4) + tile, jax.ShapeDtypeStruct((3,) + weights.shape, jnp.int32), weights.shape] + [(2, 4) + tile] * 2,
        5, any_in=5, flops=10**6, name="rim",
        scratch=[pltpu.VMEM((4,) + tile, jnp.int32), pltpu.SemaphoreType.DMA((10,))],
    )(*(pltpu.with_memory_space_constraint(x, pltpu.HBM) for x in (phase_init, flow_init, solid_mask, cells, weights)))
    odd, even = swap(odd, "vert", 1), swap(even, "vert", 0)
    (seeds,) = call(probe_kernel, [(9, 12) + tile], 2, scratch=[(192, 144), pltpu.VMEM(weights.shape, jnp.int32)], flops=2 * 10**9, name="probes")(
        probes, weights
    )
    first = message_tiles(N_FIRST, WIDE_FIRST)
    rim, phase, odd, even, rest = call(
        ring_kernel, [(27, 4) + tile, (8,) + tile] + [(first,) + tile] * 3, 4, any_in=1, flops=10**7, name="ring"
    )(seeds, main, odd, even)
    near = swap(even, "tile", 0, lambda i: not before_long(i))
    odd = swap(odd, "tile", 1)
    rest = swap(rest, "tile", 0, before_long)
    prim_in, post_in, moments = call(
        inner_kernel, [(10, 4) + tile, (26, 4) + tile, (10, 8) + tile], 4, flops=2 * 10**8, name="inner"
    )(main, rim, phase, seeds)
    second = message_tiles(N_SECOND)
    prim_out, adj, gamma, edges, odd, even = call(
        middle_kernel,
        [(10, 8) + tile, (19, 8) + tile, (8,) + tile, (4,) + tile] + [(second,) + tile] * 2,
        10,
        scratch=[(26, 8) + tile, (12,) + tile, (4, 8) + tile, (4, 8) + tile, (8,) + tile],
        flops=10**8, name="middle",
    )(main, rim, phase, near, odd, rest, seeds, moments, prim_in, post_in)
    even = swap(even, "tile", 0)
    odd = swap(odd, "tile", 1)
    flow, back, dphi = call(
        ahead_kernel, [(19, 4) + tile, (4, 8) + tile, (4,) + tile], 5, scratch=[(4, 4) + tile, (19, 8) + tile],
        flops=2 * 10**8, name="ahead",
    )(main, prim_in, prim_out, adj, gamma)
    return tuple(
        call(
            last_kernel,
            [(7, 4) + tile, (19, 4) + tile],
            11,
            scratch=[
                (12,) + tile, (4, 8) + tile, (4, 8) + tile, (4,) + tile, (7, 4) + tile, (19, 4) + tile,
                pltpu.SemaphoreType.DMA((7,)),
            ],
            flops=10**8, name="last", any_out=True,
        )(main, prim_in, prim_out, adj, gamma, edges, flow, back, dphi, even, odd)
    )


def solution(mesh):
    return jax.shard_map(
        shards,
        mesh=mesh,
        in_specs=(
            P(None, "tile", None, "vert"),
            P(None, "tile", None, "vert"),
            P("tile", None, "vert"),
            P(),
            P(),
        ),
        out_specs=(P(None, "tile", None, "vert"), P(None, "tile", None, "vert")),
        check_vma=False,
    )
```

```python
import functools

import jax
import jax.numpy as jnp
import numpy as np
from jax import lax
from jax.experimental import pallas as pl
from jax.experimental.pallas import tpu as pltpu
from jax.sharding import PartitionSpec as P

DIRS = [
    (0, 0, 0), (1, 0, 0), (-1, 0, 0), (0, 1, 0), (0, -1, 0), (0, 0, 1), (0, 0, -1),
    (1, 1, 0), (-1, -1, 0), (1, -1, 0), (-1, 1, 0), (1, 0, 1), (-1, 0, -1), (1, 0, -1),
    (-1, 0, 1), (0, 1, 1), (0, -1, -1), (0, 1, -1), (0, -1, 1),
]
BACK = [0, 2, 1, 4, 3, 6, 5, 8, 7, 10, 9, 12, 11, 14, 13, 16, 15, 18, 17]
W = [1.0 / 3.0] + [1.0 / 18.0] * 6 + [1.0 / 36.0] * 12
W0, W1, W2 = 1.0 / 3.0, 1.0 / 18.0, 1.0 / 36.0
PAIRS = [(q, q + 1) for q in range(1, 19, 2)]
TO_RIGHT = [q for q in range(19) if DIRS[q][0] == 1]
TO_LEFT = [q for q in range(19) if DIRS[q][0] == -1]
RIM = 8
SHARP = 0.075
FLUID = 26
F32 = jnp.float32
VMEM_LIMIT = 40 * 2**20


def lanes():
    return lax.broadcasted_iota(jnp.int32, (16, 128), 1)


def roll(x, shift, axis):
    shift = shift % x.shape[axis]
    return x if shift == 0 else pltpu.roll(x, shift, axis)


def load_pair(ref, *at):
    *head, row = at
    return (ref[(*head, 2 * row)], ref[(*head, 2 * row + 1)])


def store_pair(ref, pair, *at):
    *head, row = at
    ref[(*head, 2 * row)] = pair[0]
    ref[(*head, 2 * row + 1)] = pair[1]


def both(fn, *pairs):
    return tuple(fn(*each) for each in zip(*pairs))


def moved(pair, step_y, step_z):
    if step_y:
        pair = both(lambda t: roll(t, -step_y, 0), pair)
    if step_z:
        a = roll(pair[0], -step_z, 1)
        b = roll(pair[1], -step_z, 1)
        edge = lanes() == (127 if step_z > 0 else 0)
        pair = (jnp.where(edge, b, a), jnp.where(edge, a, b))
    return pair


def is_odd(axis):
    return jnp.full((16, 128), lax.rem(lax.axis_index(axis), 2), jnp.int32) == 1


def rim_slots(count, wide):
    slots, at = [], 0
    for k in range(count):
        width = 8 if k in wide else 4
        if at % 128 + 2 * width > 128:
            at += 128 - at % 128
        slots.append((at // 128, at % 128, width))
        at += 2 * width
    return slots


def message_tiles(count, wide=()):
    return count + rim_slots(count, wide)[-1][0] + 1


def packed(fields, wide):
    lane = lanes()
    out = [main for main, _ in fields]
    slots = rim_slots(len(fields), wide)
    for tile in range(slots[-1][0] + 1):
        acc = jnp.zeros((16, 128), F32)
        for (at, first, width), (_, rim) in zip(slots, fields):
            if at == tile:
                mine = (lane >= first) & (lane < first + 2 * width)
                acc = jnp.where(mine, roll(rim, first + width, 1), acc)
        out.append(acc)
    return out


def pack(odd_ref, even_ref, right, left, wide=()):
    odd = is_odd("tile")
    for n, (r, l) in enumerate(zip(packed(right, wide), packed(left, wide))):
        odd_ref[n] = jnp.where(odd, r, l)
        even_ref[n] = jnp.where(odd, l, r)


def received(odd_ref, even_ref, count, wide=()):
    odd = is_odd("tile")
    slots = rim_slots(count, wide)
    tiles = message_tiles(count, wide)
    got_odd = [odd_ref[n] for n in range(tiles)]
    got_even = [even_ref[n] for n in range(tiles)]
    sides = []
    for one, two in ((got_even, got_odd), (got_odd, got_even)):
        msg = [jnp.where(odd, a, b) for a, b in zip(one, two)]
        sides.append(
            [(msg[k], roll(msg[count + at], -(first + width), 1)) for k, (at, first, width) in enumerate(slots)]
        )
    return sides


def total(values):
    out = values[0]
    for value in values[1:]:
        out = out + value
    return out


def along(step, vec):
    out = None
    for c, v in zip(step, vec):
        if c == 0:
            continue
        if out is None:
            out = v if c > 0 else -v
        else:
            out = out + v if c > 0 else out - v
    return out


def momentum_of(pops, axis):
    plus = [pops[q] for q in range(19) if DIRS[q][axis] == 1]
    minus = [pops[q] for q in range(19) if DIRS[q][axis] == -1]
    return total([a - b for a, b in zip(plus, minus)])


def state_of(phi, mom, grad, lap):
    clipped = jnp.clip(phi, 0.0, 1.0)
    rho = 0.05 + 0.95 * clipped
    omega = 1.0 / (0.6 + 0.3 * clipped)
    inv_rho = 1.0 / rho
    potential = 1.2 * phi * (phi - 1.0) * (phi - 0.5) - 0.6 * lap
    force = (
        potential * grad[0] - 0.01 * rho,
        potential * grad[1],
        potential * grad[2] - 0.02 * (rho - 0.05),
    )
    half = 0.5 * inv_rho
    vel = tuple(m + f * half for m, f in zip(mom, force))
    kappa = (1.0 - 0.5 * omega) * inv_rho
    return dict(
        phi=phi, grad=grad, omega=omega, inv_rho=inv_rho, potential=potential, force=force,
        half=half, vel=vel, kappa=kappa,
    )


def dot(a, b):
    return a[0] * b[0] + a[1] * b[1] + a[2] * b[2]


def sharpening(s):
    inv_len = lax.rsqrt(dot(s["grad"], s["grad"]) + 0.01)
    return SHARP * s["phi"] * (1.0 - s["phi"]) * inv_len, inv_len


def carried_of(s, axis):
    sharp, _ = sharpening(s)
    return s["phi"] * s["vel"][axis] + sharp * s["grad"][axis]


def post_flow(pops, fluid, pressure, s, wanted):
    vel, force, omega, kappa = s["vel"], s["force"], s["omega"], s["kappa"]
    base = omega * (pressure - 1.5 * dot(vel, vel)) - 3.0 * kappa * dot(vel, force)
    odd_vec = tuple(3.0 * (omega * v + kappa * f) for v, f in zip(vel, force))
    even_vec = tuple(4.5 * omega * v + 9.0 * kappa * f for v, f in zip(vel, force))
    keep = 1.0 - omega
    out = {}
    if 0 in wanted:
        out[0] = jnp.where(fluid, keep * pops[0] + W0 * base, pops[0])
    for q, r in PAIRS:
        if q not in wanted and r not in wanted:
            continue
        step = DIRS[q]
        even = base + along(step, vel) * along(step, even_vec)
        odd = along(step, odd_vec)
        if q in wanted:
            out[q] = jnp.where(fluid, keep * pops[q] + W[q] * (even + odd), pops[r])
        if r in wanted:
            out[r] = jnp.where(fluid, keep * pops[r] + W[q] * (even - odd), pops[q])
    return out


def post_phase(pops, fluid, s, wanted):
    sharp, _ = sharpening(s)
    carried = tuple(s["phi"] * v + sharp * g for v, g in zip(s["vel"], s["grad"]))
    out = {}
    for q in wanted:
        if q == 0:
            out[q] = jnp.where(fluid, 0.3125 * s["phi"] - 0.25 * pops[0], pops[0])
        else:
            equil = 0.15625 * s["phi"] + 0.625 * along(DIRS[q], carried)
            out[q] = jnp.where(fluid, equil - 0.25 * pops[q], pops[BACK[q]])
    return out


def moments_of(adj):
    zero = None
    m0, m1 = [], [[], [], []]
    m2 = {}
    if 0 in adj:
        m0.append(W0 * adj[0])
    groups = {W1: [], W2: []}
    for q in range(1, 19):
        if q not in adj:
            continue
        a = adj[q]
        w = W[q]
        groups[w].append(a)
    for w, items in groups.items():
        if items:
            m0.append(w * total(items))

    def weighted(terms):
        parts = []
        for w in (W1, W2):
            mine = [(sign, a) for ww, sign, a in terms if ww == w]
            if not mine:
                continue
            acc = None
            for sign, a in mine:
                if acc is None:
                    acc = a if sign > 0 else -a
                else:
                    acc = acc + a if sign > 0 else acc - a
            parts.append(w * acc)
        return total(parts) if parts else None

    for i in range(3):
        m1[i] = weighted([(W[q], DIRS[q][i], adj[q]) for q in range(1, 19) if q in adj and DIRS[q][i]])
    for i in range(3):
        for j in range(i, 3):
            m2[(i, j)] = weighted(
                [
                    (W[q], DIRS[q][i] * DIRS[q][j], adj[q])
                    for q in range(1, 19)
                    if q in adj and DIRS[q][i] and DIRS[q][j]
                ]
            )
            m2[(j, i)] = m2[(i, j)]
    return total(m0), m1, m2


def apply_m2(m2, vec):
    out = []
    for i in range(3):
        terms = [m2[(i, j)] * vec[j] for j in range(3) if m2[(i, j)] is not None]
        out.append(total(terms))
    return out


def pull_stencil(s, m0, m1, m2, n1):
    vel, force = s["vel"], s["force"]
    omega, kappa, half = s["omega"], s["kappa"], s["half"]
    m2v = apply_m2(m2, vel)
    m2f = apply_m2(m2, force)
    m0_3 = 3.0 * m0
    lean = []
    for i in range(3):
        term = 9.0 * m2v[i] - m0_3 * vel[i]
        lean.append(term if m1[i] is None else term + 3.0 * m1[i])
    push = [9.0 * m2f[i] - m0_3 * force[i] for i in range(3)]
    d_vel = [omega * a + kappa * b for a, b in zip(lean, push)]
    if n1 is not None:
        five_phi = 5.0 * s["phi"]
        d_vel = [d + five_phi * n for d, n in zip(d_vel, n1)]
    d_force = [kappa * a + half * d for a, d in zip(lean, d_vel)]
    d_potential = dot(d_force, s["grad"])
    d_grad = [s["potential"] * x for x in d_force]
    if n1 is not None:
        sharp, inv_len = sharpening(s)
        tilt = dot(s["grad"], n1) * inv_len * inv_len
        sharp5 = 5.0 * sharp
        d_grad = [d + sharp5 * (n - g * tilt) for d, n, g in zip(d_grad, n1, s["grad"])]
    d_lap = -0.6 * d_potential
    return d_grad, d_lap, d_potential, d_force, d_vel, m2v, m2f


def inside_clip(phi):
    return jnp.where((phi > 0.0) & (phi < 1.0), 1.0, jnp.where((phi == 0.0) | (phi == 1.0), 0.5, 0.0))


def pull_all(s, pressure, adj, kept, m0, m1, m2, n0, n1):
    d_grad, d_lap, d_potential, d_force, d_vel, m2v, m2f = pull_stencil(s, m0, m1, m2, n1)
    phi, vel, force = s["phi"], s["vel"], s["force"]
    omega, kappa, inv_rho, half = s["omega"], s["kappa"], s["inv_rho"], s["half"]
    relaxed = m0 * (pressure - 1.5 * dot(vel, vel)) + 3.0 * dot(m1, vel) + 4.5 * dot(m2v, vel)
    forced = 3.0 * dot(m1, force) - 3.0 * m0 * dot(vel, force) + 9.0 * dot(m2v, force)
    d_omega = relaxed - kept - 0.5 * inv_rho * forced
    d_rho = (
        -kappa * inv_rho * forced
        - 0.01 * d_force[0]
        - 0.02 * d_force[2]
        - dot(d_vel, force) * half * inv_rho
    )
    d_clip = 0.95 * d_rho - 0.3 * omega * omega * d_omega
    d_phi = d_potential * (1.2 * (3.0 * phi * (phi - 1.0) + 0.5)) + d_clip * inside_clip(phi)
    if n1 is not None:
        _, inv_len = sharpening(s)
        d_phi = d_phi + 1.25 * n0 + 5.0 * (
            dot(n1, vel) + SHARP * (1.0 - 2.0 * phi) * inv_len * dot(n1, s["grad"])
        )
    d_pressure = omega * m0
    keep = 1.0 - omega
    kept_part = lambda q, rest: keep * adj[q] + rest if q in adj else rest
    d_flow = {0: kept_part(0, d_pressure)}
    for q, r in PAIRS:
        lift = along(DIRS[q], d_vel)
        d_flow[q] = kept_part(q, d_pressure + lift)
        d_flow[r] = kept_part(r, d_pressure - lift)
    return d_flow, d_phi, d_grad, d_lap


def pull_along_x(s, n0, n):
    phi, grad = s["phi"], s["grad"]
    sharp, inv_len = sharpening(s)
    d_vel = 5.0 * phi * n
    d_force = s["half"] * d_vel
    d_potential = d_force * grad[0]
    sharp5 = 5.0 * sharp
    tilt = sharp5 * (grad[0] * n * inv_len * inv_len)
    d_grad = [s["potential"] * d_force + sharp5 * n - grad[0] * tilt, -grad[1] * tilt, -grad[2] * tilt]
    d_rho = -0.01 * d_force - d_force * s["force"][0] * s["inv_rho"]
    d_phi = (
        d_potential * (1.2 * (3.0 * phi * (phi - 1.0) + 0.5))
        + 0.95 * d_rho * inside_clip(phi)
        + 1.25 * n0
        + 5.0 * n * (s["vel"][0] + SHARP * (1.0 - 2.0 * phi) * inv_len * grad[0])
    )
    return d_vel, d_phi, d_grad, -0.6 * d_potential


def gradients(behind, centre, ahead):
    ahead_y, behind_y = moved(centre, 1, 0), moved(centre, -1, 0)
    ahead_z, behind_z = moved(centre, 0, 1), moved(centre, 0, -1)
    diff = lambda a, b: 0.5 * (a - b)
    lap = both(
        lambda a, b, c, d, e, f, m: a + b + c + d + e + f - 6.0 * m,
        ahead, behind, ahead_y, behind_y, ahead_z, behind_z, centre,
    )
    return both(diff, ahead, behind), both(diff, ahead_y, behind_y), both(diff, ahead_z, behind_z), lap


def behind_part(d_grad, d_lap):
    return 0.5 * d_grad + d_lap


def ahead_part(d_grad, d_lap):
    return d_lap - 0.5 * d_grad


NEAR = 5
OWN_TILE = 24


def rim_place(k, x):
    return (x, NEAR * k) if k < OWN_TILE else (4, 30 * x + NEAR * (k - OWN_TILE))


def rim_kernel(
    g_ref, f_ref, solid_ref, cells_ref, weights_ref,
    main_ref, probes_ref, probe_weights_ref, odd_ref, even_ref, mask_ref, sems,
):
    parts = [(range(0, 7), pltpu.make_async_copy(g_ref, main_ref.at[pl.ds(0, 7)], sems.at[1]))]
    for n, (first, count) in enumerate(((0, 5), (5, 5), (10, 5), (15, 4))):
        copy = pltpu.make_async_copy(
            f_ref.at[pl.ds(first, count)], main_ref.at[pl.ds(7 + first, count)], sems.at[2 + n]
        )
        parts.append((range(7 + first, 7 + first + count), copy))
    parts.append((range(FLUID, FLUID + 1), pltpu.make_async_copy(solid_ref, mask_ref, sems.at[0])))
    later = [pltpu.make_async_copy(weights_ref, probe_weights_ref, sems.at[6])]
    for i in range(3):
        later.append(pltpu.make_async_copy(cells_ref.at[:, i, :], probes_ref.at[i], sems.at[7 + i]))
    for _, copy in parts:
        copy.start()
    for copy in later:
        copy.start()
    lane = lanes()
    odd = is_odd("vert")
    up = [jnp.zeros((16, 128), F32)] * 5
    down = [jnp.zeros((16, 128), F32)] * 5
    phase = [None] * 4

    def put(cells, width, tile, first):
        turned = roll(cells, first + width, 1)
        up[tile] = jnp.where((lane >= first) & (lane < first + width), turned, up[tile])
        down[tile] = jnp.where((lane >= first + width) & (lane < first + 2 * width), turned, down[tile])

    for fields, copy in parts:
        copy.wait()
        for k in fields:
            for x in range(4):
                if k == FLUID:
                    main_ref[FLUID, x] = 1.0 - mask_ref[x].astype(F32)
                cells = main_ref[k, x]
                put(cells, NEAR, *rim_place(k, x))
                if k < 7:
                    phase[x] = cells if k == 0 else phase[x] + cells
    for x in range(4):
        tile, first = rim_place(FLUID + 2, x)
        up[tile] = jnp.where(lane == first, roll(phase[x], first - (127 - NEAR), 1), up[tile])
        down[tile] = jnp.where(lane == first, roll(phase[x], first - NEAR, 1), down[tile])
    for tile in range(5):
        odd_ref[tile] = jnp.where(odd, up[tile], down[tile])
        even_ref[tile] = jnp.where(odd, down[tile], up[tile])
    for copy in later:
        copy.wait()


def ring_kernel(main_ref, odd_in_ref, even_in_ref, rim_ref, phase_ref, odd_ref, even_ref):
    lane = lanes()
    odd = is_odd("vert")

    def row(x):
        mixed = []
        for tile in (x, 4):
            above = jnp.where(odd, odd_in_ref[tile], even_in_ref[tile])
            below = jnp.where(odd, even_in_ref[tile], odd_in_ref[tile])
            even_group = lane // NEAR % 2 == 0
            mixed.append((jnp.where(even_group, below, above), jnp.where(even_group, above, below)))
        sums = [None, None]
        for k in range(27):
            cells = main_ref[k, x]
            tile, first = rim_place(k, x)
            rim = roll(mixed[tile == 4][first // NEAR % 2], 128 - NEAR - first, 1)
            rim_ref[k, x] = rim
            if k < 7:
                sums = [a if b is None else a + b for a, b in zip((cells, rim), sums)]
        _, first = rim_place(FLUID + 2, x)
        sums[1] = jnp.where(lane == NEAR, roll(above, NEAR - first, 1), sums[1])
        sums[1] = jnp.where(lane == 127 - NEAR, roll(below, 127 - NEAR - first, 1), sums[1])
        phase_ref[2 * x] = sums[0]
        phase_ref[2 * x + 1] = sums[1]

    for x in (3, 2, 1, 0):
        row(x)

    def cells_of(k, row):
        return (main_ref[k, row], rim_ref[k, row])

    messages = []
    for edge, inner, crossing, out in ((3, 2, TO_RIGHT, 1), (0, 1, TO_LEFT, 2)):
        pops = [cells_of(7 + q, edge) for q in range(19)]
        g = [cells_of(q, edge) for q in range(7)]
        fluid = both(lambda a: a > 0.5, cells_of(FLUID, edge))
        phi = load_pair(phase_ref, edge)
        pressure = both(lambda *p: total(p), *pops)
        omega = both(lambda p: 1.0 / (0.6 + 0.3 * jnp.clip(p, 0.0, 1.0)), phi)
        fields = [
            both(
                lambda a, b, f, o, p: jnp.where(f, (1.0 - o) * a + W[q] * (o * p), b),
                pops[q], pops[BACK[q]], fluid, omega, pressure,
            )
            for q in crossing
        ]
        turn = lambda a, b, f: jnp.where(f, -0.25 * a, b)
        fields.append(both(turn, g[out], g[BACK[out]], fluid))
        parts = [both(turn, g[0], g[0], fluid)]
        for q in range(3, 7):
            parts.append(moved(both(turn, g[q], g[BACK[q]], fluid), -DIRS[q][1], -DIRS[q][2]))
        grads = gradients(*(load_pair(phase_ref, inner + d) for d in (-1, 0, 1)))
        inner_phi = load_pair(phase_ref, inner)
        inner_pops = [cells_of(7 + q, inner) for q in range(19)]
        crossing_phase = []
        for t in range(2):
            mom = [momentum_of([p[t] for p in inner_pops], 0)] + [jnp.zeros((16, 128), F32)] * 2
            s = state_of(inner_phi[t], mom, tuple(gr[t] for gr in grads[:3]), grads[3][t])
            equil = 0.15625 * inner_phi[t] + (0.625 if out == 1 else -0.625) * carried_of(s, 0)
            crossing_phase.append(
                jnp.where(
                    cells_of(FLUID, inner)[t] > 0.5,
                    equil - 0.25 * cells_of(out, inner)[t],
                    cells_of(BACK[out], inner)[t],
                )
            )
        parts.append(tuple(crossing_phase))
        fields.append(both(lambda *p: total(p), *parts))
        fields.append(phi)
        for axis in range(3):
            fields.append(both(lambda *p: momentum_of(p, axis), *pops))
        fields.append(cells_of(FLUID, edge))
        fields.append(inner_phi)
        messages.append(fields)
    pack(odd_ref, even_ref, *messages, wide=WIDE_FIRST)


SHIFTS = sorted({c[1:] for c in DIRS})
BF16 = jnp.bfloat16


def probe_kernel(probes_ref, weights_ref, out_ref, acc_ref, code_ref):
    first_x = lax.axis_index("tile") * 4
    first_z = lax.axis_index("vert") * 128
    acc_ref[...] = jnp.zeros_like(acc_ref)
    count = jnp.zeros((8, 128), jnp.int32)
    groups = probes_ref.shape[1] // 8
    for i in range(groups):
        at = slice(8 * i, 8 * i + 8)
        x = probes_ref[0, at, :] - (first_x - 1)
        y = probes_ref[1, at, :]
        z = probes_ref[2, at, :] - first_z
        here = (x >= 0) & (x < 6) & (z >= -RIM) & (z < 128 + RIM)
        ring = jnp.where(z >= 0, z, z + 144)
        code_ref[at, :] = jnp.where(here, (x * 16 + y) * 256 + ring, -1)
        count = count + here.astype(jnp.int32)
    passes = jnp.max(count)
    across = lax.broadcasted_iota(jnp.int32, (96, 128), 0).astype(F32).astype(BF16)
    height = lax.broadcasted_iota(jnp.int32, (144, 128), 0).astype(F32).astype(BF16)
    zero = jnp.zeros((), BF16)
    one = jnp.ones((), BF16)

    def one_pass(i, carry):
        code = jnp.full((8, 128), -1, jnp.int32)
        weight = jnp.zeros((8, 128), F32)
        for i in range(groups):
            at = slice(8 * i, 8 * i + 8)
            here = code_ref[at, :]
            take = (here >= 0) & (code < 0)
            code = jnp.where(take, here, code)
            weight = jnp.where(take, weights_ref[at, :], weight)
            code_ref[at, :] = jnp.where(take, -1, here)
        code_xy = (code >> 8).astype(F32)
        code_z = (code & 255).astype(F32)
        high = weight.astype(BF16).astype(F32)
        low = weight - high
        lhs, rhs = [], []
        for n in range(8):
            line = lambda v: v[n : n + 1, :].astype(BF16)
            hit = across == line(code_xy)
            lhs.append(
                jnp.concatenate([jnp.where(hit, line(high), zero), jnp.where(hit, line(low), zero)], axis=0)
            )
            rhs.append(jnp.where(height == line(code_z), one, zero))
        acc_ref[...] += lax.dot_general(
            jnp.concatenate(lhs, axis=1), jnp.concatenate(rhs, axis=1), (((1,), (1,)), ((), ())),
            preferred_element_type=F32,
        )
        return carry

    lax.fori_loop(0, passes, one_pass, 0)
    lane = lanes()
    for x in range(6):
        rows = pl.ds(16 * x, 16)
        lows = pl.ds(96 + 16 * x, 16)
        main = acc_ref[rows, 0:128] + acc_ref[lows, 0:128]
        rim = acc_ref[rows, 128:144] + acc_ref[lows, 128:144]
        rim = jnp.concatenate([rim, jnp.zeros((16, 112), F32)], axis=1)
        rim = jnp.where(lane < RIM, rim, jnp.where(lane >= 120, roll(rim, 112, 1), 0.0))
        for n, (cy, cz) in enumerate(SHIFTS):
            store_pair(out_ref, moved((main, rim), cy, cz), n, x)


N_FIRST = 13
WIDE_FIRST = (7,)
N_SECOND = 8
HALVES = (slice(0, 8), slice(8, 16))
SENT_ROWS = ((0, 1), (1,), (-1,), (0, -1))
M2_KEYS = ((0, 0), (0, 1), (0, 2), (1, 1), (1, 2), (2, 2))


def spot(refs, row):
    if row in (1, 2):
        return refs[0], row - 1
    return refs[1], {-1: 0, 0: 1, 3: 2, 4: 3}[row]


def prim_at(prims, row, t, h):
    ref, at = spot(prims, row)
    vals = [ref[k, 2 * at + t, h, :] for k in range(10)]
    return state_of(vals[0], vals[6:9], tuple(vals[1:4]), vals[4]), vals[5], vals[9] > 0.5


def put_gradients(prims, phase_pairs, row):
    ref, at = spot(prims, row)
    grads = gradients(*phase_pairs)
    store_pair(ref, phase_pairs[1], 0, at)
    for i in range(4):
        store_pair(ref, grads[i], 1 + i, at)


def forward(cells_ref, prims, posts, row, t):
    prim_ref, at = spot(prims, row)
    post_ref, _ = spot(posts, row)
    i = 2 * at + t
    for h in HALVES:
        g = [cells_ref[q, row, h, :] for q in range(7)]
        f = [cells_ref[7 + q, row, h, :] for q in range(19)]
        prim_ref[5, i, h, :] = total(f)
        for axis in range(3):
            prim_ref[6 + axis, i, h, :] = momentum_of(f, axis)
        prim_ref[9, i, h, :] = cells_ref[FLUID, row, h, :]
        s, pressure, fluid = prim_at(prims, row, t, h)
        for q, v in post_flow(f, fluid, pressure, s, range(19)).items():
            post_ref[7 + q, i, h, :] = v
        for q, v in post_phase(g, fluid, s, range(7)).items():
            post_ref[q, i, h, :] = v


def stream(posts, row):
    ref, at = spot(posts, row)
    for q in range(19):
        _, cy, cz = DIRS[q]
        if (cy or cz) and 0 <= row + DIRS[q][0] < 4:
            store_pair(ref, moved(load_pair(ref, 7 + q, at), -cy, -cz), 7 + q, at)


def inner_kernel(main_ref, rim_ref, phase_ref, seeds_ref, prim_ref, post_ref, moments_ref):
    prims, posts = (prim_ref, None), (post_ref, None)
    for row in (1, 2):
        put_gradients(prims, [load_pair(phase_ref, row + d) for d in (-1, 0, 1)], row)
        for t, cells_ref in enumerate((main_ref, rim_ref)):
            forward(cells_ref, prims, posts, row, t)
        stream(posts, row)

    def moments(i, carry):
        for h in HALVES:
            adj = {q: seeds_ref[SHIFTS.index(DIRS[q][1:]), i + 2 + 2 * DIRS[q][0], h, :] for q in range(19)}
            m0, m1, m2 = moments_of(adj)
            for k, v in enumerate([m0] + m1 + [m2[key] for key in M2_KEYS]):
                moments_ref[k, i, h, :] = v
        return carry

    lax.fori_loop(0, 8, moments, 0)


def middle_kernel(
    main_ref, rim_ref, phase_ref, odd_in_ref, even_in_ref, seeds_ref, moments_ref, prim_in_ref, post_in_ref,
    prim_ref, adj_ref, gamma_ref, edges_ref, odd_ref, even_ref,
    post_ref, phase_mid_ref, grad_mid_ref, back_ref, dphi_ref,
):
    prims, posts = (prim_in_ref, prim_ref), (post_in_ref, post_ref)
    from_left, from_right = received(odd_in_ref, even_in_ref, N_FIRST, WIDE_FIRST)
    sides = ((from_left, -1, TO_RIGHT, 1), (from_right, 4, TO_LEFT, 2))
    for got, row, crossing, out in sides:
        _, at = spot(prims, row)
        for i in range(3):
            store_pair(prim_ref, got[8 + i], 6 + i, at)
        store_pair(prim_ref, got[11], 9, at)
        for q, pair in zip(crossing, got[:5]):
            store_pair(post_ref, pair, 7 + q, at)
        store_pair(post_ref, got[5], out, at)
    phases = [from_left[12], from_left[7]] + [load_pair(phase_ref, r) for r in range(4)]
    phases += [from_right[7], from_right[12]]
    for row in (-1, 0, 3, 4):
        put_gradients(prims, phases[row + 1 : row + 4], row)
    for row in (0, 3):
        for t, cells_ref in enumerate((main_ref, rim_ref)):
            forward(cells_ref, prims, posts, row, t)
        stream(posts, row)

    mid_parts = {}
    for got, row, crossing, out in sides:
        _, at = spot(posts, row)
        spread = [[], [], []]
        for t in range(2):
            i = 2 * at + t
            halves = [[], [], []]
            for h in HALVES:
                vals = [prim_ref[k, i, h, :] for k in range(10) if k != 5]
                s = state_of(vals[0], vals[5:8], tuple(vals[1:4]), vals[4])
                fluid = vals[8] > 0.5
                vel, force, omega, kappa = s["vel"], s["force"], s["omega"], s["kappa"]
                base = -1.5 * omega * dot(vel, vel) - 3.0 * kappa * dot(vel, force)
                odd_vec = tuple(3.0 * (omega * v + kappa * f) for v, f in zip(vel, force))
                even_vec = tuple(4.5 * omega * v + 9.0 * kappa * f for v, f in zip(vel, force))
                for q in crossing:
                    step = DIRS[q]
                    gain = base + along(step, vel) * along(step, even_vec) + along(step, odd_vec)
                    kept = post_ref[7 + q, i, h, :]
                    post_ref[7 + q, i, h, :] = jnp.where(fluid, kept + W[q] * gain, kept)
                sharp, _ = sharpening(s)
                carried = tuple(s["phi"] * v + sharp * gr for v, gr in zip(vel, s["grad"]))
                kept = post_ref[out, i, h, :]
                gain = 0.15625 * s["phi"] + 0.625 * along(DIRS[out], carried)
                post_ref[out, i, h, :] = jnp.where(fluid, kept + gain, kept)
                halves[0].append(jnp.where(fluid, s["phi"], 0.0))
                halves[1].append(jnp.where(fluid, carried[1], 0.0))
                halves[2].append(jnp.where(fluid, carried[2], 0.0))
            for n in range(3):
                spread[n].append(jnp.concatenate(halves[n], axis=0))
        stream(posts, row)
        phi, cy, cz = (tuple(x) for x in spread)
        gain_y = lambda sign: both(lambda p, c: 0.15625 * p + sign * 0.625 * c, phi, cy)
        gain_z = lambda sign: both(lambda p, c: 0.15625 * p + sign * 0.625 * c, phi, cz)
        mid_parts[row] = [
            got[6], both(lambda p: 0.3125 * p, phi),
            moved(gain_y(1.0), -1, 0), moved(gain_y(-1.0), 1, 0),
            moved(gain_z(1.0), 0, -1), moved(gain_z(-1.0), 0, 1),
        ]
    def post_pair(q, row):
        ref, at = spot(posts, row)
        return load_pair(ref, q, at)

    for row in range(-1, 5):
        parts = mid_parts.get(row)
        if parts is None:
            parts = [post_pair(0, row)]
            for q in range(3, 7):
                parts.append(moved(post_pair(q, row), -DIRS[q][1], -DIRS[q][2]))
        if row > -1:
            parts.append(post_pair(1, row - 1))
        if row < 4:
            parts.append(post_pair(2, row + 1))
        store_pair(phase_mid_ref, both(lambda *p: total(p), *parts), row + 1)
    for row in range(4):
        grads = gradients(*(load_pair(phase_mid_ref, row + d) for d in (0, 1, 2)))
        for i in range(4):
            store_pair(grad_mid_ref, grads[i], i, row)
    def backward(row, t, h):
        i = 2 * row + t
        f = []
        for q in range(19):
            ref, at = spot(posts, row - DIRS[q][0])
            f.append(ref[7 + q, 2 * at + t, h, :])
        adj = {q: seeds_ref[SHIFTS.index(DIRS[q][1:]), i + 2 + 2 * DIRS[q][0], h, :] for q in range(19)}
        ref, at = spot(prims, row)
        fluid = ref[9, 2 * at + t, h, :] > 0.5
        phi = phase_mid_ref[i + 2, h, :]
        mom = [momentum_of(f, axis) for axis in range(3)]
        s = state_of(phi, mom, tuple(grad_mid_ref[k, i, h, :] for k in range(3)), grad_mid_ref[3, i, h, :])
        kept = total([adj[q] * f[q] for q in range(19)])
        m = [moments_ref[k, i, h, :] for k in range(10)]
        m2 = {}
        for key, value in zip(M2_KEYS, m[4:]):
            m2[key] = m2[key[::-1]] = value
        d_flow, d_phi, d_grad, d_lap = pull_all(s, total(f), adj, kept, m[0], m[1:4], m2, None, None)
        for q in range(19):
            adj_ref[q, i, h, :] = jnp.where(fluid, d_flow[q], adj[BACK[q]])
        dphi_ref[i, h, :] = jnp.where(fluid, d_phi, 0.0)
        for k in range(3):
            back_ref[k, i, h, :] = jnp.where(fluid, d_grad[k], 0.0)
        back_ref[3, i, h, :] = jnp.where(fluid, d_lap, 0.0)

    for row in range(4):
        for t in range(2):
            for h in HALVES:
                backward(row, t, h)

    for row in range(4):
        for q in range(19):
            if DIRS[q][1:] != (0, 0) and DIRS[q][0] in SENT_ROWS[row]:
                store_pair(adj_ref, moved(load_pair(adj_ref, q, row), *DIRS[q][1:]), q, row)

    for row in range(4):
        store_pair(gamma_ref, stencil_back(back_ref, dphi_ref, row), row)
    edge_parts = []
    for row, part in ((0, ahead_part), (3, behind_part)):
        pair = both(part, load_pair(back_ref, 0, row), load_pair(back_ref, 3, row))
        store_pair(edges_ref, pair, 0 if row == 0 else 1)
        edge_parts.append(pair)

    messages = []
    for row, out_dirs, part, sign, edge_pair in (
        (3, TO_RIGHT, behind_part, -1.0, edge_parts[1]),
        (0, TO_LEFT, ahead_part, 1.0, edge_parts[0]),
    ):
        gamma = load_pair(gamma_ref, row)
        next_gamma = load_pair(gamma_ref, row - 1 if row == 3 else row + 1)
        n1 = turn_gamma(both(lambda a: sign * a, next_gamma), gamma)
        partial = []
        for t in range(2):
            s, _, fluid = prim_at(prims, row, t, slice(None))
            adj = {
                q: adj_ref[q, 2 * (row + DIRS[q][0]) + t] for q in range(19) if q not in out_dirs
            }
            m0, m1, m2 = moments_of(adj)
            d_grad, d_lap = pull_stencil(s, m0, m1, m2, [n[t] for n in n1])[:2]
            partial.append(jnp.where(fluid, part(d_grad[0], d_lap), 0.0))
        back_dirs = TO_LEFT if row == 3 else TO_RIGHT
        fields = [load_pair(adj_ref, q, row) for q in back_dirs]
        fields += [gamma, edge_pair, tuple(partial)]
        messages.append(fields)
    pack(odd_ref, even_ref, *messages)


def turn_gamma(along_x, centre):
    diff = lambda a, b: 0.125 * (a - b)
    return (
        both(lambda a: 0.125 * a, along_x),
        both(diff, moved(centre, 1, 0), moved(centre, -1, 0)),
        both(diff, moved(centre, 0, 1), moved(centre, 0, -1)),
    )


def stencil_back(back_ref, start_ref, row, first=None, last=None):
    gy, gz, lap = (load_pair(back_ref, k, row) for k in (1, 2, 3))
    fold = lambda l, gyb, gya, lyb, lya, gzb, gza, lzb, lza: (
        0.5 * (gyb - gya) + lyb + lya + 0.5 * (gzb - gza) + lzb + lza - 6.0 * l
    )
    out = both(
        fold, lap,
        moved(gy, -1, 0), moved(gy, 1, 0), moved(lap, -1, 0), moved(lap, 1, 0),
        moved(gz, 0, -1), moved(gz, 0, 1), moved(lap, 0, -1), moved(lap, 0, 1),
    )
    add = lambda a, b: a + b
    if start_ref is not None:
        out = both(add, out, load_pair(start_ref, row))
    if row > 0:
        out = both(add, out, both(behind_part, load_pair(back_ref, 0, row - 1), load_pair(back_ref, 3, row - 1)))
    elif first is not None:
        out = both(add, out, first)
    if row < 3:
        out = both(add, out, both(ahead_part, load_pair(back_ref, 0, row + 1), load_pair(back_ref, 3, row + 1)))
    elif last is not None:
        out = both(add, out, last)
    return out


def ahead_kernel(
    main_ref, prim_in_ref, prim_out_ref, adj_ref, gamma_ref,
    flow_ref, back_ref, dphi_ref,
    turned_ref, shifted_ref,
):
    prims = (prim_in_ref, prim_out_ref)
    for row in range(4):
        for q in range(19):
            if DIRS[q][1:] != (0, 0) and DIRS[q][0] not in SENT_ROWS[row]:
                store_pair(shifted_ref, moved(load_pair(adj_ref, q, row), *DIRS[q][1:]), q, row)

    def adjoint(q, row, t, h):
        step = DIRS[q]
        at = row + step[0]
        ref = adj_ref if step[1:] == (0, 0) or step[0] in SENT_ROWS[at] else shifted_ref
        return ref[q, 2 * at + t, h, :]

    for row in (1, 2):
        centre = load_pair(gamma_ref, row)
        for n, (cy, cz) in enumerate(((1, 0), (-1, 0), (0, 1), (0, -1))):
            store_pair(turned_ref, moved(centre, cy, cz), n, row - 1)
    for row in range(4):
        for t in range(2):
            for h in HALVES:
                i = 2 * row + t
                s, pressure, fluid = prim_at(prims, row, t, h)
                adj = {q: adjoint(q, row, t, h) for q in range(19) if 0 <= row + DIRS[q][0] < 4}
                m0, m1, m2 = moments_of(adj)
                n0 = n1 = None
                if row in (1, 2):
                    g = [gamma_ref[i + 2, h, :], gamma_ref[i - 2, h, :]]
                    g += [turned_ref[n, i - 2, h, :] for n in range(4)]
                    n1 = [0.125 * (g[a] - g[a + 1]) for a in (0, 2, 4)]
                if t == 1:
                    d_grad, d_lap = pull_stencil(s, m0, m1, m2, n1)[:2]
                else:
                    if row in (1, 2):
                        n0 = 0.25 * gamma_ref[i, h, :] + 0.125 * total(g)
                    kept = total([a * main_ref[7 + q, row, h, :] for q, a in adj.items()])
                    d_flow, d_phi, d_grad, d_lap = pull_all(s, pressure, adj, kept, m0, m1, m2, n0, n1)
                    for q in range(19):
                        flow_ref[q, row, h, :] = jnp.where(fluid, d_flow[q], adj.get(BACK[q], 0.0))
                    dphi_ref[row, h, :] = jnp.where(fluid, d_phi, 0.0)
                for k in range(3):
                    back_ref[k, i, h, :] = jnp.where(fluid, d_grad[k], 0.0)
                back_ref[3, i, h, :] = jnp.where(fluid, d_lap, 0.0)


def last_kernel(
    main_ref, prim_in_ref, prim_out_ref, adj_ref, gamma_ref, edges_ref, flow_ref, back_in_ref, dphi_in_ref,
    odd_in_ref, even_in_ref,
    out_g_ref, out_f_ref,
    gamma_wide_ref, turned_ref, back_ref, dphi_ref, g_ref, f_ref, sems,
):
    add = lambda a, b: a + b
    prims = (prim_in_ref, prim_out_ref)
    copies = []

    def send(src, dst):
        copies.append(pltpu.make_async_copy(src, dst, sems.at[len(copies)]))
        copies[-1].start()

    got_left, got_right = received(odd_in_ref, even_in_ref, N_SECOND)
    own_first = load_pair(edges_ref, 0)
    own_last = load_pair(edges_ref, 1)

    for row, more, sign in ((1, got_left[6], -0.125), (2, got_right[6], 0.125)):
        for t in range(2):
            for n, h in enumerate(HALVES):
                i = 2 * row + t
                s, _, fluid = prim_at(prims, row, t, h)
                delta = more[t][8 * n : 8 * n + 8]
                d_vel, d_phi, d_grad, d_lap = pull_along_x(s, 0.125 * delta, sign * delta)
                if t == 0:
                    lift = jnp.where(fluid, d_vel, 0.0)
                    for q in range(19):
                        base = flow_ref[q, row, h, :]
                        f_ref[q, row, h, :] = base + DIRS[q][0] * lift if DIRS[q][0] else base
                    dphi_ref[row, h, :] = dphi_in_ref[row, h, :] + jnp.where(fluid, d_phi, 0.0)
                for k in range(3):
                    back_ref[k, i, h, :] = back_in_ref[k, i, h, :] + jnp.where(fluid, d_grad[k], 0.0)
                back_ref[3, i, h, :] = back_in_ref[3, i, h, :] + jnp.where(fluid, d_lap, 0.0)
    send(f_ref.at[:, pl.ds(1, 2)], out_f_ref.at[:, pl.ds(1, 2)])

    for row in (1, 2):
        store_pair(gamma_wide_ref, load_pair(gamma_ref, row), row + 1)
    store_pair(gamma_wide_ref, both(add, load_pair(gamma_ref, 0), got_left[6]), 1)
    store_pair(gamma_wide_ref, both(add, load_pair(gamma_ref, 3), got_right[6]), 4)
    store_pair(gamma_wide_ref, both(add, got_left[5], own_first), 0)
    store_pair(gamma_wide_ref, both(add, got_right[5], own_last), 5)
    for row in range(4):
        centre = load_pair(gamma_wide_ref, row + 1)
        for n, (cy, cz) in enumerate(((1, 0), (-1, 0), (0, 1), (0, -1))):
            store_pair(turned_ref, moved(centre, cy, cz), n, row)

    def phase_adjoints(i, h):
        at = [gamma_wide_ref[i + 2, h, :], gamma_wide_ref[i + 4, h, :], gamma_wide_ref[i, h, :]]
        return at + [turned_ref[n, i, h, :] for n in range(4)]

    for row, got, dirs in ((0, got_left, TO_LEFT), (3, got_right, TO_RIGHT)):
        for t in range(2):
            for n, h in enumerate(HALVES):
                i = 2 * row + t
                s, pressure, fluid = prim_at(prims, row, t, h)
                adj = {q: pair[t][8 * n : 8 * n + 8] for q, pair in zip(dirs, got[:5])}
                g = phase_adjoints(i, h)
                n1 = [0.125 * (g[a] - g[a + 1]) for a in (1, 3, 5)]
                m0, m1, m2 = moments_of(adj)
                if t == 1:
                    d_grad, d_lap = pull_stencil(s, m0, m1, m2, n1)[:2]
                else:
                    n0 = 0.25 * g[0] + 0.125 * total(g[1:])
                    kept = total([a * main_ref[7 + q, row, h, :] for q, a in adj.items()])
                    d_flow, d_phi, d_grad, d_lap = pull_all(s, pressure, adj, kept, m0, m1, m2, n0, n1)
                    for q in range(19):
                        more = jnp.where(fluid, d_flow[q], adj.get(BACK[q], 0.0))
                        f_ref[q, row, h, :] = flow_ref[q, row, h, :] + more
                    dphi_ref[row, h, :] = dphi_in_ref[row, h, :] + jnp.where(fluid, d_phi, 0.0)
                for k in range(3):
                    back_ref[k, i, h, :] = back_in_ref[k, i, h, :] + jnp.where(fluid, d_grad[k], 0.0)
                back_ref[3, i, h, :] = back_in_ref[3, i, h, :] + jnp.where(fluid, d_lap, 0.0)
        send(f_ref.at[:, pl.ds(row, 1)], out_f_ref.at[:, pl.ds(row, 1)])

    edge_parts = []
    for got, prim_row, row, own, out_dirs, part, sign in (
        (got_left, -1, 0, own_first, TO_RIGHT, behind_part, 1.0),
        (got_right, 4, 3, own_last, TO_LEFT, ahead_part, -1.0),
    ):
        gamma = load_pair(gamma_wide_ref, row + 1)
        n1 = turn_gamma(both(lambda a: sign * a, gamma), own)
        pair = []
        for t in range(2):
            s, _, fluid = prim_at(prims, prim_row, t, slice(None))
            adj = {q: adj_ref[q, 2 * row + t] for q in out_dirs}
            m0, m1, m2 = moments_of(adj)
            d_grad, d_lap = pull_stencil(s, m0, m1, m2, [n[t] for n in n1])[:2]
            pair.append(got[7][t] + jnp.where(fluid, part(d_grad[0], d_lap), 0.0))
        edge_parts.append(tuple(pair))

    for row in range(4):
        rest = stencil_back(back_ref, None, row, edge_parts[0], edge_parts[1])[0]
        ref, at = spot(prims, row)
        fluid = ref[9, 2 * at] > 0.5
        base = rest + dphi_ref[row]
        phase_adj = phase_adjoints(2 * row, slice(None))
        for q in range(7):
            g_ref[q, row] = jnp.where(fluid, base - 0.25 * phase_adj[q], rest + phase_adj[BACK[q]])
        send(g_ref.at[:, pl.ds(row, 1)], out_g_ref.at[:, pl.ds(row, 1)])
    for copy in copies:
        copy.wait()


def call(kernel, outs, n_in, scratch=(), flops=0, name=None, any_in=0, any_out=False):
    vmem = pl.BlockSpec(memory_space=pltpu.VMEM)
    return pl.pallas_call(
        kernel,
        out_shape=[jax.ShapeDtypeStruct(x, F32) if isinstance(x, tuple) else x for x in outs],
        in_specs=[pl.BlockSpec(memory_space=pl.ANY)] * any_in + [vmem] * (n_in - any_in),
        out_specs=[pl.BlockSpec(memory_space=pl.ANY) if any_out else vmem] * len(outs),
        scratch_shapes=[pltpu.VMEM(x, F32) if isinstance(x, tuple) else x for x in scratch],
        compiler_params=pltpu.CompilerParams(vmem_limit_bytes=VMEM_LIMIT),
        cost_estimate=pl.CostEstimate(flops=flops, bytes_accessed=flops // 8, transcendentals=0),
        name=name,
    )


def swap(x, axis, first):
    pairs = []
    for i in range(first, lax.axis_size(axis) - 1, 2):
        pairs += [(i, i + 1), (i + 1, i)]
    return lax.ppermute(x, axis, pairs)


def shards(phase_init, flow_init, solid_mask, sensor_cells, sensor_weights):
    tile = (16, 128)
    cells = sensor_cells.reshape(3, -1, 128).transpose(1, 0, 2)
    weights = sensor_weights.reshape(-1, 128)
    main, probes, weights, odd, even = call(
        rim_kernel,
        [(27, 4) + tile, jax.ShapeDtypeStruct((3,) + weights.shape, jnp.int32), weights.shape] + [(5,) + tile] * 2,
        5, any_in=5, flops=10**6, name="rim",
        scratch=[pltpu.VMEM((4,) + tile, jnp.int32), pltpu.SemaphoreType.DMA((10,))],
    )(*(pltpu.with_memory_space_constraint(x, pltpu.HBM) for x in (phase_init, flow_init, solid_mask, cells, weights)))
    odd, even = swap(odd, "vert", 1), swap(even, "vert", 0)
    (seeds,) = call(probe_kernel, [(9, 12) + tile], 2, scratch=[(192, 144), pltpu.VMEM(weights.shape, jnp.int32)], flops=2 * 10**9, name="probes")(
        probes, weights
    )
    first = message_tiles(N_FIRST, WIDE_FIRST)
    rim, phase, odd, even = call(
        ring_kernel, [(27, 4) + tile, (8,) + tile] + [(first,) + tile] * 2, 3, flops=10**7, name="ring"
    )(main, odd, even)
    odd, even = swap(odd, "tile", 1), swap(even, "tile", 0)
    prim_in, post_in, moments = call(
        inner_kernel, [(10, 4) + tile, (26, 4) + tile, (10, 8) + tile], 4, flops=2 * 10**8, name="inner"
    )(main, rim, phase, seeds)
    second = message_tiles(N_SECOND)
    prim_out, adj, gamma, edges, odd, even = call(
        middle_kernel,
        [(10, 8) + tile, (19, 8) + tile, (8,) + tile, (4,) + tile] + [(second,) + tile] * 2,
        9,
        scratch=[(26, 8) + tile, (12,) + tile, (4, 8) + tile, (4, 8) + tile, (8,) + tile],
        flops=10**8, name="middle",
    )(main, rim, phase, odd, even, seeds, moments, prim_in, post_in)
    odd, even = swap(odd, "tile", 1), swap(even, "tile", 0)
    flow, back, dphi = call(
        ahead_kernel, [(19, 4) + tile, (4, 8) + tile, (4,) + tile], 5, scratch=[(4, 4) + tile, (19, 8) + tile],
        flops=2 * 10**8, name="ahead",
    )(main, prim_in, prim_out, adj, gamma)
    return tuple(
        call(
            last_kernel,
            [(7, 4) + tile, (19, 4) + tile],
            11,
            scratch=[
                (12,) + tile, (4, 8) + tile, (4, 8) + tile, (4,) + tile, (7, 4) + tile, (19, 4) + tile,
                pltpu.SemaphoreType.DMA((7,)),
            ],
            flops=10**8, name="last", any_out=True,
        )(main, prim_in, prim_out, adj, gamma, edges, flow, back, dphi, odd, even)
    )


def solution(mesh):
    return jax.shard_map(
        shards,
        mesh=mesh,
        in_specs=(
            P(None, "tile", None, "vert"),
            P(None, "tile", None, "vert"),
            P("tile", None, "vert"),
            P(),
            P(),
        ),
        out_specs=(P(None, "tile", None, "vert"), P(None, "tile", None, "vert")),
        check_vma=False,
    )
```
